32 devices in a mesh: ctx: 8 (over z, y), head: 4 (over x, core).
Axes of the slice: x: 2, y: 2, z: 4, core: 2. Of those that a mesh axis runs over, the one named last changes fastest.
Arguments:
- queries: bfloat16 [4096, 5120], P('ctx', 'head'), may hold values from -34 to 34
- key_rows: bfloat16 [4096, 5120], P('ctx', 'head'), may hold values from -8 to 8
- value_rows: bfloat16 [4096, 5120], P('ctx', 'head'), may hold values from -23 to 23
- learning_rates: float32 [8, 4096], P('head', 'ctx'), may hold values from 0.02 to 1
- fast_gate: bfloat16 [8, 640, 640], P('head'), may hold values from -0.25 to 0.25
- fast_lift: bfloat16 [8, 640, 640], P('head'), may hold values from -0.25 to 0.25
- fast_down: bfloat16 [8, 640, 640], P('head'), may hold values from -0.25 to 0.25
- output_gain: float32 [5120], P('head'), may hold values from 0.25 to 1.75
- output_weight: bfloat16 [5120, 5120], P(None, 'head'), may hold values from -0.078125 to 0.078125
Outputs:
- layer_output: bfloat16 [4096, 5120], P('ctx', 'head')
The draws below stay inside these ranges and needn't reach their ends.
All inputs are finite; a program needn't handle non-finite values.
Results may differ from the reference program's by a relative error of at most 0.025.
Values may be sent and summed in bfloat16 or wider, within the bound.
No kernel may reach another device: no remote copies, remote signals or barrier semaphores. Data moves between devices by JAX's collectives and lax.ppermute only.
A program may use at most 128 MiB of HBM per device.

```python
import math
import jax
import jax.numpy as jnp
from jax import lax

D = 5120
HEADS = 8
HD = 640
ATT_HD = 128
WINDOW = 512
NS_ITERS = 3
TOK_DEV = 512
GROUP = 4096


def feature_signs(key, count):
    return 2.0 * jax.random.bernoulli(key, 0.5, (count,)).astype(jnp.float32) - 1.0


def drawn_pair(key):
    base_key = jax.random.fold_in(key, 4111)
    first_key, second_key = jax.random.split(base_key)
    sign_key, level_key = jax.random.split(jax.random.fold_in(key, 5227))
    feature_count = HEADS * HD
    feature = jnp.arange(feature_count, dtype=jnp.int32) % HD
    spread = 0.6 * 3.0 ** (feature.astype(jnp.float32) / (HD - 1))
    shared = 0.4 * feature_signs(sign_key, feature_count) * jax.random.uniform(level_key, (feature_count,), jnp.float32, 0.5, 1.5)
    raw_keys = jnp.clip(jax.random.normal(first_key, (GROUP, feature_count), jnp.float32), -4.0, 4.0)
    raw_queries = jnp.clip(jax.random.normal(second_key, (GROUP, feature_count), jnp.float32), -4.0, 4.0)
    key_values = jnp.clip((raw_keys + shared[None, :]) * spread[None, :], -8.0, 8.0)
    query_values = raw_queries + (shared * spread)[None, :]
    return (query_values, key_values)


def draw_queries(key, part):
    query_values, key_values = drawn_pair(key)
    return query_values.astype(jnp.bfloat16)


def draw_key_rows(key, part):
    query_values, key_values = drawn_pair(key)
    return key_values.astype(jnp.bfloat16)


def draw_value_rows(key, part):
    base_key = jax.random.fold_in(key, 7307)
    sign_key, level_key, noise_key = jax.random.split(base_key, 3)
    feature_count = HEADS * HD
    shared = 0.35 * feature_signs(sign_key, feature_count) * jax.random.uniform(level_key, (feature_count,), jnp.float32, 0.5, 1.5)
    raw_values = jnp.clip(jax.random.normal(noise_key, (GROUP, feature_count), jnp.float32), -5.0, 5.0)
    return (4.0 * (raw_values + shared[None, :])).astype(jnp.bfloat16)


def steps_of(key, dims, shards, low, high):
    gain = 1.0
    for position, shards_of in shards:
        heights = jax.random.uniform(jax.random.fold_in(jax.random.fold_in(key, 6), position), (shards_of,), jnp.float32, low / len(shards), high / len(shards))
        gain = gain * jnp.repeat(jnp.exp(heights), dims[position] // shards_of).reshape((-1,) + (1,) * (len(dims) - 1 - position))
    return gain


def normal_values(own_key, extent, width, reach, cuts=(), held_as=jnp.bfloat16):
    level = steps_of(own_key, extent, cuts, -0.22, 0.18) if cuts else 1.0
    drawn = jax.random.normal(own_key, extent, jnp.float32) * width * level
    return jnp.minimum(jnp.maximum(drawn, -reach), reach).astype(held_as)


def setup_inputs(seed: int = 0) -> dict:
    key_of = jax.random.split(jax.random.key(seed), 10)
    queries = draw_queries(jax.random.fold_in(key_of[9], 71), 0)
    key_rows = draw_key_rows(jax.random.fold_in(key_of[9], 71), 0)
    value_rows = draw_value_rows(jax.random.fold_in(key_of[9], 71), 0)
    learning_rates = jnp.clip(jnp.exp(math.log(1.0) - 3.912023 * jax.random.uniform(key_of[3], (HEADS, GROUP), jnp.float32) ** steps_of(key_of[3], (HEADS, GROUP), ((0, 4), (1, 8)), -0.2, 0.2)), 0.02, 1.0)
    fast_gate = normal_values(key_of[4], (HEADS, HD, HD), HD ** -0.5, 0.25, ((0, 4),))
    fast_lift = normal_values(key_of[5], (HEADS, HD, HD), HD ** -0.5, 0.25, ((0, 4),))
    fast_down = normal_values(key_of[6], (HEADS, HD, HD), HD ** -0.5, 0.25, ((0, 4),))
    output_gain = jnp.clip(1.0 + 0.15 * jax.random.normal(key_of[7], (HEADS * HD,), jnp.float32), 0.25, 1.75)
    output_weight = normal_values(key_of[8], (HEADS * HD, D), (HEADS * HD) ** -0.5, 0.078125, ((1, 4),))
    return dict(queries=queries, key_rows=key_rows, value_rows=value_rows, learning_rates=learning_rates, fast_gate=fast_gate, fast_lift=fast_lift, fast_down=fast_down, output_gain=output_gain, output_weight=output_weight)


quintic_first = 3.4445
quintic_second = -4.775
quintic_third = 2.0315

def settle(values):
    return lax.optimization_barrier(values.astype(jnp.bfloat16))

def silu_slope(inputs):
    logistic = jax.nn.sigmoid(inputs)
    return logistic * (1.0 + inputs * (1.0 - logistic))

def window_attention(head_queries, head_keys, head_values):
    stride = min(512, TOK_DEV)
    blocks = GROUP // stride
    padding = jnp.zeros((WINDOW, ATT_HD), jnp.bfloat16)
    keys_padded = jnp.concatenate([padding, head_keys], axis=0)
    values_padded = jnp.concatenate([padding, head_values], axis=0)

    def one_block(number):
        first_row = number * stride
        query_block = lax.dynamic_slice_in_dim(head_queries, first_row, stride, 0)
        key_block = lax.dynamic_slice_in_dim(keys_padded, first_row, stride + WINDOW, 0)
        value_block = lax.dynamic_slice_in_dim(values_padded, first_row, stride + WINDOW, 0)
        scores = jnp.dot(query_block, key_block.T, preferred_element_type=jnp.float32) * ATT_HD ** (-0.5)
        query_place = first_row + jnp.arange(stride, dtype=jnp.int32)[:, None]
        key_place = first_row - WINDOW + jnp.arange(stride + WINDOW, dtype=jnp.int32)[None, :]
        allowed = (key_place > query_place - WINDOW) & (key_place <= query_place) & (key_place >= 0)
        scores = jnp.where(allowed, scores, -1e+30)
        row_peak = lax.optimization_barrier(jnp.max(scores, axis=1, keepdims=True))
        weights = jnp.exp(scores - row_peak)
        row_total = lax.optimization_barrier(jnp.sum(weights, axis=1, keepdims=True))
        probabilities = (weights / row_total).astype(jnp.bfloat16)
        return jnp.dot(probabilities, value_block, preferred_element_type=jnp.float32)
    attended = lax.map(one_block, jnp.arange(blocks, dtype=jnp.int32))
    return attended.reshape(GROUP, ATT_HD)

def orthogonalize(gradients):
    squares = lax.optimization_barrier(jnp.sum(gradients * gradients, axis=(1, 2), keepdims=True))
    current = settle(gradients / (jnp.sqrt(squares) + 1e-06))
    for iteration in range(NS_ITERS):
        widened = current.astype(jnp.float32)
        gram_full = settle(jnp.einsum('mrd,med->mre', widened, widened, precision=lax.Precision.HIGHEST))
        product = settle(jnp.einsum('mre,med->mrd', gram_full.astype(jnp.float32), widened, precision=lax.Precision.HIGHEST))
        second = jnp.einsum('mre,med->mrd', gram_full.astype(jnp.float32), product.astype(jnp.float32), precision=lax.Precision.HIGHEST)
        current = settle(quintic_first * widened + quintic_second * product.astype(jnp.float32) + quintic_third * second)
    return current

def head_output(head_queries, head_keys, head_values, head_rates, gate_init, lift_init, down_init, head_gain):
    gate_pre = jnp.dot(head_keys, gate_init, preferred_element_type=jnp.float32)
    lift_pre = jnp.dot(head_keys, lift_init, preferred_element_type=jnp.float32)
    hidden = (jax.nn.silu(gate_pre) * lift_pre).astype(jnp.bfloat16)
    scaled = (head_rates[:, None] * head_values.astype(jnp.float32)).astype(jnp.bfloat16)
    backward = jnp.dot(scaled, down_init.T, preferred_element_type=jnp.float32)
    grad_gate = (backward * lift_pre * silu_slope(gate_pre)).astype(jnp.bfloat16)
    grad_lift = (backward * jax.nn.silu(gate_pre)).astype(jnp.bfloat16)
    gradients = jnp.stack([jnp.dot(head_keys.T, grad_gate, preferred_element_type=jnp.float32), jnp.dot(head_keys.T, grad_lift, preferred_element_type=jnp.float32), jnp.dot(hidden.T, scaled, preferred_element_type=jnp.float32)])
    directions = orthogonalize(gradients)
    initial = jnp.stack([gate_init, lift_init, down_init]).astype(jnp.float32)
    updated = initial + directions.astype(jnp.float32)
    target = jnp.sqrt(lax.optimization_barrier(jnp.sum(initial * initial, axis=1, keepdims=True)))
    current = jnp.sqrt(lax.optimization_barrier(jnp.sum(updated * updated, axis=1, keepdims=True)) + 1e-06)
    renewed = (updated * (target / current)).astype(jnp.bfloat16)
    applied_gate = jnp.dot(head_queries, renewed[0], preferred_element_type=jnp.float32)
    applied_lift = jnp.dot(head_queries, renewed[1], preferred_element_type=jnp.float32)
    applied_hidden = (jax.nn.silu(applied_gate) * applied_lift).astype(jnp.bfloat16)
    fast_result = jnp.dot(applied_hidden, renewed[2], preferred_element_type=jnp.float32)
    scale_back = lax.rsqrt(lax.optimization_barrier(jnp.mean(fast_result * fast_result, axis=1, keepdims=True)) + 1e-06)
    return fast_result * scale_back * head_gain[None, :]

def reference(queries, key_rows, value_rows, learning_rates, fast_gate, fast_lift, fast_down, output_gain, output_weight):
    pieces = []
    for head_number in range(HEADS):
        low = head_number * HD
        head_queries = queries[:, low:low + HD]
        head_keys = key_rows[:, low:low + HD]
        head_values = value_rows[:, low:low + HD]
        attended_parts = []
        for inner in range(HD // ATT_HD):
            start = inner * ATT_HD
            attended_parts.append(window_attention(head_queries[:, start:start + ATT_HD], head_keys[:, start:start + ATT_HD], head_values[:, start:start + ATT_HD]))
        attended = jnp.concatenate(attended_parts, axis=1)
        fast_part = head_output(head_queries, head_keys, head_values, learning_rates[head_number], fast_gate[head_number], fast_lift[head_number], fast_down[head_number], output_gain[low:low + HD])
        pieces.append((attended + fast_part).astype(jnp.bfloat16))
    combined = jnp.concatenate(pieces, axis=1)
    return jnp.dot(combined, output_weight, preferred_element_type=jnp.float32).astype(jnp.bfloat16)
```

```python
import functools
import math

import jax
import jax.numpy as jnp
from jax import lax
from jax.experimental import pallas as pl
from jax.experimental.pallas import tpu as pltpu
from jax.sharding import PartitionSpec as P

ATT_HD = 128
WINDOW = 512
NS_ITERS = 3
PIECES = 2
VMEM_BYTES = 56 * 1024 * 1024

quintic_first = 3.4445
quintic_second = -4.775
quintic_third = 2.0315

f32 = jnp.float32
bf16 = jnp.bfloat16


def mm(a, b, dims=((1,), (0,))):
    return lax.dot_general(a, b, (dims, ((), ())), preferred_element_type=f32)


def after(value, *earlier):
    return lax.optimization_barrier((value, *earlier))[0]


def pick(blocks, which):
    out = blocks[0]
    for number in range(1, len(blocks)):
        out = jnp.where(which == number, blocks[number], out)
    return out


def tree_low(low, high):
    levels, step = [], 1
    while step < high - low:
        levels.append(
            [(i + step, i) for i in range(low, high, 2 * step) if i + step < high]
        )
        step *= 2
    return levels


def tree_high(low, high):
    return [
        [(low + high - 1 - a, low + high - 1 - b) for a, b in level]
        for level in tree_low(low, high)
    ]


def tree_mid(count):
    middle = count // 2
    left, right = tree_high(0, middle), tree_low(middle, count)
    levels = []
    for k in range(max(len(left), len(right))):
        levels.append((left[k] if k < len(left) else []) + (right[k] if k < len(right) else []))
    return levels + [[(middle - 1, middle)]]


def attention_kernel(first_ref, q_ref, kp_ref, k_ref, vp_ref, v_ref, out_ref, k_all, v_all):
    tokens = q_ref.shape[0]
    tile = ATT_HD
    span = WINDOW + tile
    k_all[:WINDOW] = kp_ref[...]
    k_all[WINDOW:] = k_ref[...]
    v_all[:WINDOW] = vp_ref[...]
    v_all[WINDOW:] = v_ref[...]
    is_first = first_ref[0] == 0
    row = lax.broadcasted_iota(jnp.int32, (tile, span), 0)
    col = lax.broadcasted_iota(jnp.int32, (tile, span), 1)
    allowed = (col > row) & (col <= row + WINDOW)
    scale = ATT_HD**-0.5 * math.log2(math.e)
    for number in range(tokens // tile):
        start = number * tile
        s = mm(q_ref[start : start + tile], k_all[start : start + span], ((1,), (1,))) * scale
        keep = allowed
        if start < WINDOW:
            keep = keep & ((col >= WINDOW - start) | jnp.logical_not(is_first))
        s = jnp.where(keep, s, -1e30)
        w = jnp.exp2(s - jnp.max(s, axis=1, keepdims=True))
        total = jnp.sum(w, axis=1, keepdims=True)
        o = mm(w.astype(bf16), v_all[start : start + span])
        out_ref[start : start + tile] = o / total


def attention(q, kp, k, vp, v, plane):
    tokens, width = q.shape
    wide = pl.BlockSpec((tokens, ATT_HD), lambda a, s: (0, a))
    before = pl.BlockSpec((WINDOW, ATT_HD), lambda a, s: (0, a))
    return pl.pallas_call(
        attention_kernel,
        out_shape=jax.ShapeDtypeStruct((tokens, width), f32),
        grid_spec=pltpu.PrefetchScalarGridSpec(
            num_scalar_prefetch=1,
            grid=(width // ATT_HD,),
            in_specs=[wide, before, wide, before, wide],
            out_specs=wide,
            scratch_shapes=[pltpu.VMEM((WINDOW + tokens, ATT_HD), bf16)] * 2,
        ),
        compiler_params=pltpu.CompilerParams(vmem_limit_bytes=VMEM_BYTES),
        cost_estimate=pl.CostEstimate(
            flops=4 * tokens * (WINDOW + ATT_HD) * width,
            bytes_accessed=12 * tokens * width,
            transcendentals=tokens * (WINDOW + ATT_HD) * (width // ATT_HD),
        ),
    )(jnp.reshape(plane, (1,)).astype(jnp.int32), q, kp, k, vp, v)


def settle_kernel(grad_ref, init_ref, out_ref, x_ref):
    g = grad_ref[...]
    square = jnp.sum(jnp.sum(g * g, axis=0, keepdims=True), axis=1, keepdims=True)
    x_ref[...] = (g / (jnp.sqrt(square) + 1e-06)).astype(bf16)

    @pl.loop(0, NS_ITERS)
    def _(_):
        x = x_ref[...]
        gram = mm(x, x, ((1,), (1,))).astype(bf16)
        product = mm(gram, x).astype(bf16)
        second = mm(gram, product)
        x_ref[...] = (
            quintic_first * x.astype(f32)
            + quintic_second * product.astype(f32)
            + quintic_third * second
        ).astype(bf16)

    initial = init_ref[...].astype(f32)
    updated = initial + x_ref[...].astype(f32)
    target = jnp.sqrt(jnp.sum(initial * initial, axis=0, keepdims=True))
    current = jnp.sqrt(jnp.sum(updated * updated, axis=0, keepdims=True) + 1e-06)
    out_ref[...] = (updated * (target / current)).astype(bf16)


def renew(gradient, initial):
    rows, columns = gradient.shape
    return pl.pallas_call(
        settle_kernel,
        out_shape=jax.ShapeDtypeStruct((rows, columns), bf16),
        scratch_shapes=[pltpu.VMEM((rows, columns), bf16)],
        compiler_params=pltpu.CompilerParams(vmem_limit_bytes=VMEM_BYTES),
        cost_estimate=pl.CostEstimate(
            flops=6 * NS_ITERS * rows * rows * columns,
            bytes_accessed=8 * rows * columns,
            transcendentals=0,
        ),
    )(gradient, initial)


def apply_kernel(which_ref, q_ref, gate_ref, lift_ref, down_ref, att_ref, gain_ref, out_ref):
    q = q_ref[...]
    gate = mm(q, gate_ref[...])
    lift = mm(q, lift_ref[...])
    hidden = (gate / (1.0 + jnp.exp(-gate)) * lift).astype(bf16)
    result = mm(hidden, down_ref[...])
    scale = lax.rsqrt(jnp.mean(result * result, axis=1, keepdims=True) + 1e-06)
    out_ref[...] = (att_ref[...] + result * scale * gain_ref[...]).astype(bf16)


def apply_fast(q, gate, lift, down, attended, gain, which):
    tokens, width = q.shape
    rows = min(256, tokens)
    blocks = tokens // rows
    whole = pl.BlockSpec((width, width), lambda i, s: (0, 0))
    return pl.pallas_call(
        apply_kernel,
        out_shape=jax.ShapeDtypeStruct((tokens, width), bf16),
        grid_spec=pltpu.PrefetchScalarGridSpec(
            num_scalar_prefetch=1,
            grid=(blocks,),
            in_specs=[
                pl.BlockSpec((rows, width), lambda i, s: (i, 0)),
                whole,
                whole,
                whole,
                pl.BlockSpec((rows, width), lambda i, s: (s[0] * blocks + i, 0)),
                pl.BlockSpec((1, width), lambda i, s: (0, 0)),
            ],
            out_specs=pl.BlockSpec((rows, width), lambda i, s: (i, 0)),
        ),
        compiler_params=pltpu.CompilerParams(vmem_limit_bytes=VMEM_BYTES),
        cost_estimate=pl.CostEstimate(
            flops=6 * tokens * width * width,
            bytes_accessed=10 * tokens * width + 6 * width * width,
            transcendentals=tokens * width,
        ),
    )(jnp.reshape(which, (1,)).astype(jnp.int32), q, gate, lift, down, attended, gain)


def project_kernel(count, has_total, is_last, *refs):
    chunk_refs = refs[1 : 1 + count]
    w_ref = refs[1 + count]
    total_ref = refs[2 + count] if has_total else None
    out_ref, sum_ref = refs[-2:]
    step = pl.program_id(0)
    for number in range(count):

        @pl.when(step == number)
        def _(number=number):
            part = mm(chunk_refs[number][...], w_ref[...])
            if number > 0:
                part += sum_ref[...]
            elif has_total:
                part += total_ref[...]
            if number == count - 1:
                out_ref[...] = part.astype(out_ref.dtype)
            else:
                sum_ref[...] = part


def project(chunks, places, weight, total, is_last):
    count = len(chunks)
    tokens, depth = chunks[0].shape
    columns = weight.shape[1]
    fixed = pl.BlockSpec((tokens, depth), lambda k, s: (0, 0))
    square = pl.BlockSpec((tokens, columns), lambda k, s: (0, 0))
    operands = list(chunks) + [weight]
    specs = [fixed] * count + [pl.BlockSpec((depth, columns), lambda k, s: (s[k], 0))]
    if total is not None:
        operands.append(total)
        specs.append(square)
    return pl.pallas_call(
        functools.partial(project_kernel, count, total is not None, is_last),
        out_shape=jax.ShapeDtypeStruct((tokens, columns), bf16 if is_last else f32),
        grid_spec=pltpu.PrefetchScalarGridSpec(
            num_scalar_prefetch=1,
            grid=(count,),
            in_specs=specs,
            out_specs=square,
            scratch_shapes=[pltpu.VMEM((tokens, columns), f32)],
        ),
        compiler_params=pltpu.CompilerParams(vmem_limit_bytes=VMEM_BYTES),
        cost_estimate=pl.CostEstimate(
            flops=2 * count * tokens * depth * columns,
            bytes_accessed=2 * count * (tokens + columns) * depth + 8 * tokens * columns,
            transcendentals=0,
        ),
    )(jnp.stack(places).astype(jnp.int32), *operands)


def token_gradients(keys, values, rates, gate, lift, down):
    gate_pre = mm(keys, gate)
    lift_pre = mm(keys, lift)
    logistic = jax.nn.sigmoid(gate_pre)
    silu = gate_pre * logistic
    hidden = (silu * lift_pre).astype(bf16)
    scaled = (rates[:, None] * values.astype(f32)).astype(bf16)
    backward = mm(scaled, down, ((1,), (1,)))
    grad_gate = (backward * lift_pre * (logistic * (1.0 + gate_pre * (1.0 - logistic)))).astype(bf16)
    grad_lift = (backward * silu).astype(bf16)
    over_tokens = ((0,), (0,))
    return (
        mm(keys, grad_gate, over_tokens),
        mm(keys, grad_lift, over_tokens),
        mm(hidden, scaled, over_tokens),
    )


def on_device(
    queries,
    key_rows,
    value_rows,
    learning_rates,
    fast_gate,
    fast_lift,
    fast_down,
    output_gain,
    output_weight,
):
    tokens = queries.shape[0]
    group, width = fast_gate.shape[0], fast_gate.shape[1]
    context = lax.axis_size("ctx")
    columns_of = lax.axis_size("head")
    planes = context // group
    place = lax.axis_index("ctx")
    member, plane = place % group, place // group
    head_place = lax.axis_index("head")

    def to_member(array, by):
        pairs = [(i, i // group * group + (i + by) % group) for i in range(context)]
        return lax.ppermute(array, "ctx", pairs)

    def between_planes(array, pairs):
        return lax.ppermute(
            array,
            "ctx",
            [(a * group + m, b * group + m) for a, b in pairs for m in range(group)],
        )

    def head_columns(array, by):
        return lax.dynamic_slice_in_dim(array, (member + by) % group * width, width, 1)

    gate, lift, down = (
        lax.dynamic_index_in_dim(w, member, 0, keepdims=False)
        for w in (fast_gate, fast_lift, fast_down)
    )
    gain = lax.dynamic_slice_in_dim(output_gain, member * width, width, 0)[None]

    keys, values, rates, asked = [], [], [], []
    for by in range(group):
        key_part, value_part = head_columns(key_rows, by), head_columns(value_rows, by)
        rate_part = lax.dynamic_index_in_dim(learning_rates, (member + by) % group, 0, keepdims=False)
        query_part = head_columns(queries, by)
        if by > 0:
            rate_part = to_member(rate_part, by)
            key_part = to_member(key_part, by)
            value_part = to_member(value_part, by)
            query_part = to_member(after(query_part, value_part), by)
        keys.append(key_part)
        values.append(value_part)
        rates.append(rate_part)
        asked.append(query_part)

    totals = None
    for by in range(group):
        parts = token_gradients(keys[by], values[by], rates[by], gate, lift, down)
        totals = parts if totals is None else tuple(a + b for a, b in zip(totals, parts))

    trees = (tree_low(0, planes), tree_high(0, planes), tree_mid(planes))
    owners = (0, planes - 1, planes // 2)
    rows = width // PIECES
    pieces = {}
    for piece in range(PIECES):
        for kind in range(3):
            pieces[kind, piece] = totals[kind][piece * rows : (piece + 1) * rows]
    for level in range(max(map(len, trees))):
        for piece in range(PIECES):
            for kind in range(3):
                if level < len(trees[kind]):
                    own = pieces[kind, piece]
                    pieces[kind, piece] = own + between_planes(own.astype(bf16), trees[kind][level]).astype(f32)
    sums = [jnp.concatenate([pieces[kind, piece] for piece in range(PIECES)]) for kind in range(3)]

    def by_owner(options):
        return jnp.where(
            plane == owners[0], options[0], jnp.where(plane == owners[1], options[1], options[2])
        )

    renewed = renew(by_owner(sums), by_owner((gate, lift, down)))

    ordered_keys = [pick(keys, (member - j) % group) for j in range(group)]
    ordered_values = [pick(values, (member - j) % group) for j in range(group)]
    ordered_queries = [pick(asked, (member - j) % group) for j in range(group)]
    onward = [(i, i + 1) for i in range(planes - 1)]
    earlier_keys = between_planes(ordered_keys[-1][-WINDOW:], onward)
    earlier_values = between_planes(ordered_values[-1][-WINDOW:], onward)
    attended = attention(
        jnp.concatenate(ordered_queries),
        earlier_keys,
        jnp.concatenate(ordered_keys),
        earlier_values,
        jnp.concatenate(ordered_values),
        plane,
    )

    held = {}
    for piece in range(PIECES):
        for kind in range(3):
            held[kind, piece] = renewed[piece * rows : (piece + 1) * rows]
    depth = max(map(len, trees))
    for level in reversed(range(depth)):
        for piece in range(PIECES):
            for kind in range(3):
                if level < len(trees[kind]):
                    pairs = [(b, a) for a, b in trees[kind][level]]
                    own = held[kind, piece]
                    got = between_planes(own, pairs)
                    here = functools.reduce(jnp.logical_or, [plane == b for _, b in pairs])
                    held[kind, piece] = jnp.where(here, got, own)
    new_gate, new_lift, new_down = (
        jnp.concatenate([held[kind, piece] for piece in range(PIECES)]) for kind in range(3)
    )

    chunks = []
    for by in list(range(1, group)) + [0]:
        owner = (member - by) % group
        combined = apply_fast(asked[by], new_gate, new_lift, new_down, attended, gain, owner)
        if by > 0:
            combined = to_member(combined, (group - by) % group)
        chunks.append((combined, (member + by) % group))
    chunks = chunks[-1:] + chunks[:-1]

    total = None
    for number, (chunk, head) in enumerate(chunks):
        parts, offsets = [chunk], [0]
        bit = columns_of // 2
        while bit:
            pairs = [(i, i ^ bit) for i in range(columns_of)]
            parts = parts + [lax.ppermute(part, "head", pairs) for part in parts]
            offsets = offsets + [o ^ bit for o in offsets]
            bit //= 2
        places = [(head_place ^ o) * group + head for o in offsets]
        total = project(parts, places, output_weight, total, number == len(chunks) - 1)
    return total


def solution(mesh):
    return jax.shard_map(
        on_device,
        mesh=mesh,
        in_specs=(
            P("ctx", "head"),
            P("ctx", "head"),
            P("ctx", "head"),
            P("head", "ctx"),
            P("head", None, None),
            P("head", None, None),
            P("head", None, None),
            P("head"),
            P(None, "head"),
        ),
        out_specs=P("ctx", "head"),
        check_vma=False,
    )
```

```python
import functools
import math

import jax
import jax.numpy as jnp
from jax import lax
from jax.experimental import pallas as pl
from jax.experimental.pallas import tpu as pltpu
from jax.sharding import PartitionSpec as P

ATT_HD = 128
WINDOW = 512
NS_ITERS = 3
PIECES = 2
VMEM_BYTES = 24 * 1024 * 1024

quintic_first = 3.4445
quintic_second = -4.775
quintic_third = 2.0315

f32 = jnp.float32
bf16 = jnp.bfloat16


def mm(a, b, dims=((1,), (0,))):
    return lax.dot_general(a, b, (dims, ((), ())), preferred_element_type=f32)


def after(value, *earlier):
    return lax.optimization_barrier((value, *earlier))[0]


def pick(blocks, which):
    out = blocks[0]
    for number in range(1, len(blocks)):
        out = jnp.where(which == number, blocks[number], out)
    return out


def tree_low(low, high):
    levels, step = [], 1
    while step < high - low:
        levels.append(
            [(i + step, i) for i in range(low, high, 2 * step) if i + step < high]
        )
        step *= 2
    return levels


def tree_high(low, high):
    return [
        [(low + high - 1 - a, low + high - 1 - b) for a, b in level]
        for level in tree_low(low, high)
    ]


def tree_far(count):
    levels, size = [], count
    while size > 1:
        half = (size + 1) // 2
        levels.append([(i + half, i) for i in range(size - half)])
        size = half
    return levels


def tree_mid(count):
    middle = count // 2
    left, right = tree_high(0, middle), tree_low(middle, count)
    levels = []
    for k in range(max(len(left), len(right))):
        levels.append((left[k] if k < len(left) else []) + (right[k] if k < len(right) else []))
    return levels + [[(middle - 1, middle)]]


def spread_halves(count):
    half = count // 2
    low = [[(b, a) for a, b in level] for level in reversed(tree_low(0, half))]
    return [level + [(count - 1 - a, count - 1 - b) for a, b in level] for level in low]


def attention_kernel(first_ref, q_ref, kp_ref, k_ref, vp_ref, v_ref, out_ref, k_all, v_all):
    tokens = q_ref.shape[0]
    tile = ATT_HD
    span = WINDOW + tile
    k_all[:WINDOW] = kp_ref[...]
    k_all[WINDOW:] = k_ref[...]
    v_all[:WINDOW] = vp_ref[...]
    v_all[WINDOW:] = v_ref[...]
    is_first = first_ref[0] == 0
    row = lax.broadcasted_iota(jnp.int32, (tile, span), 0)
    col = lax.broadcasted_iota(jnp.int32, (tile, span), 1)
    allowed = (col > row) & (col <= row + WINDOW)
    scale = ATT_HD**-0.5 * math.log2(math.e)
    for number in range(tokens // tile):
        start = number * tile
        s = mm(q_ref[start : start + tile], k_all[start : start + span], ((1,), (1,))) * scale
        keep = allowed
        if start < WINDOW:
            keep = keep & ((col >= WINDOW - start) | jnp.logical_not(is_first))
        s = jnp.where(keep, s, -1e30)
        w = jnp.exp2(s - jnp.max(s, axis=1, keepdims=True))
        total = jnp.sum(w, axis=1, keepdims=True)
        o = mm(w.astype(bf16), v_all[start : start + span])
        out_ref[start : start + tile] = o / total


def attention(q, kp, k, vp, v, plane):
    tokens, width = q.shape
    wide = pl.BlockSpec((tokens, ATT_HD), lambda a, s: (0, a))
    before = pl.BlockSpec((WINDOW, ATT_HD), lambda a, s: (0, a))
    return pl.pallas_call(
        attention_kernel,
        out_shape=jax.ShapeDtypeStruct((tokens, width), f32),
        grid_spec=pltpu.PrefetchScalarGridSpec(
            num_scalar_prefetch=1,
            grid=(width // ATT_HD,),
            in_specs=[wide, before, wide, before, wide],
            out_specs=wide,
            scratch_shapes=[pltpu.VMEM((WINDOW + tokens, ATT_HD), bf16)] * 2,
        ),
        compiler_params=pltpu.CompilerParams(vmem_limit_bytes=VMEM_BYTES),
        cost_estimate=pl.CostEstimate(
            flops=4 * tokens * (WINDOW + ATT_HD) * width,
            bytes_accessed=12 * tokens * width,
            transcendentals=tokens * (WINDOW + ATT_HD) * (width // ATT_HD),
        ),
    )(jnp.reshape(plane, (1,)).astype(jnp.int32), q, kp, k, vp, v)


def settle_kernel(active_ref, grad_ref, init_ref, out_ref, x_ref):
    @pl.when(active_ref[0] == 1)
    def _():
        g = grad_ref[...]
        square = jnp.sum(jnp.sum(g * g, axis=0, keepdims=True), axis=1, keepdims=True)
        x_ref[...] = (g / (jnp.sqrt(square) + 1e-06)).astype(bf16)

        @pl.loop(0, NS_ITERS)
        def _(_):
            x = x_ref[...]
            gram = mm(x, x, ((1,), (1,))).astype(bf16)
            product = mm(gram, x).astype(bf16)
            second = mm(gram, product)
            x_ref[...] = (
                quintic_first * x.astype(f32)
                + quintic_second * product.astype(f32)
                + quintic_third * second
            ).astype(bf16)

        initial = init_ref[...].astype(f32)
        updated = initial + x_ref[...].astype(f32)
        target = jnp.sqrt(jnp.sum(initial * initial, axis=0, keepdims=True))
        current = jnp.sqrt(jnp.sum(updated * updated, axis=0, keepdims=True) + 1e-06)
        out_ref[...] = (updated * (target / current)).astype(bf16)

    @pl.when(active_ref[0] == 0)
    def _():
        out_ref[...] = jnp.zeros_like(out_ref)


def renew(gradient, initial, active):
    rows, columns = gradient.shape
    vmem = pl.BlockSpec(memory_space=pltpu.VMEM)
    return pl.pallas_call(
        settle_kernel,
        out_shape=jax.ShapeDtypeStruct((rows, columns), bf16),
        in_specs=[pl.BlockSpec(memory_space=pltpu.SMEM), vmem, vmem],
        out_specs=vmem,
        scratch_shapes=[pltpu.VMEM((rows, columns), bf16)],
        compiler_params=pltpu.CompilerParams(vmem_limit_bytes=VMEM_BYTES),
        cost_estimate=pl.CostEstimate(
            flops=6 * NS_ITERS * rows * rows * columns,
            bytes_accessed=8 * rows * columns,
            transcendentals=0,
        ),
    )(jnp.reshape(active, (1,)).astype(jnp.int32), gradient, initial)


def apply_kernel(which_ref, q_ref, gate_ref, lift_ref, down_ref, att_ref, gain_ref, out_ref):
    q = q_ref[...]
    gate = mm(q, gate_ref[...])
    lift = mm(q, lift_ref[...])
    hidden = (gate / (1.0 + jnp.exp(-gate)) * lift).astype(bf16)
    result = mm(hidden, down_ref[...])
    scale = lax.rsqrt(jnp.mean(result * result, axis=1, keepdims=True) + 1e-06)
    out_ref[...] = (att_ref[...] + result * scale * gain_ref[...]).astype(bf16)


def apply_fast(q, gate, lift, down, attended, gain, which):
    tokens, width = q.shape
    rows = min(256, tokens)
    blocks = tokens // rows
    whole = pl.BlockSpec((width, width), lambda i, s: (0, 0))
    return pl.pallas_call(
        apply_kernel,
        out_shape=jax.ShapeDtypeStruct((tokens, width), bf16),
        grid_spec=pltpu.PrefetchScalarGridSpec(
            num_scalar_prefetch=1,
            grid=(blocks,),
            in_specs=[
                pl.BlockSpec((rows, width), lambda i, s: (i, 0)),
                whole,
                whole,
                whole,
                pl.BlockSpec((rows, width), lambda i, s: (s[0] * blocks + i, 0)),
                pl.BlockSpec((1, width), lambda i, s: (0, 0)),
            ],
            out_specs=pl.BlockSpec((rows, width), lambda i, s: (i, 0)),
        ),
        compiler_params=pltpu.CompilerParams(vmem_limit_bytes=VMEM_BYTES),
        cost_estimate=pl.CostEstimate(
            flops=6 * tokens * width * width,
            bytes_accessed=10 * tokens * width + 6 * width * width,
            transcendentals=tokens * width,
        ),
    )(jnp.reshape(which, (1,)).astype(jnp.int32), q, gate, lift, down, attended, gain)


def project_kernel(count, has_total, is_last, *refs):
    chunk_refs = refs[1 : 1 + count]
    w_ref = refs[1 + count]
    total_ref = refs[2 + count] if has_total else None
    out_ref, sum_ref = refs[-2:]
    step = pl.program_id(0)
    for number in range(count):

        @pl.when(step == number)
        def _(number=number):
            part = mm(chunk_refs[number][...], w_ref[...])
            if number > 0:
                part += sum_ref[...]
            elif has_total:
                part += total_ref[...]
            if number == count - 1:
                out_ref[...] = part.astype(out_ref.dtype)
            else:
                sum_ref[...] = part


def project(chunks, places, weight, total, is_last):
    count = len(chunks)
    tokens, depth = chunks[0].shape
    columns = weight.shape[1]
    fixed = pl.BlockSpec((tokens, depth), lambda k, s: (0, 0))
    square = pl.BlockSpec((tokens, columns), lambda k, s: (0, 0))
    operands = list(chunks) + [weight]
    specs = [fixed] * count + [pl.BlockSpec((depth, columns), lambda k, s: (s[k], 0))]
    if total is not None:
        operands.append(total)
        specs.append(square)
    return pl.pallas_call(
        functools.partial(project_kernel, count, total is not None, is_last),
        out_shape=jax.ShapeDtypeStruct((tokens, columns), bf16 if is_last else f32),
        grid_spec=pltpu.PrefetchScalarGridSpec(
            num_scalar_prefetch=1,
            grid=(count,),
            in_specs=specs,
            out_specs=square,
            scratch_shapes=[pltpu.VMEM((tokens, columns), f32)],
        ),
        compiler_params=pltpu.CompilerParams(vmem_limit_bytes=VMEM_BYTES),
        cost_estimate=pl.CostEstimate(
            flops=2 * count * tokens * depth * columns,
            bytes_accessed=2 * count * (tokens + columns) * depth + 8 * tokens * columns,
            transcendentals=0,
        ),
    )(jnp.stack(places).astype(jnp.int32), *operands)


OVER_TOKENS = ((0,), (0,))


def forward(keys, gate, lift):
    gate_pre = mm(keys, gate)
    lift_pre = mm(keys, lift)
    logistic = jax.nn.sigmoid(gate_pre)
    silu = gate_pre * logistic
    hidden = (silu * lift_pre).astype(bf16)
    return hidden, lift_pre * (logistic * (1.0 + gate_pre * (1.0 - logistic))), silu


def on_device(
    queries,
    key_rows,
    value_rows,
    learning_rates,
    fast_gate,
    fast_lift,
    fast_down,
    output_gain,
    output_weight,
):
    tokens = queries.shape[0]
    group, width = fast_gate.shape[0], fast_gate.shape[1]
    context = lax.axis_size("ctx")
    columns_of = lax.axis_size("head")
    planes = context // group
    place = lax.axis_index("ctx")
    member, plane = place % group, place // group
    head_place = lax.axis_index("head")

    def to_member(array, by):
        pairs = [(i, i // group * group + (i + by) % group) for i in range(context)]
        return lax.ppermute(array, "ctx", pairs)

    def between_planes(array, pairs):
        return lax.ppermute(
            array,
            "ctx",
            [(a * group + m, b * group + m) for a, b in pairs for m in range(group)],
        )

    def head_columns(array, by):
        return lax.dynamic_slice_in_dim(array, (member + by) % group * width, width, 1)

    gate, lift, down = (
        lax.dynamic_index_in_dim(w, member, 0, keepdims=False)
        for w in (fast_gate, fast_lift, fast_down)
    )
    gain = lax.dynamic_slice_in_dim(output_gain, member * width, width, 0)[None]

    onward = [(i, i + 1) for i in range(planes - 1)]

    def in_order(blocks):
        return [pick(blocks, (member - j) % group) for j in range(group)]

    keys = [head_columns(key_rows, by) for by in range(group)]
    values = [head_columns(value_rows, by) for by in range(group)]
    asked = [head_columns(queries, by) for by in range(group)]
    rates = [
        lax.dynamic_index_in_dim(learning_rates, (member + by) % group, 0, keepdims=False)
        for by in range(group)
    ]
    keys = keys[:1] + [to_member(keys[by], by) for by in range(1, group)]
    rates = rates[:1] + [to_member(rates[by], by) for by in range(1, group)]
    values = values[:1] + [to_member(values[by], by) for by in range(1, group)]
    asked = asked[:1] + [to_member(after(asked[by], values[-1]), by) for by in range(1, group)]
    ordered_keys, ordered_values = in_order(keys), in_order(values)
    earlier_keys = between_planes(ordered_keys[-1][-WINDOW:], onward)

    hiddens, slopes, silus, scaleds = [], [], [], []
    total_down = 0.0
    for by in range(group):
        hidden, slope, silu = forward(keys[by], gate, lift)
        scaled = (rates[by][:, None] * after(values[by], hidden, earlier_keys).astype(f32)).astype(bf16)
        total_down = total_down + mm(hidden, scaled, OVER_TOKENS)
        slopes.append(slope)
        silus.append(silu)
        scaleds.append(scaled)
    total_gate, total_lift = 0.0, 0.0
    for by in range(group):
        scaled = scaleds[by] if by < group - 1 else after(scaleds[by], total_down)
        backward = mm(scaled, down, ((1,), (1,)))
        total_gate = total_gate + mm(keys[by], (backward * slopes[by]).astype(bf16), OVER_TOKENS)
        total_lift = total_lift + mm(keys[by], (backward * silus[by]).astype(bf16), OVER_TOKENS)

    rows = width // PIECES

    def cut(matrix):
        return [matrix[piece * rows : (piece + 1) * rows] for piece in range(PIECES)]

    def summed(pieces, level):
        return [own + between_planes(own.astype(bf16), level).astype(f32) for own in pieces]

    gate_tree, lift_tree, down_tree = tree_far(planes), tree_high(0, planes), tree_mid(planes)
    down_pieces = summed(cut(total_down), down_tree[0])
    gate_pieces, lift_pieces = [], []
    for piece, (a, b) in enumerate(zip(cut(total_gate), cut(total_lift))):
        before = down_pieces[:1] if piece == 0 else down_pieces[1:] + asked[-1:]
        gate_pieces += summed([after(a, *before)], gate_tree[0])
        lift_pieces += summed([after(b, *before)], lift_tree[0])
    for level in down_tree[1:]:
        down_pieces = summed(down_pieces, level)
    met = gate_pieces[:1] + lift_pieces[:1]
    for level in range(1, len(gate_tree)):
        gate_pieces = summed(gate_pieces, gate_tree[level])
        lift_pieces = summed(lift_pieces, lift_tree[level])

    middle_plane = plane == planes // 2
    new_down = renew(after(jnp.concatenate(down_pieces), *met), down, middle_plane)

    def spread(own, pairs):
        got = between_planes(own, pairs)
        here = functools.reduce(jnp.logical_or, [plane == b for _, b in pairs])
        return jnp.where(here, got, own)

    down_levels = [[(b, a) for a, b in level] for level in reversed(down_tree)]
    down_pieces = [spread(own, down_levels[0]) for own in cut(new_down)]

    low_plane, high_plane = plane == 0, plane == planes - 1
    new_sums = jnp.concatenate(
        [jnp.where(low_plane, a, b) for a, b in zip(gate_pieces, lift_pieces)]
    )
    earlier_values = between_planes(after(ordered_values[-1][-WINDOW:], new_sums), onward)
    new_outer = renew(
        after(new_sums, down_pieces[0]),
        jnp.where(low_plane, gate, lift),
        low_plane | high_plane,
    )
    for level in down_levels[1:]:
        down_pieces = [spread(own, level) for own in down_pieces]
    half = planes // 2
    swap = [(i, (i + half) % planes) for i in range(planes)]
    owners = [pair for pair in swap if pair[0] in (0, planes - 1)]
    others = [pair for pair in swap if pair not in owners]
    is_owner_swap = functools.reduce(jnp.logical_or, [plane == b for _, b in owners])
    near, far = [], []
    for piece, own in enumerate(cut(new_outer)):
        own = own if piece == 0 else after(own, earlier_values)
        far_own = between_planes(own, owners)
        for level in spread_halves(planes):
            own = spread(own, level)
        near.append(own)
        far.append(far_own)
    far = [
        jnp.where(is_owner_swap, first, between_planes(own, others))
        for own, first in zip(near, far)
    ]
    lower = plane < half
    new_gate = jnp.concatenate([jnp.where(lower, a, b) for a, b in zip(near, far)])
    new_lift = jnp.concatenate([jnp.where(lower, b, a) for a, b in zip(near, far)])
    new_down = jnp.concatenate(down_pieces)

    attended = attention(
        after(jnp.concatenate(in_order(asked)), *near),
        earlier_keys,
        jnp.concatenate(ordered_keys),
        earlier_values,
        jnp.concatenate(ordered_values),
        plane,
    )

    chunks, combined = [], None
    for by in list(range(1, group)) + [0]:
        owner = (member - by) % group
        wanted = asked[by] if combined is None else after(asked[by], combined)
        combined = apply_fast(wanted, new_gate, new_lift, new_down, attended, gain, owner)
        chunk = to_member(combined, group - by) if by > 0 else combined
        chunks.append((chunk, (member + by) % group))
    chunks = chunks[-1:] + chunks[:-1]

    total = None
    for number, (chunk, head) in enumerate(chunks):
        parts, offsets = [chunk], [0]
        bit = columns_of // 2
        while bit:
            pairs = [(i, i ^ bit) for i in range(columns_of)]
            parts = parts + [
                after(lax.ppermute(part, "head", pairs), *([] if total is None else [total]))
                for part in parts
            ]
            offsets = offsets + [o ^ bit for o in offsets]
            bit //= 2
        places = [(head_place ^ o) * group + head for o in offsets]
        total = project(parts, places, output_weight, total, number == len(chunks) - 1)
    return total


def solution(mesh):
    return jax.shard_map(
        on_device,
        mesh=mesh,
        in_specs=(
            P("ctx", "head"),
            P("ctx", "head"),
            P("ctx", "head"),
            P("head", "ctx"),
            P("head", None, None),
            P("head", None, None),
            P("head", None, None),
            P("head"),
            P(None, "head"),
        ),
        out_specs=P("ctx", "head"),
        check_vma=False,
    )
```

```python
import functools
import math

import jax
import jax.numpy as jnp
from jax import lax
from jax.experimental import pallas as pl
from jax.experimental.pallas import tpu as pltpu
from jax.sharding import PartitionSpec as P

ATT_HD = 128
WINDOW = 512
NS_ITERS = 3
PIECES = 2
VMEM_BYTES = 24 * 1024 * 1024
PROJECT_BYTES = 58 * 1024 * 1024

quintic_first = 3.4445
quintic_second = -4.775
quintic_third = 2.0315

f32 = jnp.float32
bf16 = jnp.bfloat16


def mm(a, b, dims=((1,), (0,))):
    return lax.dot_general(a, b, (dims, ((), ())), preferred_element_type=f32)


def after(value, *earlier):
    return lax.optimization_barrier((value, *earlier))[0]


def pick(blocks, which):
    out = blocks[0]
    for number in range(1, len(blocks)):
        out = jnp.where(which == number, blocks[number], out)
    return out


def tree_low(low, high):
    levels, step = [], 1
    while step < high - low:
        levels.append(
            [(i + step, i) for i in range(low, high, 2 * step) if i + step < high]
        )
        step *= 2
    return levels


def tree_high(low, high):
    return [
        [(low + high - 1 - a, low + high - 1 - b) for a, b in level]
        for level in tree_low(low, high)
    ]


def tree_ends(count):
    low = tree_low(0, count // 2)
    return [
        [(2 * a, 2 * b) for a, b in level]
        + [(count - 1 - 2 * a, count - 1 - 2 * b) for a, b in level]
        for level in low
    ]


def tree_mid(count):
    middle = count // 2
    left, right = tree_high(0, middle), tree_low(middle, count)
    levels = []
    for k in range(max(len(left), len(right))):
        levels.append((left[k] if k < len(left) else []) + (right[k] if k < len(right) else []))
    return levels + [[(middle, middle - 1)]]


def spread_halves(count):
    half = count // 2
    low = [[(b, a) for a, b in level] for level in reversed(tree_low(0, half))]
    return [level + [(count - 1 - a, count - 1 - b) for a, b in level] for level in low]


def attention_kernel(first_ref, q_ref, kp_ref, k_ref, vp_ref, v_ref, out_ref, k_all, v_all):
    tokens = q_ref.shape[0]
    tile = ATT_HD
    span = WINDOW + tile
    k_all[:WINDOW] = kp_ref[...]
    k_all[WINDOW:] = k_ref[...]
    v_all[:WINDOW] = vp_ref[...]
    v_all[WINDOW:] = v_ref[...]
    is_first = first_ref[0] == 0
    row = lax.broadcasted_iota(jnp.int32, (tile, span), 0)
    col = lax.broadcasted_iota(jnp.int32, (tile, span), 1)
    allowed = (col > row) & (col <= row + WINDOW)
    scale = ATT_HD**-0.5 * math.log2(math.e)
    for number in range(tokens // tile):
        start = number * tile
        s = mm(q_ref[start : start + tile], k_all[start : start + span], ((1,), (1,))) * scale
        keep = allowed
        if start < WINDOW:
            keep = keep & ((col >= WINDOW - start) | jnp.logical_not(is_first))
        s = jnp.where(keep, s, -1e30)
        w = jnp.exp2(s - jnp.max(s, axis=1, keepdims=True))
        total = jnp.sum(w, axis=1, keepdims=True)
        o = mm(w.astype(bf16), v_all[start : start + span])
        out_ref[start : start + tile] = o / total


def attention(q, kp, k, vp, v, plane):
    tokens, width = q.shape
    wide = pl.BlockSpec((tokens, ATT_HD), lambda a, s: (0, a))
    before = pl.BlockSpec((WINDOW, ATT_HD), lambda a, s: (0, a))
    return pl.pallas_call(
        attention_kernel,
        out_shape=jax.ShapeDtypeStruct((tokens, width), f32),
        grid_spec=pltpu.PrefetchScalarGridSpec(
            num_scalar_prefetch=1,
            grid=(width // ATT_HD,),
            in_specs=[wide, before, wide, before, wide],
            out_specs=wide,
            scratch_shapes=[pltpu.VMEM((WINDOW + tokens, ATT_HD), bf16)] * 2,
        ),
        compiler_params=pltpu.CompilerParams(vmem_limit_bytes=VMEM_BYTES),
        cost_estimate=pl.CostEstimate(
            flops=4 * tokens * (WINDOW + ATT_HD) * width,
            bytes_accessed=12 * tokens * width,
            transcendentals=tokens * (WINDOW + ATT_HD) * (width // ATT_HD),
        ),
    )(jnp.reshape(plane, (1,)).astype(jnp.int32), q, kp, k, vp, v)


def settle_kernel(active_ref, grad_ref, init_ref, out_ref, x_ref):
    @pl.when(active_ref[0] == 1)
    def _():
        g = grad_ref[...]
        square = jnp.sum(jnp.sum(g * g, axis=0, keepdims=True), axis=1, keepdims=True)
        x_ref[...] = (g / (jnp.sqrt(square) + 1e-06)).astype(bf16)

        @pl.loop(0, NS_ITERS)
        def _(_):
            x = x_ref[...]
            gram = mm(x, x, ((1,), (1,))).astype(bf16)
            product = mm(gram, x).astype(bf16)
            second = mm(gram, product)
            x_ref[...] = (
                quintic_first * x.astype(f32)
                + quintic_second * product.astype(f32)
                + quintic_third * second
            ).astype(bf16)

        initial = init_ref[...].astype(f32)
        updated = initial + x_ref[...].astype(f32)
        target = jnp.sqrt(jnp.sum(initial * initial, axis=0, keepdims=True))
        current = jnp.sqrt(jnp.sum(updated * updated, axis=0, keepdims=True) + 1e-06)
        out_ref[...] = (updated * (target / current)).astype(bf16)

    @pl.when(active_ref[0] == 0)
    def _():
        out_ref[...] = jnp.zeros_like(out_ref)


def renew(gradient, initial, active):
    rows, columns = gradient.shape
    vmem = pl.BlockSpec(memory_space=pltpu.VMEM)
    return pl.pallas_call(
        settle_kernel,
        out_shape=jax.ShapeDtypeStruct((rows, columns), bf16),
        in_specs=[pl.BlockSpec(memory_space=pltpu.SMEM), vmem, vmem],
        out_specs=vmem,
        scratch_shapes=[pltpu.VMEM((rows, columns), bf16)],
        compiler_params=pltpu.CompilerParams(vmem_limit_bytes=VMEM_BYTES),
        cost_estimate=pl.CostEstimate(
            flops=6 * NS_ITERS * rows * rows * columns,
            bytes_accessed=8 * rows * columns,
            transcendentals=0,
        ),
    )(jnp.reshape(active, (1,)).astype(jnp.int32), gradient, initial)


def apply_kernel(which_ref, q_ref, gate_ref, lift_ref, down_ref, att_ref, gain_ref, out_ref):
    q = q_ref[...]
    gate = mm(q, gate_ref[...])
    lift = mm(q, lift_ref[...])
    hidden = (gate / (1.0 + jnp.exp(-gate)) * lift).astype(bf16)
    result = mm(hidden, down_ref[...])
    scale = lax.rsqrt(jnp.mean(result * result, axis=1, keepdims=True) + 1e-06)
    out_ref[...] = (att_ref[...] + result * scale * gain_ref[...]).astype(bf16)


def apply_fast(q, gate, lift, down, attended, gain, which):
    tokens, width = q.shape
    rows = min(256, tokens)
    blocks = tokens // rows
    whole = pl.BlockSpec((width, width), lambda i, s: (0, 0))
    return pl.pallas_call(
        apply_kernel,
        out_shape=jax.ShapeDtypeStruct((tokens, width), bf16),
        grid_spec=pltpu.PrefetchScalarGridSpec(
            num_scalar_prefetch=1,
            grid=(blocks,),
            in_specs=[
                pl.BlockSpec((rows, width), lambda i, s: (i, 0)),
                whole,
                whole,
                whole,
                pl.BlockSpec((rows, width), lambda i, s: (s[0] * blocks + i, 0)),
                pl.BlockSpec((1, width), lambda i, s: (0, 0)),
            ],
            out_specs=pl.BlockSpec((rows, width), lambda i, s: (i, 0)),
        ),
        compiler_params=pltpu.CompilerParams(vmem_limit_bytes=VMEM_BYTES),
        cost_estimate=pl.CostEstimate(
            flops=6 * tokens * width * width,
            bytes_accessed=10 * tokens * width + 6 * width * width,
            transcendentals=tokens * width,
        ),
    )(jnp.reshape(which, (1,)).astype(jnp.int32), q, gate, lift, down, attended, gain)


def project_kernel(count, has_total, has_out, *refs):
    chunk_refs = refs[1 : 1 + count]
    w_ref = refs[1 + count]
    total_ref = refs[2 + count] if has_total else None
    out_ref, sum_ref = refs[-2:]
    step = pl.program_id(0)
    for number in range(count):

        @pl.when(step == number)
        def _(number=number):
            part = mm(chunk_refs[number][...], w_ref[...])
            if number > 0:
                part += sum_ref[...]
            elif has_total:
                part += total_ref[...]
            if number == count - 1:
                out_ref[...] = part.astype(out_ref.dtype)
            else:
                sum_ref[...] = part


def project(chunks, places, weight, total, out, block, is_last):
    count = len(chunks)
    rows, depth = chunks[0].shape
    columns = weight.shape[1]
    fixed = pl.BlockSpec((rows, depth), lambda k, s: (0, 0))
    square = pl.BlockSpec((rows, columns), lambda k, s: (block, 0))
    operands = list(chunks) + [weight]
    specs = [fixed] * count + [pl.BlockSpec((depth, columns), lambda k, s: (s[k], 0))]
    if total is not None:
        operands.append(total)
        specs.append(square)
    aliases = {}
    if out is not None:
        aliases = {1 + len(operands): 0}
        operands.append(out)
        specs.append(pl.BlockSpec(memory_space=pl.ANY))
    whole = rows if total is None else total.shape[0]
    return pl.pallas_call(
        functools.partial(project_kernel, count, total is not None, out is not None),
        out_shape=jax.ShapeDtypeStruct((whole, columns), bf16 if is_last else f32),
        grid_spec=pltpu.PrefetchScalarGridSpec(
            num_scalar_prefetch=1,
            grid=(count,),
            in_specs=specs,
            out_specs=square,
            scratch_shapes=[pltpu.VMEM((rows, columns), f32)],
        ),
        input_output_aliases=aliases,
        compiler_params=pltpu.CompilerParams(vmem_limit_bytes=PROJECT_BYTES),
        cost_estimate=pl.CostEstimate(
            flops=2 * count * rows * depth * columns,
            bytes_accessed=2 * count * (rows + columns) * depth + 8 * rows * columns,
            transcendentals=0,
        ),
    )(places, *operands)


OVER_TOKENS = ((0,), (0,))


def forward(keys, gate, lift):
    gate_pre = mm(keys, gate)
    lift_pre = mm(keys, lift)
    logistic = jax.nn.sigmoid(gate_pre)
    silu = gate_pre * logistic
    hidden = (silu * lift_pre).astype(bf16)
    return hidden, lift_pre * (logistic * (1.0 + gate_pre * (1.0 - logistic))), silu


def on_device(
    queries,
    key_rows,
    value_rows,
    learning_rates,
    fast_gate,
    fast_lift,
    fast_down,
    output_gain,
    output_weight,
):
    tokens = queries.shape[0]
    group, width = fast_gate.shape[0], fast_gate.shape[1]
    context = lax.axis_size("ctx")
    columns_of = lax.axis_size("head")
    planes = context // group
    place = lax.axis_index("ctx")
    member, plane = place % group, place // group
    head_place = lax.axis_index("head")

    def to_member(array, by):
        pairs = [(i, i // group * group + (i + by) % group) for i in range(context)]
        return lax.ppermute(array, "ctx", pairs)

    def between_planes(array, pairs):
        return lax.ppermute(
            array,
            "ctx",
            [(a * group + m, b * group + m) for a, b in pairs for m in range(group)],
        )

    def head_columns(array, by):
        return lax.dynamic_slice_in_dim(array, (member + by) % group * width, width, 1)

    gate, lift, down = (
        lax.dynamic_index_in_dim(w, member, 0, keepdims=False)
        for w in (fast_gate, fast_lift, fast_down)
    )
    gain = lax.dynamic_slice_in_dim(output_gain, member * width, width, 0)[None]

    onward = [(i, i + 1) for i in range(planes - 1)]

    def in_order(blocks):
        return [pick(blocks, (member - j) % group) for j in range(group)]

    keys = [head_columns(key_rows, by) for by in range(group)]
    values = [head_columns(value_rows, by) for by in range(group)]
    asked = [head_columns(queries, by) for by in range(group)]
    rates = [
        lax.dynamic_index_in_dim(learning_rates, (member + by) % group, 0, keepdims=False)
        for by in range(group)
    ]
    keys = keys[:1] + [to_member(keys[by], by) for by in range(1, group)]
    rates = rates[:1] + [to_member(rates[by], by) for by in range(1, group)]
    values = values[:1] + [to_member(values[by], by) for by in range(1, group)]
    ordered_keys = in_order(keys)
    earlier_keys = between_planes(ordered_keys[-1][-WINDOW:], onward)
    forwards = [forward(block, gate, lift) for block in keys]
    hidden = forwards[-1][0]
    asked = asked[:1] + [to_member(after(asked[by], hidden), by) for by in range(1, group)]
    values = values[:1] + [after(block, hidden) for block in values[1:]]
    ordered_values = in_order(values)
    earlier_values = between_planes(ordered_values[-1][-WINDOW:], onward)

    hiddens, slopes, silus, scaleds = [], [], [], []
    total_down = 0.0
    for by in range(group):
        hidden, slope, silu = forwards[by]
        block = values[by] if by < group - 1 else after(values[by], earlier_keys)
        scaled = (rates[by][:, None] * block.astype(f32)).astype(bf16)
        total_down = total_down + mm(hidden, scaled, OVER_TOKENS)
        slopes.append(slope)
        silus.append(silu)
        scaleds.append(scaled)
    total_gate, total_lift = 0.0, 0.0
    for by in range(group):
        scaled = scaleds[by] if by < group - 1 else after(scaleds[by], total_down)
        backward = mm(scaled, down, ((1,), (1,)))
        total_gate = total_gate + mm(keys[by], (backward * slopes[by]).astype(bf16), OVER_TOKENS)
        total_lift = total_lift + mm(keys[by], (backward * silus[by]).astype(bf16), OVER_TOKENS)

    rows = width // PIECES

    def cut(matrix):
        return [matrix[piece * rows : (piece + 1) * rows] for piece in range(PIECES)]

    def add_from(own, pairs):
        return own + between_planes(own.astype(bf16), pairs).astype(f32)

    down_levels = tree_mid(planes)
    sum_down = add_from(total_down, down_levels[0])
    attended = attention(
        after(jnp.concatenate(in_order(asked)), earlier_values),
        earlier_keys,
        jnp.concatenate(ordered_keys),
        earlier_values,
        jnp.concatenate(ordered_values),
        plane,
    )
    odd = plane % 2 == 1
    kept = cut(jnp.where(odd, total_lift, total_gate))
    given = cut(jnp.where(odd, total_gate, total_lift).astype(bf16))
    neighbours = [(i, i ^ 1) for i in range(planes)]
    given = [between_planes(after(other, sum_down, attended), neighbours) for other in given]
    for level in down_levels[1:]:
        sum_down = add_from(sum_down, level)
    kept = [own + got.astype(f32) for own, got in zip(kept, given)]
    met = list(kept)
    for level in tree_ends(planes):
        moved = []
        for own in kept:
            moved.append(add_from(after(own, sum_down, *moved) if moved else own, level))
        kept = moved

    middle_plane = plane == planes // 2 - 1
    new_down = renew(after(sum_down, *met), down, middle_plane)

    def spread(own, pairs):
        got = between_planes(own, pairs)
        here = functools.reduce(jnp.logical_or, [plane == b for _, b in pairs])
        return jnp.where(here, got, own)

    low_plane, high_plane = plane == 0, plane == planes - 1
    new_sums = jnp.concatenate(kept)
    new_outer = renew(after(new_sums, new_down), jnp.where(low_plane, gate, lift), low_plane | high_plane)
    half = planes // 2
    swap = [(i, (i + half) % planes) for i in range(planes)]
    owners = [pair for pair in swap if pair[0] in (0, planes - 1)]
    others = [pair for pair in swap if pair not in owners]
    is_owner_swap = functools.reduce(jnp.logical_or, [plane == b for _, b in owners])
    near, far = [], []
    new_down = spread(new_down, [(b, a) for a, b in down_levels[-1]])
    for piece, own in enumerate(cut(new_outer)):
        own = own if piece == 0 else after(own, new_down)
        far_own = between_planes(own, owners)
        for level in spread_halves(planes):
            own = spread(own, level)
        near.append(own)
        far.append(far_own)
    far = [
        jnp.where(is_owner_swap, first, between_planes(own, others))
        for own, first in zip(near, far)
    ]
    lower = plane < half
    new_gate = jnp.concatenate([jnp.where(lower, a, b) for a, b in zip(near, far)])
    new_lift = jnp.concatenate([jnp.where(lower, b, a) for a, b in zip(near, far)])
    for level in reversed(down_levels[:-1]):
        new_down = spread(after(new_down, near[0]), [(b, a) for a, b in level])

    bits = [1 << k for k in reversed(range(columns_of.bit_length() - 1))]

    def gathered(part, first=()):
        parts, offsets = [part], [0]
        for bit in bits:
            pairs = [(i, i ^ bit) for i in range(columns_of)]
            parts = parts + [after(lax.ppermute(p, "head", pairs), *first) for p in parts]
            offsets = offsets + [o ^ bit for o in offsets]
        return parts, offsets

    def places(offsets, head):
        return jnp.stack([(head_place ^ o) * group + head for o in offsets]).astype(jnp.int32)

    combined = apply_fast(asked[0], new_gate, new_lift, new_down, attended, gain, member)
    parts, offsets = gathered(combined)
    arrived = []
    for by in range(1, group):
        combined = apply_fast(
            after(asked[by], combined), new_gate, new_lift, new_down, attended, gain, (member - by) % group
        )
        half_rows = tokens // 2
        arrived.append(
            [to_member(combined[r : r + half_rows], group - by) for r in (0, half_rows)]
        )
    if not arrived:
        return project(parts, places(offsets, member), output_weight, None, None, 0, True)
    total = project(parts, places(offsets, member), output_weight, None, None, 0, False)
    for by in range(1, group):
        is_last = by == group - 1
        out = None
        for number, chunk in enumerate(arrived[by - 1]):
            first = [total] if number == 0 else [out]
            parts, offsets = gathered(chunk, first)
            out = project(
                parts, places(offsets, (member + by) % group), output_weight, total, out, number, is_last
            )
        total = out
    return total


def solution(mesh):
    return jax.shard_map(
        on_device,
        mesh=mesh,
        in_specs=(
            P("ctx", "head"),
            P("ctx", "head"),
            P("ctx", "head"),
            P("head", "ctx"),
            P("head", None, None),
            P("head", None, None),
            P("head", None, None),
            P("head"),
            P(None, "head"),
        ),
        out_specs=P("ctx", "head"),
        check_vma=False,
    )
```

```python
import functools
import math

import jax
import jax.numpy as jnp
from jax import lax
from jax.experimental import pallas as pl
from jax.experimental.pallas import tpu as pltpu
from jax.sharding import PartitionSpec as P

ATT_HD = 128
WINDOW = 512
NS_ITERS = 3
PIECES = 2
VMEM_BYTES = 24 * 1024 * 1024
PROJECT_BYTES = 58 * 1024 * 1024

quintic_first = 3.4445
quintic_second = -4.775
quintic_third = 2.0315

f32 = jnp.float32
bf16 = jnp.bfloat16


def mm(a, b, dims=((1,), (0,))):
    return lax.dot_general(a, b, (dims, ((), ())), preferred_element_type=f32)


def after(value, *earlier):
    return lax.optimization_barrier((value, *earlier))[0]


def pick(blocks, which):
    out = blocks[0]
    for number in range(1, len(blocks)):
        out = jnp.where(which == number, blocks[number], out)
    return out


def tree_low(low, high):
    levels, step = [], 1
    while step < high - low:
        levels.append(
            [(i + step, i) for i in range(low, high, 2 * step) if i + step < high]
        )
        step *= 2
    return levels


def tree_high(low, high):
    return [
        [(low + high - 1 - a, low + high - 1 - b) for a, b in level]
        for level in tree_low(low, high)
    ]


def tree_ends(count):
    low = tree_low(0, count // 2)
    return [
        [(2 * a, 2 * b) for a, b in level]
        + [(count - 1 - 2 * a, count - 1 - 2 * b) for a, b in level]
        for level in low
    ]


def tree_mid(count):
    middle = count // 2
    left, right = tree_high(0, middle), tree_low(middle, count)
    levels = []
    for k in range(max(len(left), len(right))):
        levels.append((left[k] if k < len(left) else []) + (right[k] if k < len(right) else []))
    return levels + [[(middle, middle - 1)]]


def spread_halves(count):
    half = count // 2
    low = [[(b, a) for a, b in level] for level in reversed(tree_low(0, half))]
    return [level + [(count - 1 - a, count - 1 - b) for a, b in level] for level in low]


def attention_kernel(first_ref, q_ref, kp_ref, k_ref, vp_ref, v_ref, out_ref, k_all, v_all):
    tokens = q_ref.shape[0]
    tile = ATT_HD
    span = WINDOW + tile
    k_all[:WINDOW] = kp_ref[...]
    k_all[WINDOW:] = k_ref[...]
    v_all[:WINDOW] = vp_ref[...]
    v_all[WINDOW:] = v_ref[...]
    is_first = first_ref[0] == 0
    row = lax.broadcasted_iota(jnp.int32, (tile, span), 0)
    col = lax.broadcasted_iota(jnp.int32, (tile, span), 1)
    allowed = (col > row) & (col <= row + WINDOW)
    scale = ATT_HD**-0.5 * math.log2(math.e)
    for number in range(tokens // tile):
        start = number * tile
        s = mm(q_ref[start : start + tile], k_all[start : start + span], ((1,), (1,))) * scale
        keep = allowed
        if start < WINDOW:
            keep = keep & ((col >= WINDOW - start) | jnp.logical_not(is_first))
        s = jnp.where(keep, s, -1e30)
        w = jnp.exp2(s - jnp.max(s, axis=1, keepdims=True))
        total = jnp.sum(w, axis=1, keepdims=True)
        o = mm(w.astype(bf16), v_all[start : start + span])
        out_ref[start : start + tile] = o / total


def attention(q, kp, k, vp, v, plane):
    tokens, width = q.shape
    wide = pl.BlockSpec((tokens, ATT_HD), lambda a, s: (0, a))
    before = pl.BlockSpec((WINDOW, ATT_HD), lambda a, s: (0, a))
    return pl.pallas_call(
        attention_kernel,
        out_shape=jax.ShapeDtypeStruct((tokens, width), f32),
        grid_spec=pltpu.PrefetchScalarGridSpec(
            num_scalar_prefetch=1,
            grid=(width // ATT_HD,),
            in_specs=[wide, before, wide, before, wide],
            out_specs=wide,
            scratch_shapes=[pltpu.VMEM((WINDOW + tokens, ATT_HD), bf16)] * 2,
        ),
        compiler_params=pltpu.CompilerParams(vmem_limit_bytes=VMEM_BYTES),
        cost_estimate=pl.CostEstimate(
            flops=4 * tokens * (WINDOW + ATT_HD) * width,
            bytes_accessed=12 * tokens * width,
            transcendentals=tokens * (WINDOW + ATT_HD) * (width // ATT_HD),
        ),
    )(jnp.reshape(plane, (1,)).astype(jnp.int32), q, kp, k, vp, v)


def settle_kernel(active_ref, grad_ref, init_ref, out_ref, x_ref):
    @pl.when(active_ref[0] == 1)
    def _():
        g = grad_ref[...]
        square = jnp.sum(jnp.sum(g * g, axis=0, keepdims=True), axis=1, keepdims=True)
        x_ref[...] = (g / (jnp.sqrt(square) + 1e-06)).astype(bf16)

        @pl.loop(0, NS_ITERS)
        def _(_):
            x = x_ref[...]
            gram = mm(x, x, ((1,), (1,))).astype(bf16)
            product = mm(gram, x).astype(bf16)
            second = mm(gram, product)
            x_ref[...] = (
                quintic_first * x.astype(f32)
                + quintic_second * product.astype(f32)
                + quintic_third * second
            ).astype(bf16)

        initial = init_ref[...].astype(f32)
        updated = initial + x_ref[...].astype(f32)
        target = jnp.sqrt(jnp.sum(initial * initial, axis=0, keepdims=True))
        current = jnp.sqrt(jnp.sum(updated * updated, axis=0, keepdims=True) + 1e-06)
        out_ref[...] = (updated * (target / current)).astype(bf16)

    @pl.when(active_ref[0] == 0)
    def _():
        out_ref[...] = jnp.zeros_like(out_ref)


def renew(gradient, initial, active):
    rows, columns = gradient.shape
    vmem = pl.BlockSpec(memory_space=pltpu.VMEM)
    return pl.pallas_call(
        settle_kernel,
        out_shape=jax.ShapeDtypeStruct((rows, columns), bf16),
        in_specs=[pl.BlockSpec(memory_space=pltpu.SMEM), vmem, vmem],
        out_specs=vmem,
        scratch_shapes=[pltpu.VMEM((rows, columns), bf16)],
        compiler_params=pltpu.CompilerParams(vmem_limit_bytes=VMEM_BYTES),
        cost_estimate=pl.CostEstimate(
            flops=6 * NS_ITERS * rows * rows * columns,
            bytes_accessed=8 * rows * columns,
            transcendentals=0,
        ),
    )(jnp.reshape(active, (1,)).astype(jnp.int32), gradient, initial)


def apply_kernel(which_ref, q_ref, gate_ref, lift_ref, down_ref, att_ref, gain_ref, out_ref):
    q = q_ref[...]
    gate = mm(q, gate_ref[...])
    lift = mm(q, lift_ref[...])
    hidden = (gate / (1.0 + jnp.exp(-gate)) * lift).astype(bf16)
    result = mm(hidden, down_ref[...])
    scale = lax.rsqrt(jnp.mean(result * result, axis=1, keepdims=True) + 1e-06)
    out_ref[...] = (att_ref[...] + result * scale * gain_ref[...]).astype(bf16)


def apply_fast(q, gate, lift, down, attended, gain, which):
    tokens, width = q.shape
    rows = min(256, tokens)
    blocks = tokens // rows
    whole = pl.BlockSpec((width, width), lambda i, s: (0, 0))
    return pl.pallas_call(
        apply_kernel,
        out_shape=jax.ShapeDtypeStruct((tokens, width), bf16),
        grid_spec=pltpu.PrefetchScalarGridSpec(
            num_scalar_prefetch=1,
            grid=(blocks,),
            in_specs=[
                pl.BlockSpec((rows, width), lambda i, s: (i, 0)),
                whole,
                whole,
                whole,
                pl.BlockSpec((rows, width), lambda i, s: (s[0] * blocks + i, 0)),
                pl.BlockSpec((1, width), lambda i, s: (0, 0)),
            ],
            out_specs=pl.BlockSpec((rows, width), lambda i, s: (i, 0)),
        ),
        compiler_params=pltpu.CompilerParams(vmem_limit_bytes=VMEM_BYTES),
        cost_estimate=pl.CostEstimate(
            flops=6 * tokens * width * width,
            bytes_accessed=10 * tokens * width + 6 * width * width,
            transcendentals=tokens * width,
        ),
    )(jnp.reshape(which, (1,)).astype(jnp.int32), q, gate, lift, down, attended, gain)


def project_kernel(count, has_total, *refs):
    chunk_refs = refs[1 : 1 + count]
    w_ref = refs[1 + count]
    total_ref = refs[2 + count] if has_total else None
    out_ref, sum_ref = refs[-2:]
    step = pl.program_id(0)
    for number in range(count):

        @pl.when(step == number)
        def _(number=number):
            part = mm(chunk_refs[number][...], w_ref[...])
            if number > 0:
                part += sum_ref[...]
            elif has_total:
                part += total_ref[...]
            if number == count - 1:
                out_ref[...] = part.astype(out_ref.dtype)
            else:
                sum_ref[...] = part


def project(chunks, places, weight, total, is_last):
    count = len(chunks)
    rows, depth = chunks[0].shape
    columns = weight.shape[1]
    fixed = pl.BlockSpec((rows, depth), lambda k, s: (0, 0))
    square = pl.BlockSpec((rows, columns), lambda k, s: (0, 0))
    operands = list(chunks) + [weight]
    specs = [fixed] * count + [pl.BlockSpec((depth, columns), lambda k, s: (s[k], 0))]
    if total is not None:
        operands.append(total)
        specs.append(square)
    return pl.pallas_call(
        functools.partial(project_kernel, count, total is not None),
        out_shape=jax.ShapeDtypeStruct((rows, columns), bf16 if is_last else f32),
        grid_spec=pltpu.PrefetchScalarGridSpec(
            num_scalar_prefetch=1,
            grid=(count,),
            in_specs=specs,
            out_specs=square,
            scratch_shapes=[pltpu.VMEM((rows, columns), f32)],
        ),
        compiler_params=pltpu.CompilerParams(vmem_limit_bytes=PROJECT_BYTES),
        cost_estimate=pl.CostEstimate(
            flops=2 * count * rows * depth * columns,
            bytes_accessed=2 * count * (rows + columns) * depth + 8 * rows * columns,
            transcendentals=0,
        ),
    )(jnp.stack(places).astype(jnp.int32), *operands)


OVER_TOKENS = ((0,), (0,))


def forward(keys, gate, lift):
    gate_pre = mm(keys, gate)
    lift_pre = mm(keys, lift)
    logistic = jax.nn.sigmoid(gate_pre)
    silu = gate_pre * logistic
    hidden = (silu * lift_pre).astype(bf16)
    return hidden, lift_pre * (logistic * (1.0 + gate_pre * (1.0 - logistic))), silu


def on_device(
    queries,
    key_rows,
    value_rows,
    learning_rates,
    fast_gate,
    fast_lift,
    fast_down,
    output_gain,
    output_weight,
):
    tokens = queries.shape[0]
    group, width = fast_gate.shape[0], fast_gate.shape[1]
    context = lax.axis_size("ctx")
    columns_of = lax.axis_size("head")
    planes = context // group
    place = lax.axis_index("ctx")
    member, plane = place % group, place // group
    head_place = lax.axis_index("head")

    def to_member(array, by):
        pairs = [(i, i // group * group + (i + by) % group) for i in range(context)]
        return lax.ppermute(array, "ctx", pairs)

    def between_planes(array, pairs):
        return lax.ppermute(
            array,
            "ctx",
            [(a * group + m, b * group + m) for a, b in pairs for m in range(group)],
        )

    def head_columns(array, by):
        return lax.dynamic_slice_in_dim(array, (member + by) % group * width, width, 1)

    gate, lift, down = (
        lax.dynamic_index_in_dim(w, member, 0, keepdims=False)
        for w in (fast_gate, fast_lift, fast_down)
    )
    gain = lax.dynamic_slice_in_dim(output_gain, member * width, width, 0)[None]

    onward = [(i, i + 1) for i in range(planes - 1)]

    def in_order(blocks):
        return [pick(blocks, (member - j) % group) for j in range(group)]

    keys = [head_columns(key_rows, by) for by in range(group)]
    values = [head_columns(value_rows, by) for by in range(group)]
    asked = [head_columns(queries, by) for by in range(group)]
    rates = [
        lax.dynamic_index_in_dim(learning_rates, (member + by) % group, 0, keepdims=False)
        for by in range(group)
    ]
    keys = keys[:1] + [to_member(keys[by], by) for by in range(1, group)]
    rates = rates[:1] + [to_member(rates[by], by) for by in range(1, group)]
    values = values[:1] + [to_member(values[by], by) for by in range(1, group)]
    ordered_keys = in_order(keys)
    earlier_keys = between_planes(ordered_keys[-1][-WINDOW:], onward)
    forwards = [forward(block, gate, lift) for block in keys]
    hidden = forwards[-1][0]
    asked = asked[:1] + [to_member(after(asked[by], hidden), by) for by in range(1, group)]
    values = values[:1] + [after(block, hidden) for block in values[1:]]
    ordered_values = in_order(values)

    hiddens, slopes, silus, scaleds = [], [], [], []
    total_down = 0.0
    for by in range(group):
        hidden, slope, silu = forwards[by]
        block = values[by] if by < group - 1 else after(values[by], earlier_keys)
        scaled = (rates[by][:, None] * block.astype(f32)).astype(bf16)
        total_down = total_down + mm(hidden, scaled, OVER_TOKENS)
        slopes.append(slope)
        silus.append(silu)
        scaleds.append(scaled)
    total_gate, total_lift = 0.0, 0.0
    for by in range(group):
        scaled = scaleds[by] if by < group - 1 else after(scaleds[by], total_down)
        backward = mm(scaled, down, ((1,), (1,)))
        total_gate = total_gate + mm(keys[by], (backward * slopes[by]).astype(bf16), OVER_TOKENS)
        total_lift = total_lift + mm(keys[by], (backward * silus[by]).astype(bf16), OVER_TOKENS)

    rows = width // PIECES

    def cut(matrix):
        return [matrix[piece * rows : (piece + 1) * rows] for piece in range(PIECES)]

    def add_from(own, pairs):
        return own + between_planes(own.astype(bf16), pairs).astype(f32)

    down_levels = tree_mid(planes)
    sum_down = add_from(total_down, down_levels[0])
    odd = plane % 2 == 1
    kept = cut(jnp.where(odd, total_lift, total_gate))
    given = cut(jnp.where(odd, total_gate, total_lift).astype(bf16))
    neighbours = [(i, i ^ 1) for i in range(planes)]
    given = [between_planes(after(other, sum_down), neighbours) for other in given]
    for level in down_levels[1:]:
        sum_down = add_from(sum_down, level)
    kept = [own + got.astype(f32) for own, got in zip(kept, given)]
    met = list(kept)
    middle_plane = plane == planes // 2 - 1
    new_down = renew(after(sum_down, *met), down, middle_plane)
    for level in tree_ends(planes):
        kept = [
            after(own, new_down) + between_planes(own.astype(bf16), level).astype(f32) for own in kept
        ]

    def spread(own, pairs):
        got = between_planes(own, pairs)
        here = functools.reduce(jnp.logical_or, [plane == b for _, b in pairs])
        return jnp.where(here, got, own)

    low_plane, high_plane = plane == 0, plane == planes - 1
    new_sums = jnp.concatenate(kept)
    earlier_values = between_planes(after(ordered_values[-1][-WINDOW:], new_sums), onward)
    new_outer = renew(after(new_sums, new_down), jnp.where(low_plane, gate, lift), low_plane | high_plane)
    half = planes // 2
    swap = [(i, (i + half) % planes) for i in range(planes)]
    owners = [pair for pair in swap if pair[0] in (0, planes - 1)]
    others = [pair for pair in swap if pair not in owners]
    is_owner_swap = functools.reduce(jnp.logical_or, [plane == b for _, b in owners])
    near, far = [], []
    new_down = spread(new_down, [(b, a) for a, b in down_levels[-1]])
    near, far = [], []
    for piece, own in enumerate(cut(new_outer)):
        own = own if piece == 0 else after(own, earlier_values)
        first = between_planes(own, owners)
        passed = own
        for level in spread_halves(planes):
            got = between_planes(own, level)
            here = functools.reduce(jnp.logical_or, [plane == b for _, b in level])
            own = jnp.where(here, got, own)
            passed = got
        passed = passed if len(spread_halves(planes)) == 1 else own
        near.append(own)
        far.append((first, between_planes(passed, others)))
    for level in reversed(down_levels[:-1]):
        new_down = spread(after(new_down, *near), [(b, a) for a, b in level])

    attended = attention(
        after(jnp.concatenate(in_order(asked)), *near),
        earlier_keys,
        jnp.concatenate(ordered_keys),
        earlier_values,
        jnp.concatenate(ordered_values),
        plane,
    )
    lower = plane < half
    far = [jnp.where(is_owner_swap, after(first, attended), after(other, attended)) for first, other in far]
    new_gate = jnp.concatenate([jnp.where(lower, a, b) for a, b in zip(near, far)])
    new_lift = jnp.concatenate([jnp.where(lower, b, a) for a, b in zip(near, far)])
    bits = [1 << k for k in reversed(range(columns_of.bit_length() - 1))]

    def swapped(part, bit):
        return lax.ppermute(part, "head", [(i, i ^ bit) for i in range(columns_of)])

    def places(offsets, head):
        return [(head_place ^ o) * group + head for o in offsets]

    arrived, combined = [], None
    for by in list(range(1, group)) + [0]:
        wanted = asked[by] if combined is None else after(asked[by], combined)
        combined = apply_fast(wanted, new_gate, new_lift, new_down, attended, gain, (member - by) % group)
        if by > 0:
            arrived.append((to_member(combined, group - by), (member + by) % group))
    arrived = [(combined, member)] + arrived

    total, far_parts, far_offsets = None, [], []
    for number, (chunk, head) in enumerate(arrived):
        near_parts, near_offsets = [chunk, swapped(chunk, 1)], [0, 1]
        if total is not None:
            total = project(far_parts, far_places, output_weight, total, False)
        far_parts, far_offsets = [], []
        for bit in bits[:-1]:
            step = [swapped(part, bit) for part in [chunk] + far_parts[::2]]
            for part, offset in zip(step, [bit] + [o ^ bit for o in far_offsets[::2]]):
                far_parts += [part, swapped(part, 1)]
                far_offsets += [offset, offset ^ 1]
        far_places = places(far_offsets, head)
        total = project(near_parts, places(near_offsets, head), output_weight, total, False)
    return project(far_parts, far_places, output_weight, total, True)


def solution(mesh):
    return jax.shard_map(
        on_device,
        mesh=mesh,
        in_specs=(
            P("ctx", "head"),
            P("ctx", "head"),
            P("ctx", "head"),
            P("head", "ctx"),
            P("head", None, None),
            P("head", None, None),
            P("head", None, None),
            P("head"),
            P(None, "head"),
        ),
        out_specs=P("ctx", "head"),
        check_vma=False,
    )
```

```python
import functools
import math

import jax
import jax.numpy as jnp
from jax import lax
from jax.experimental import pallas as pl
from jax.experimental.pallas import tpu as pltpu
from jax.sharding import PartitionSpec as P

ATT_HD = 128
WINDOW = 512
NS_ITERS = 3
PIECES = 2
VMEM_BYTES = 24 * 1024 * 1024
PROJECT_BYTES = 32 * 1024 * 1024

quintic_first = 3.4445
quintic_second = -4.775
quintic_third = 2.0315

f32 = jnp.float32
bf16 = jnp.bfloat16


def mm(a, b, dims=((1,), (0,))):
    return lax.dot_general(a, b, (dims, ((), ())), preferred_element_type=f32)


def after(value, *earlier):
    return lax.optimization_barrier((value, *earlier))[0]


def pick(blocks, which):
    out = blocks[0]
    for number in range(1, len(blocks)):
        out = jnp.where(which == number, blocks[number], out)
    return out


def tree_low(low, high):
    levels, step = [], 1
    while step < high - low:
        levels.append(
            [(i + step, i) for i in range(low, high, 2 * step) if i + step < high]
        )
        step *= 2
    return levels


def tree_high(low, high):
    return [
        [(low + high - 1 - a, low + high - 1 - b) for a, b in level]
        for level in tree_low(low, high)
    ]


def tree_ends(count):
    low = tree_low(0, count // 2)
    return [
        [(2 * a, 2 * b) for a, b in level]
        + [(count - 1 - 2 * a, count - 1 - 2 * b) for a, b in level]
        for level in low
    ]


def tree_mid(count):
    middle = count // 2
    left, right = tree_high(0, middle), tree_low(middle, count)
    levels = []
    for k in range(max(len(left), len(right))):
        levels.append((left[k] if k < len(left) else []) + (right[k] if k < len(right) else []))
    return levels + [[(middle, middle - 1)]]


def spread_halves(count):
    half = count // 2
    low = [[(b, a) for a, b in level] for level in reversed(tree_low(0, half))]
    return [level + [(count - 1 - a, count - 1 - b) for a, b in level] for level in low]


def attention_kernel(first_ref, q_ref, kp_ref, k_ref, vp_ref, v_ref, out_ref, k_all, v_all):
    tokens = q_ref.shape[0]
    tile = ATT_HD
    span = WINDOW + tile
    k_all[:WINDOW] = kp_ref[...]
    k_all[WINDOW:] = k_ref[...]
    v_all[:WINDOW] = vp_ref[...]
    v_all[WINDOW:] = v_ref[...]
    is_first = first_ref[0] == 0
    row = lax.broadcasted_iota(jnp.int32, (tile, span), 0)
    col = lax.broadcasted_iota(jnp.int32, (tile, span), 1)
    allowed = (col > row) & (col <= row + WINDOW)
    scale = ATT_HD**-0.5 * math.log2(math.e)
    for number in range(tokens // tile):
        start = number * tile
        s = mm(q_ref[start : start + tile], k_all[start : start + span], ((1,), (1,))) * scale
        keep = allowed
        if start < WINDOW:
            keep = keep & ((col >= WINDOW - start) | jnp.logical_not(is_first))
        s = jnp.where(keep, s, -1e30)
        w = jnp.exp2(s - jnp.max(s, axis=1, keepdims=True))
        total = jnp.sum(w, axis=1, keepdims=True)
        o = mm(w.astype(bf16), v_all[start : start + span])
        out_ref[start : start + tile] = o / total


def attention(q, kp, k, vp, v, plane):
    tokens, width = q.shape
    wide = pl.BlockSpec((tokens, ATT_HD), lambda a, s: (0, a))
    before = pl.BlockSpec((WINDOW, ATT_HD), lambda a, s: (0, a))
    return pl.pallas_call(
        attention_kernel,
        out_shape=jax.ShapeDtypeStruct((tokens, width), f32),
        grid_spec=pltpu.PrefetchScalarGridSpec(
            num_scalar_prefetch=1,
            grid=(width // ATT_HD,),
            in_specs=[wide, before, wide, before, wide],
            out_specs=wide,
            scratch_shapes=[pltpu.VMEM((WINDOW + tokens, ATT_HD), bf16)] * 2,
        ),
        compiler_params=pltpu.CompilerParams(vmem_limit_bytes=VMEM_BYTES),
        cost_estimate=pl.CostEstimate(
            flops=4 * tokens * (WINDOW + ATT_HD) * width,
            bytes_accessed=12 * tokens * width,
            transcendentals=tokens * (WINDOW + ATT_HD) * (width // ATT_HD),
        ),
    )(jnp.reshape(plane, (1,)).astype(jnp.int32), q, kp, k, vp, v)


def settle_kernel(active_ref, grad_ref, init_ref, out_ref, x_ref):
    @pl.when(active_ref[0] == 1)
    def _():
        g = grad_ref[...]
        square = jnp.sum(jnp.sum(g * g, axis=0, keepdims=True), axis=1, keepdims=True)
        x_ref[...] = (g / (jnp.sqrt(square) + 1e-06)).astype(bf16)

        @pl.loop(0, NS_ITERS)
        def _(_):
            x = x_ref[...]
            gram = mm(x, x, ((1,), (1,))).astype(bf16)
            product = mm(gram, x).astype(bf16)
            second = mm(gram, product)
            x_ref[...] = (
                quintic_first * x.astype(f32)
                + quintic_second * product.astype(f32)
                + quintic_third * second
            ).astype(bf16)

        initial = init_ref[...].astype(f32)
        updated = initial + x_ref[...].astype(f32)
        target = jnp.sqrt(jnp.sum(initial * initial, axis=0, keepdims=True))
        current = jnp.sqrt(jnp.sum(updated * updated, axis=0, keepdims=True) + 1e-06)
        out_ref[...] = (updated * (target / current)).astype(bf16)

    @pl.when(active_ref[0] == 0)
    def _():
        out_ref[...] = jnp.zeros_like(out_ref)


def renew(gradient, initial, active):
    rows, columns = gradient.shape
    vmem = pl.BlockSpec(memory_space=pltpu.VMEM)
    return pl.pallas_call(
        settle_kernel,
        out_shape=jax.ShapeDtypeStruct((rows, columns), bf16),
        in_specs=[pl.BlockSpec(memory_space=pltpu.SMEM), vmem, vmem],
        out_specs=vmem,
        scratch_shapes=[pltpu.VMEM((rows, columns), bf16)],
        compiler_params=pltpu.CompilerParams(vmem_limit_bytes=VMEM_BYTES),
        cost_estimate=pl.CostEstimate(
            flops=6 * NS_ITERS * rows * rows * columns,
            bytes_accessed=8 * rows * columns,
            transcendentals=0,
        ),
    )(jnp.reshape(active, (1,)).astype(jnp.int32), gradient, initial)


def apply_kernel(which_ref, q_ref, gate_ref, lift_ref, down_ref, att_ref, gain_ref, out_ref):
    q = q_ref[...]
    gate = mm(q, gate_ref[...])
    lift = mm(q, lift_ref[...])
    hidden = (gate / (1.0 + jnp.exp(-gate)) * lift).astype(bf16)
    result = mm(hidden, down_ref[...])
    scale = lax.rsqrt(jnp.mean(result * result, axis=1, keepdims=True) + 1e-06)
    out_ref[...] = (att_ref[...] + result * scale * gain_ref[...]).astype(bf16)


def apply_fast(q, gate, lift, down, attended, gain, which):
    tokens, width = q.shape
    rows = min(256, tokens)
    blocks = tokens // rows
    whole = pl.BlockSpec((width, width), lambda i, s: (0, 0))
    return pl.pallas_call(
        apply_kernel,
        out_shape=jax.ShapeDtypeStruct((tokens, width), bf16),
        grid_spec=pltpu.PrefetchScalarGridSpec(
            num_scalar_prefetch=1,
            grid=(blocks,),
            in_specs=[
                pl.BlockSpec((rows, width), lambda i, s: (i, 0)),
                whole,
                whole,
                whole,
                pl.BlockSpec((rows, width), lambda i, s: (s[0] * blocks + i, 0)),
                pl.BlockSpec((1, width), lambda i, s: (0, 0)),
            ],
            out_specs=pl.BlockSpec((rows, width), lambda i, s: (i, 0)),
        ),
        compiler_params=pltpu.CompilerParams(vmem_limit_bytes=VMEM_BYTES),
        cost_estimate=pl.CostEstimate(
            flops=6 * tokens * width * width,
            bytes_accessed=10 * tokens * width + 6 * width * width,
            transcendentals=tokens * width,
        ),
    )(jnp.reshape(which, (1,)).astype(jnp.int32), q, gate, lift, down, attended, gain)


def project_kernel(offsets, group, has_total, spot_ref, w_ref, *refs):
    count = len(offsets)
    chunk_refs = refs[:count]
    total_ref = refs[count] if has_total else None
    out_ref, sum_ref, w_rows, arrived = refs[-4:]
    depth = w_rows.shape[1]
    copies = []
    for number, offset in enumerate(offsets):
        start = ((spot_ref[0] ^ offset) * group + spot_ref[1]) * depth
        copy = pltpu.make_async_copy(
            w_ref.at[pl.ds(pl.multiple_of(start, depth), depth)], w_rows.at[number], arrived.at[number]
        )
        copy.start()
        copies.append(copy)
    for number in range(count):
        copies[number].wait()
        part = mm(chunk_refs[number][...], w_rows[number])
        if number > 0:
            part += sum_ref[...]
        elif has_total:
            part += total_ref[...]
        if number == count - 1:
            out_ref[...] = part.astype(out_ref.dtype)
        else:
            sum_ref[...] = part


def project(chunks, offsets, group, spot, weight, total, is_last):
    count = len(chunks)
    rows, depth = chunks[0].shape
    columns = weight.shape[1]
    vmem = pl.BlockSpec(memory_space=pltpu.VMEM)
    operands = [spot, weight] + list(chunks) + ([] if total is None else [total])
    return pl.pallas_call(
        functools.partial(project_kernel, offsets, group, total is not None),
        out_shape=jax.ShapeDtypeStruct((rows, columns), bf16 if is_last else f32),
        in_specs=[pl.BlockSpec(memory_space=pltpu.SMEM), pl.BlockSpec(memory_space=pltpu.HBM)]
        + [vmem] * (len(operands) - 2),
        out_specs=vmem,
        scratch_shapes=[
            pltpu.VMEM((rows, columns), f32),
            pltpu.VMEM((count, depth, columns), bf16),
            pltpu.SemaphoreType.DMA((count,)),
        ],
        compiler_params=pltpu.CompilerParams(vmem_limit_bytes=PROJECT_BYTES),
        cost_estimate=pl.CostEstimate(
            flops=2 * count * rows * depth * columns,
            bytes_accessed=2 * count * (rows + columns) * depth + 8 * rows * columns,
            transcendentals=0,
        ),
    )(*operands)


OVER_TOKENS = ((0,), (0,))


def forward(keys, gate, lift):
    gate_pre = mm(keys, gate)
    lift_pre = mm(keys, lift)
    logistic = jax.nn.sigmoid(gate_pre)
    silu = gate_pre * logistic
    hidden = (silu * lift_pre).astype(bf16)
    return hidden, lift_pre * (logistic * (1.0 + gate_pre * (1.0 - logistic))), silu


def on_device(
    queries,
    key_rows,
    value_rows,
    learning_rates,
    fast_gate,
    fast_lift,
    fast_down,
    output_gain,
    output_weight,
):
    tokens = queries.shape[0]
    group, width = fast_gate.shape[0], fast_gate.shape[1]
    context = lax.axis_size("ctx")
    columns_of = lax.axis_size("head")
    planes = context // group
    place = lax.axis_index("ctx")
    member, plane = place % group, place // group
    head_place = lax.axis_index("head")

    def to_member(array, by):
        pairs = [(i, i // group * group + (i + by) % group) for i in range(context)]
        return lax.ppermute(array, "ctx", pairs)

    def between_planes(array, pairs):
        return lax.ppermute(
            array,
            "ctx",
            [(a * group + m, b * group + m) for a, b in pairs for m in range(group)],
        )

    def head_columns(array, by):
        return lax.dynamic_slice_in_dim(array, (member + by) % group * width, width, 1)

    gate, lift, down = (
        lax.dynamic_index_in_dim(w, member, 0, keepdims=False)
        for w in (fast_gate, fast_lift, fast_down)
    )
    gain = lax.dynamic_slice_in_dim(output_gain, member * width, width, 0)[None]

    onward = [(i, i + 1) for i in range(planes - 1)]

    def in_order(blocks):
        return [pick(blocks, (member - j) % group) for j in range(group)]

    keys = [head_columns(key_rows, by) for by in range(group)]
    values = [head_columns(value_rows, by) for by in range(group)]
    asked = [head_columns(queries, by) for by in range(group)]
    rates = [
        lax.dynamic_index_in_dim(learning_rates, (member + by) % group, 0, keepdims=False)
        for by in range(group)
    ]
    keys = keys[:1] + [to_member(keys[by], by) for by in range(1, group)]
    rates = rates[:1] + [to_member(rates[by], by) for by in range(1, group)]
    values = values[:1] + [to_member(values[by], by) for by in range(1, group)]
    ordered_keys = in_order(keys)
    earlier_keys = between_planes(ordered_keys[-1][-WINDOW:], onward)
    forwards = [forward(block, gate, lift) for block in keys]
    hidden = forwards[-1][0]
    asked = asked[:1] + [to_member(after(asked[by], hidden), by) for by in range(1, group)]
    values = values[:1] + [after(block, hidden) for block in values[1:]]

    hiddens, slopes, silus, scaleds = [], [], [], []
    total_down = 0.0
    for by in range(group):
        hidden, slope, silu = forwards[by]
        block = values[by] if by < group - 1 else after(values[by], earlier_keys)
        scaled = (rates[by][:, None] * block.astype(f32)).astype(bf16)
        total_down = total_down + mm(hidden, scaled, OVER_TOKENS)
        slopes.append(slope)
        silus.append(silu)
        scaleds.append(scaled)
    total_gate, total_lift = 0.0, 0.0
    for by in range(group):
        scaled = scaleds[by] if by < group - 1 else after(scaleds[by], total_down)
        backward = mm(scaled, down, ((1,), (1,)))
        total_gate = total_gate + mm(keys[by], (backward * slopes[by]).astype(bf16), OVER_TOKENS)
        total_lift = total_lift + mm(keys[by], (backward * silus[by]).astype(bf16), OVER_TOKENS)

    ordered_values = in_order([after(block, total_down) for block in values])
    window_values = ordered_values[-1][-WINDOW:]
    values_early = between_planes(window_values, onward[1:])

    rows = width // PIECES

    def cut(matrix):
        return [matrix[piece * rows : (piece + 1) * rows] for piece in range(PIECES)]

    def add_from(own, pairs):
        return own + between_planes(own.astype(bf16), pairs).astype(f32)

    down_levels = tree_mid(planes)
    sum_down = add_from(total_down, down_levels[0])
    odd = plane % 2 == 1
    kept = cut(jnp.where(odd, total_lift, total_gate))
    given = cut(jnp.where(odd, total_gate, total_lift).astype(bf16))
    neighbours = [(i, i ^ 1) for i in range(planes)]
    given = [between_planes(after(other, sum_down), neighbours) for other in given]
    first_sum = sum_down
    for level in down_levels[1:]:
        sum_down = add_from(sum_down, level)
    kept = [own + got.astype(f32) for own, got in zip(kept, given)]
    met = list(kept)
    values_first = between_planes(after(window_values, first_sum), onward[:1])
    earlier_values = jnp.where(plane == 1, values_first, values_early)
    middle_plane = plane == planes // 2 - 1
    new_down = renew(after(sum_down, values_first, *met), down, middle_plane)
    for level in tree_ends(planes):
        kept = [
            after(own, new_down) + between_planes(own.astype(bf16), level).astype(f32) for own in kept
        ]

    def spread(own, pairs):
        got = between_planes(own, pairs)
        here = functools.reduce(jnp.logical_or, [plane == b for _, b in pairs])
        return jnp.where(here, got, own)

    low_plane, high_plane = plane == 0, plane == planes - 1
    new_sums = jnp.concatenate(kept)
    new_outer = renew(after(new_sums, new_down), jnp.where(low_plane, gate, lift), low_plane | high_plane)
    half = planes // 2
    swap = [(i, (i + half) % planes) for i in range(planes)]
    owners = [pair for pair in swap if pair[0] in (0, planes - 1)]
    others = [pair for pair in swap if pair not in owners]
    is_owner_swap = functools.reduce(jnp.logical_or, [plane == b for _, b in owners])
    near, far = [], []
    new_down = spread(new_down, [(b, a) for a, b in down_levels[-1]])
    near, far = [], []
    for own in cut(new_outer):
        first = between_planes(own, owners)
        passed = own
        for level in spread_halves(planes):
            got = between_planes(own, level)
            here = functools.reduce(jnp.logical_or, [plane == b for _, b in level])
            own = jnp.where(here, got, own)
            passed = got
        passed = passed if len(spread_halves(planes)) == 1 else own
        near.append(own)
        far.append((first, between_planes(passed, others)))
    for level in reversed(down_levels[:-1]):
        new_down = spread(after(new_down, *near), [(b, a) for a, b in level])

    attended = attention(
        after(jnp.concatenate(in_order(asked)), *near),
        earlier_keys,
        jnp.concatenate(ordered_keys),
        earlier_values,
        jnp.concatenate(ordered_values),
        plane,
    )
    lower = plane < half
    far = [jnp.where(is_owner_swap, after(first, attended), after(other, attended)) for first, other in far]
    new_gate = jnp.concatenate([jnp.where(lower, a, b) for a, b in zip(near, far)])
    new_lift = jnp.concatenate([jnp.where(lower, b, a) for a, b in zip(near, far)])
    bits = [1 << k for k in reversed(range(columns_of.bit_length() - 1))]

    def swapped(part, bit):
        return lax.ppermute(part, "head", [(i, i ^ bit) for i in range(columns_of)])

    arrived, combined = [], None
    for by in list(range(1, group)) + [0]:
        wanted = asked[by] if combined is None else after(asked[by], combined)
        combined = apply_fast(wanted, new_gate, new_lift, new_down, attended, gain, (member - by) % group)
        if by > 0:
            arrived.append((to_member(combined, group - by), (member + by) % group))
    arrived = [(combined, member)] + arrived

    total = None
    for number, (chunk, head) in enumerate(arrived):
        parts = [chunk]
        for bit in bits:
            got = [swapped(part, bit) for part in parts]
            if total is not None and bit == bits[0]:
                got = [after(part, total) for part in got]
            parts = [p for pair in zip(parts, got) for p in pair]
        offsets = [0]
        for bit in bits:
            offsets = [p for o in offsets for p in (o, o ^ bit)]
        spot = jnp.stack([head_place, head]).astype(jnp.int32)
        total = project(parts, offsets, group, spot, output_weight, total, number == len(arrived) - 1)
    return total


def solution(mesh):
    return jax.shard_map(
        on_device,
        mesh=mesh,
        in_specs=(
            P("ctx", "head"),
            P("ctx", "head"),
            P("ctx", "head"),
            P("head", "ctx"),
            P("head", None, None),
            P("head", None, None),
            P("head", None, None),
            P("head"),
            P(None, "head"),
        ),
        out_specs=P("ctx", "head"),
        check_vma=False,
    )
```

```python
import functools
import math

import jax
import jax.numpy as jnp
from jax import lax
from jax.experimental import pallas as pl
from jax.experimental.pallas import tpu as pltpu
from jax.sharding import PartitionSpec as P

ATT_HD = 128
WINDOW = 512
NS_ITERS = 3
PIECES = 2
VMEM_BYTES = 24 * 1024 * 1024
PROJECT_BYTES = 52 * 1024 * 1024

quintic_first = 3.4445
quintic_second = -4.775
quintic_third = 2.0315

f32 = jnp.float32
bf16 = jnp.bfloat16


def mm(a, b, dims=((1,), (0,))):
    return lax.dot_general(a, b, (dims, ((), ())), preferred_element_type=f32)


def after(value, *earlier):
    return lax.optimization_barrier((value, *earlier))[0]


def pick(blocks, which):
    out = blocks[0]
    for number in range(1, len(blocks)):
        out = jnp.where(which == number, blocks[number], out)
    return out


def tree_low(low, high):
    levels, step = [], 1
    while step < high - low:
        levels.append(
            [(i + step, i) for i in range(low, high, 2 * step) if i + step < high]
        )
        step *= 2
    return levels


def tree_high(low, high):
    return [
        [(low + high - 1 - a, low + high - 1 - b) for a, b in level]
        for level in tree_low(low, high)
    ]


def tree_ends(count):
    low = tree_low(0, count // 2)
    return [
        [(2 * a, 2 * b) for a, b in level]
        + [(count - 1 - 2 * a, count - 1 - 2 * b) for a, b in level]
        for level in low
    ]


def tree_mid(count):
    middle = count // 2
    left, right = tree_high(0, middle), tree_low(middle, count)
    levels = []
    for k in range(max(len(left), len(right))):
        levels.append((left[k] if k < len(left) else []) + (right[k] if k < len(right) else []))
    return levels + [[(middle, middle - 1)]]


def spread_halves(count):
    half = count // 2
    low = [[(b, a) for a, b in level] for level in reversed(tree_low(0, half))]
    return [level + [(count - 1 - a, count - 1 - b) for a, b in level] for level in low]


def attention_kernel(first_ref, q_ref, kp_ref, k_ref, vp_ref, v_ref, out_ref, k_all, v_all):
    tokens = q_ref.shape[0]
    tile = ATT_HD
    span = WINDOW + tile
    k_all[:WINDOW] = kp_ref[...]
    k_all[WINDOW:] = k_ref[...]
    v_all[:WINDOW] = vp_ref[...]
    v_all[WINDOW:] = v_ref[...]
    is_first = first_ref[0] == 0
    row = lax.broadcasted_iota(jnp.int32, (tile, span), 0)
    col = lax.broadcasted_iota(jnp.int32, (tile, span), 1)
    allowed = (col > row) & (col <= row + WINDOW)
    scale = ATT_HD**-0.5 * math.log2(math.e)
    for number in range(tokens // tile):
        start = number * tile
        s = mm(q_ref[start : start + tile], k_all[start : start + span], ((1,), (1,))) * scale
        keep = allowed
        if start < WINDOW:
            keep = keep & ((col >= WINDOW - start) | jnp.logical_not(is_first))
        s = jnp.where(keep, s, -1e30)
        w = jnp.exp2(s - jnp.max(s, axis=1, keepdims=True))
        total = jnp.sum(w, axis=1, keepdims=True)
        o = mm(w.astype(bf16), v_all[start : start + span])
        out_ref[start : start + tile] = o / total


def attention(q, kp, k, vp, v, plane):
    tokens, width = q.shape
    wide = pl.BlockSpec((tokens, ATT_HD), lambda a, s: (0, a))
    before = pl.BlockSpec((WINDOW, ATT_HD), lambda a, s: (0, a))
    return pl.pallas_call(
        attention_kernel,
        out_shape=jax.ShapeDtypeStruct((tokens, width), f32),
        grid_spec=pltpu.PrefetchScalarGridSpec(
            num_scalar_prefetch=1,
            grid=(width // ATT_HD,),
            in_specs=[wide, before, wide, before, wide],
            out_specs=wide,
            scratch_shapes=[pltpu.VMEM((WINDOW + tokens, ATT_HD), bf16)] * 2,
        ),
        compiler_params=pltpu.CompilerParams(vmem_limit_bytes=VMEM_BYTES),
        cost_estimate=pl.CostEstimate(
            flops=4 * tokens * (WINDOW + ATT_HD) * width,
            bytes_accessed=12 * tokens * width,
            transcendentals=tokens * (WINDOW + ATT_HD) * (width // ATT_HD),
        ),
    )(jnp.reshape(plane, (1,)).astype(jnp.int32), q, kp, k, vp, v)


def settle_kernel(active_ref, grad_ref, init_ref, out_ref, x_ref):
    @pl.when(active_ref[0] == 1)
    def _():
        g = grad_ref[...]
        square = jnp.sum(jnp.sum(g * g, axis=0, keepdims=True), axis=1, keepdims=True)
        x_ref[...] = (g / (jnp.sqrt(square) + 1e-06)).astype(bf16)

        @pl.loop(0, NS_ITERS)
        def _(_):
            x = x_ref[...]
            gram = mm(x, x, ((1,), (1,))).astype(bf16)
            product = mm(gram, x).astype(bf16)
            second = mm(gram, product)
            x_ref[...] = (
                quintic_first * x.astype(f32)
                + quintic_second * product.astype(f32)
                + quintic_third * second
            ).astype(bf16)

        initial = init_ref[...].astype(f32)
        updated = initial + x_ref[...].astype(f32)
        target = jnp.sqrt(jnp.sum(initial * initial, axis=0, keepdims=True))
        current = jnp.sqrt(jnp.sum(updated * updated, axis=0, keepdims=True) + 1e-06)
        out_ref[...] = (updated * (target / current)).astype(bf16)

    @pl.when(active_ref[0] == 0)
    def _():
        out_ref[...] = jnp.zeros_like(out_ref)


def renew(gradient, initial, active):
    rows, columns = gradient.shape
    vmem = pl.BlockSpec(memory_space=pltpu.VMEM)
    return pl.pallas_call(
        settle_kernel,
        out_shape=jax.ShapeDtypeStruct((rows, columns), bf16),
        in_specs=[pl.BlockSpec(memory_space=pltpu.SMEM), vmem, vmem],
        out_specs=vmem,
        scratch_shapes=[pltpu.VMEM((rows, columns), bf16)],
        compiler_params=pltpu.CompilerParams(vmem_limit_bytes=VMEM_BYTES),
        cost_estimate=pl.CostEstimate(
            flops=6 * NS_ITERS * rows * rows * columns,
            bytes_accessed=8 * rows * columns,
            transcendentals=0,
        ),
    )(jnp.reshape(active, (1,)).astype(jnp.int32), gradient, initial)


def apply_kernel(which_ref, q_ref, gate_ref, lift_ref, down_ref, att_ref, gain_ref, out_ref):
    q = q_ref[...]
    gate = mm(q, gate_ref[...])
    lift = mm(q, lift_ref[...])
    hidden = (gate / (1.0 + jnp.exp(-gate)) * lift).astype(bf16)
    result = mm(hidden, down_ref[...])
    scale = lax.rsqrt(jnp.mean(result * result, axis=1, keepdims=True) + 1e-06)
    out_ref[...] = (att_ref[...] + result * scale * gain_ref[...]).astype(bf16)


def apply_fast(q, gate, lift, down, attended, gain, which):
    tokens, width = q.shape
    rows = min(256, tokens)
    blocks = tokens // rows
    whole = pl.BlockSpec((width, width), lambda i, s: (0, 0))
    return pl.pallas_call(
        apply_kernel,
        out_shape=jax.ShapeDtypeStruct((tokens, width), bf16),
        grid_spec=pltpu.PrefetchScalarGridSpec(
            num_scalar_prefetch=1,
            grid=(blocks,),
            in_specs=[
                pl.BlockSpec((rows, width), lambda i, s: (i, 0)),
                whole,
                whole,
                whole,
                pl.BlockSpec((rows, width), lambda i, s: (s[0] * blocks + i, 0)),
                pl.BlockSpec((1, width), lambda i, s: (0, 0)),
            ],
            out_specs=pl.BlockSpec((rows, width), lambda i, s: (i, 0)),
        ),
        compiler_params=pltpu.CompilerParams(vmem_limit_bytes=VMEM_BYTES),
        cost_estimate=pl.CostEstimate(
            flops=6 * tokens * width * width,
            bytes_accessed=10 * tokens * width + 6 * width * width,
            transcendentals=tokens * width,
        ),
    )(jnp.reshape(which, (1,)).astype(jnp.int32), q, gate, lift, down, attended, gain)


def project_kernel(origins, group, has_total, spot_ref, w_ref, *refs):
    count = len(origins)
    chunk_refs = refs[:count]
    total_ref = refs[count] if has_total else None
    out_ref, sum_ref, w_rows, arrived = refs[-4:]
    depth = w_rows.shape[1]
    copies = []
    for number, (offset, head) in enumerate(origins):
        start = ((spot_ref[0] ^ offset) * group + spot_ref[1 + head]) * depth
        copy = pltpu.make_async_copy(
            w_ref.at[pl.ds(pl.multiple_of(start, depth), depth)], w_rows.at[number], arrived.at[number]
        )
        copy.start()
        copies.append(copy)
    for number in range(count):
        copies[number].wait()
        part = mm(chunk_refs[number][...], w_rows[number])
        if number > 0:
            part += sum_ref[...]
        elif has_total:
            part += total_ref[...]
        if number == count - 1:
            out_ref[...] = part.astype(out_ref.dtype)
        else:
            sum_ref[...] = part


def project(parts, group, spot, weight, total, is_last):
    chunks, origins = [part[0] for part in parts], [part[1:] for part in parts]
    count = len(chunks)
    rows, depth = chunks[0].shape
    columns = weight.shape[1]
    vmem = pl.BlockSpec(memory_space=pltpu.VMEM)
    operands = [spot, weight] + list(chunks) + ([] if total is None else [total])
    return pl.pallas_call(
        functools.partial(project_kernel, origins, group, total is not None),
        out_shape=jax.ShapeDtypeStruct((rows, columns), bf16 if is_last else f32),
        in_specs=[pl.BlockSpec(memory_space=pltpu.SMEM), pl.BlockSpec(memory_space=pltpu.HBM)]
        + [vmem] * (len(operands) - 2),
        out_specs=vmem,
        scratch_shapes=[
            pltpu.VMEM((rows, columns), f32),
            pltpu.VMEM((count, depth, columns), bf16),
            pltpu.SemaphoreType.DMA((count,)),
        ],
        compiler_params=pltpu.CompilerParams(vmem_limit_bytes=PROJECT_BYTES),
        cost_estimate=pl.CostEstimate(
            flops=2 * count * rows * depth * columns,
            bytes_accessed=2 * count * (rows + columns) * depth + 8 * rows * columns,
            transcendentals=0,
        ),
    )(*operands)


OVER_TOKENS = ((0,), (0,))


def forward(keys, gate, lift):
    gate_pre = mm(keys, gate)
    lift_pre = mm(keys, lift)
    logistic = jax.nn.sigmoid(gate_pre)
    silu = gate_pre * logistic
    hidden = (silu * lift_pre).astype(bf16)
    return hidden, lift_pre * (logistic * (1.0 + gate_pre * (1.0 - logistic))), silu


def on_device(
    queries,
    key_rows,
    value_rows,
    learning_rates,
    fast_gate,
    fast_lift,
    fast_down,
    output_gain,
    output_weight,
):
    tokens = queries.shape[0]
    group, width = fast_gate.shape[0], fast_gate.shape[1]
    context = lax.axis_size("ctx")
    columns_of = lax.axis_size("head")
    planes = context // group
    place = lax.axis_index("ctx")
    member, plane = place % group, place // group
    head_place = lax.axis_index("head")

    def to_member(array, by):
        pairs = [(i, i // group * group + (i + by) % group) for i in range(context)]
        return lax.ppermute(array, "ctx", pairs)

    def between_planes(array, pairs):
        return lax.ppermute(
            array,
            "ctx",
            [(a * group + m, b * group + m) for a, b in pairs for m in range(group)],
        )

    def by_side(array, pairs):
        moves = []
        for h in range(columns_of):
            for a, b in pairs:
                a, b = (a, b) if h % 2 == 0 else (planes - 1 - a, planes - 1 - b)
                moves += [
                    ((a * group + m) * columns_of + h, (b * group + m) * columns_of + h) for m in range(group)
                ]
        return lax.ppermute(array, ("ctx", "head"), moves)

    def head_columns(array, by):
        return lax.dynamic_slice_in_dim(array, (member + by) % group * width, width, 1)

    gate, lift, down = (
        lax.dynamic_index_in_dim(w, member, 0, keepdims=False)
        for w in (fast_gate, fast_lift, fast_down)
    )
    gain = lax.dynamic_slice_in_dim(output_gain, member * width, width, 0)[None]

    onward = [(i, i + 1) for i in range(planes - 1)]

    def in_order(blocks):
        return [pick(blocks, (member - j) % group) for j in range(group)]

    keys = [head_columns(key_rows, by) for by in range(group)]
    values = [head_columns(value_rows, by) for by in range(group)]
    asked = [head_columns(queries, by) for by in range(group)]
    rates = [
        lax.dynamic_index_in_dim(learning_rates, (member + by) % group, 0, keepdims=False)
        for by in range(group)
    ]
    sent_keys = keys[-1]
    keys = keys[:1] + [to_member(keys[by], by) for by in range(1, group)]
    rates = rates[:1] + [to_member(after(rates[by], sent_keys), by) for by in range(1, group)]
    values = values[:1] + [to_member(values[by], by) for by in range(1, group)]
    ordered_keys = in_order(keys)
    earlier_keys = between_planes(ordered_keys[-1][-WINDOW:], onward)
    forwards = [forward(block, gate, lift) for block in keys]
    hidden = forwards[-1][0]
    asked = asked[:1] + [to_member(after(asked[by], hidden), by) for by in range(1, group)]
    values = values[:1] + [after(block, hidden) for block in values[1:]]

    hiddens, slopes, silus, scaleds = [], [], [], []
    total_down = 0.0
    for by in range(group):
        hidden, slope, silu = forwards[by]
        scaled = (rates[by][:, None] * values[by].astype(f32)).astype(bf16)
        total_down = total_down + mm(hidden, scaled, OVER_TOKENS)
        slopes.append(slope)
        silus.append(silu)
        scaleds.append(scaled)
    total_gate, total_lift = 0.0, 0.0
    for by in range(group):
        scaled = scaleds[by] if by < group - 1 else after(scaleds[by], total_down, earlier_keys)
        backward = mm(scaled, down, ((1,), (1,)))
        total_gate = total_gate + mm(keys[by], (backward * slopes[by]).astype(bf16), OVER_TOKENS)
        total_lift = total_lift + mm(keys[by], (backward * silus[by]).astype(bf16), OVER_TOKENS)

    ordered_values = in_order([after(block, total_down) for block in values])
    window_values = ordered_values[-1][-WINDOW:]
    values_early = between_planes(window_values, onward[1:])

    rows = width // PIECES

    def cut(matrix):
        return [matrix[piece * rows : (piece + 1) * rows] for piece in range(PIECES)]

    def add_from(own, pairs):
        return own + between_planes(own.astype(bf16), pairs).astype(f32)

    down_levels = tree_mid(planes)
    side_plane = jnp.where(head_place % 2 == 0, plane, planes - 1 - plane)

    def add_side(own, pairs):
        return own + by_side(own.astype(bf16), pairs).astype(f32)

    sum_down = add_side(total_down, down_levels[0])
    odd = plane % 2 == 1
    kept = cut(jnp.where(odd, total_lift, total_gate))
    given = cut(jnp.where(odd, total_gate, total_lift).astype(bf16))
    neighbours = [(i, i ^ 1) for i in range(planes)]
    given = [between_planes(after(other, sum_down, values_early), neighbours) for other in given]
    first_sum = sum_down
    for level in down_levels[1:]:
        sum_down = add_side(sum_down, level)
    kept = [own + got.astype(f32) for own, got in zip(kept, given)]
    met = list(kept)
    values_first = between_planes(after(window_values, *met), onward[:1])
    earlier_values = jnp.where(plane == 1, values_first, values_early)
    middle_plane = side_plane == planes // 2 - 1
    new_down = renew(after(sum_down, values_first, *met), down, middle_plane)
    for level in tree_ends(planes):
        kept = [
            after(own, new_down) + between_planes(own.astype(bf16), level).astype(f32) for own in kept
        ]

    def spread(own, pairs):
        got = between_planes(own, pairs)
        here = functools.reduce(jnp.logical_or, [plane == b for _, b in pairs])
        return jnp.where(here, got, own)

    low_plane, high_plane = plane == 0, plane == planes - 1
    new_sums = jnp.concatenate(kept)
    new_outer = renew(after(new_sums, new_down), jnp.where(low_plane, gate, lift), low_plane | high_plane)
    half = planes // 2
    swap = [(i, (i + half) % planes) for i in range(planes)]
    owners = [pair for pair in swap if pair[0] in (0, planes - 1)]
    others = [pair for pair in swap if pair not in owners]
    is_owner_swap = functools.reduce(jnp.logical_or, [plane == b for _, b in owners])
    near, far = [], []
    owned_down, owner = new_down, planes // 2 - 1
    passed_on = []
    for level in reversed(down_levels):
        from_owner = [(b, a) for a, b in level if b == owner]
        got = by_side(owned_down, from_owner)
        here = functools.reduce(jnp.logical_or, [side_plane == b for _, b in from_owner])
        new_down = jnp.where(here, got, new_down)
        passed_on.append([(b, a) for a, b in level if b != owner])
    near, far = [], []
    for own in cut(new_outer):
        first = between_planes(own, owners)
        passed = own
        for level in spread_halves(planes):
            got = between_planes(own, level)
            here = functools.reduce(jnp.logical_or, [plane == b for _, b in level])
            own = jnp.where(here, got, own)
            passed = got
        passed = passed if len(spread_halves(planes)) == 1 else own
        near.append(own)
        far.append((first, between_planes(passed, others)))
    for pairs in passed_on:
        if pairs:
            got = by_side(after(new_down, near[0]), pairs)
            here = functools.reduce(jnp.logical_or, [side_plane == b for _, b in pairs])
            new_down = jnp.where(here, got, new_down)

    attended = attention(
        after(jnp.concatenate(in_order(asked)), *near),
        earlier_keys,
        jnp.concatenate(ordered_keys),
        earlier_values,
        jnp.concatenate(ordered_values),
        plane,
    )
    lower = plane < half
    far = [jnp.where(is_owner_swap, after(first, attended), after(other, attended)) for first, other in far]
    new_gate = jnp.concatenate([jnp.where(lower, a, b) for a, b in zip(near, far)])
    new_lift = jnp.concatenate([jnp.where(lower, b, a) for a, b in zip(near, far)])
    bits = [1 << k for k in reversed(range(columns_of.bit_length() - 1))]

    def swapped(part, bit):
        return lax.ppermute(part, "head", [(i, i ^ bit) for i in range(columns_of)])

    arrived, combined = [], None
    for by in list(range(1, group)) + [0]:
        wanted = asked[by] if combined is None else after(asked[by], combined)
        combined = apply_fast(wanted, new_gate, new_lift, new_down, attended, gain, (member - by) % group)
        if by > 0:
            arrived.append((to_member(combined, group - by), (member + by) % group))
    arrived = [(combined, member)] + arrived

    spot = jnp.stack([head_place] + [head for _, head in arrived]).astype(jnp.int32)

    def widened(parts, bits):
        for bit in bits:
            parts = [p for part, o, n in parts for p in ((part, o, n), (swapped(part, bit), o ^ bit, n))]
        return parts

    total, waiting = None, []
    for number, (chunk, _) in enumerate(arrived):
        waiting += widened([(chunk, 0, number)], bits[1:])
        far = [(swapped(chunk, bits[0]), bits[0], number)]
        if number == len(arrived) - 1:
            total = project(waiting, group, spot, output_weight, total, False)
            far = [(after(part, total), o, n) for part, o, n in far]
            waiting = []
        waiting += widened(far, bits[1:])
    return project(waiting, group, spot, output_weight, total, True)


def solution(mesh):
    return jax.shard_map(
        on_device,
        mesh=mesh,
        in_specs=(
            P("ctx", "head"),
            P("ctx", "head"),
            P("ctx", "head"),
            P("head", "ctx"),
            P("head", None, None),
            P("head", None, None),
            P("head", None, None),
            P("head"),
            P(None, "head"),
        ),
        out_specs=P("ctx", "head"),
        check_vma=False,
    )
```

```python
import functools
import math

import jax
import jax.numpy as jnp
from jax import lax
from jax.experimental import pallas as pl
from jax.experimental.pallas import tpu as pltpu
from jax.sharding import PartitionSpec as P

ATT_HD = 128
WINDOW = 512
NS_ITERS = 3
PIECES = 2
VMEM_BYTES = 20 * 1024 * 1024
PROJECT_BYTES = 28 * 1024 * 1024

quintic_first = 3.4445
quintic_second = -4.775
quintic_third = 2.0315

f32 = jnp.float32
bf16 = jnp.bfloat16


def mm(a, b, dims=((1,), (0,))):
    return lax.dot_general(a, b, (dims, ((), ())), preferred_element_type=f32)


def after(value, *earlier):
    return lax.optimization_barrier((value, *earlier))[0]


def pick(blocks, which):
    out = blocks[0]
    for number in range(1, len(blocks)):
        out = jnp.where(which == number, blocks[number], out)
    return out


def tree_low(low, high):
    levels, step = [], 1
    while step < high - low:
        levels.append(
            [(i + step, i) for i in range(low, high, 2 * step) if i + step < high]
        )
        step *= 2
    return levels


def tree_high(low, high):
    return [
        [(low + high - 1 - a, low + high - 1 - b) for a, b in level]
        for level in tree_low(low, high)
    ]


def tree_ends(count):
    low = tree_low(0, count // 2)
    return [
        [(2 * a, 2 * b) for a, b in level]
        + [(count - 1 - 2 * a, count - 1 - 2 * b) for a, b in level]
        for level in low
    ]


def tree_mid(count):
    middle = count // 2
    left, right = tree_high(0, middle), tree_low(middle, count)
    levels = []
    for k in range(max(len(left), len(right))):
        levels.append((left[k] if k < len(left) else []) + (right[k] if k < len(right) else []))
    return levels + [[(middle, middle - 1)]]


def spread_ends(count):
    levels, step = [], count // 2
    while step > 1:
        low = [(i, i + step) for i in range(0, count, 2 * step)]
        levels.append(low + [(count - 1 - a, count - 1 - b) for a, b in low])
        step //= 2
    return levels


def attention_kernel(first_ref, q_ref, kp_ref, k_ref, vp_ref, v_ref, out_ref, k_all, v_turned):
    tokens = q_ref.shape[0]
    tile = ATT_HD
    span = WINDOW + tile
    k_all[:WINDOW] = kp_ref[...]
    k_all[WINDOW:] = k_ref[...]
    v_turned[:, :WINDOW] = vp_ref[...].T
    v_turned[:, WINDOW:] = v_ref[...].T
    is_first = first_ref[0] == 0
    key = lax.broadcasted_iota(jnp.int32, (tile, tile), 0)
    query = lax.broadcasted_iota(jnp.int32, (tile, tile), 1)
    scale = ATT_HD**-0.5 * math.log2(math.e)
    for number in range(tokens // tile):
        start = number * tile
        s = mm(k_all[start : start + span], q_ref[start : start + tile], ((1,), (1,)))
        inner = s[tile:WINDOW]
        head_rows = key > query
        if start < WINDOW:
            head_rows = head_rows & jnp.logical_not(is_first)
            place = start + tile + lax.broadcasted_iota(jnp.int32, inner.shape, 0)
            inner = jnp.where((place >= WINDOW) | jnp.logical_not(is_first), inner, -1e30)
        s = jnp.concatenate(
            [
                jnp.where(head_rows, s[:tile], -1e30),
                inner,
                jnp.where(key <= query, s[WINDOW:], -1e30),
            ]
        )
        peak = jnp.max(s, axis=0, keepdims=True)
        w = jnp.exp2((s - peak) * scale)
        total = jnp.sum(w, axis=0, keepdims=True)
        o = mm(v_turned[:, start : start + span], w.astype(bf16))
        out_ref[start : start + tile] = (o / total).T


def attention(q, kp, k, vp, v, plane):
    tokens, width = q.shape
    wide = pl.BlockSpec((tokens, ATT_HD), lambda a, s: (0, a))
    before = pl.BlockSpec((WINDOW, ATT_HD), lambda a, s: (0, a))
    return pl.pallas_call(
        attention_kernel,
        out_shape=jax.ShapeDtypeStruct((tokens, width), f32),
        grid_spec=pltpu.PrefetchScalarGridSpec(
            num_scalar_prefetch=1,
            grid=(width // ATT_HD,),
            in_specs=[wide, before, wide, before, wide],
            out_specs=wide,
            scratch_shapes=[
                pltpu.VMEM((WINDOW + tokens, ATT_HD), bf16),
                pltpu.VMEM((ATT_HD, WINDOW + tokens), bf16),
            ],
        ),
        compiler_params=pltpu.CompilerParams(vmem_limit_bytes=VMEM_BYTES),
        cost_estimate=pl.CostEstimate(
            flops=4 * tokens * (WINDOW + ATT_HD) * width,
            bytes_accessed=12 * tokens * width,
            transcendentals=tokens * (WINDOW + ATT_HD) * (width // ATT_HD),
        ),
    )(jnp.reshape(plane, (1,)).astype(jnp.int32), q, kp, k, vp, v)


def settle_kernel(active_ref, grad_ref, init_ref, out_ref, x_ref):
    @pl.when(active_ref[0] == 1)
    def _():
        g = grad_ref[...]
        square = jnp.sum(jnp.sum(g * g, axis=0, keepdims=True), axis=1, keepdims=True)
        x_ref[...] = (g / (jnp.sqrt(square) + 1e-06)).astype(bf16)

        @pl.loop(0, NS_ITERS)
        def _(_):
            x = x_ref[...]
            gram = mm(x, x, ((1,), (1,))).astype(bf16)
            product = mm(gram, x).astype(bf16)
            second = mm(gram, product)
            x_ref[...] = (
                quintic_first * x.astype(f32)
                + quintic_second * product.astype(f32)
                + quintic_third * second
            ).astype(bf16)

        initial = init_ref[...].astype(f32)
        updated = initial + x_ref[...].astype(f32)
        target = jnp.sqrt(jnp.sum(initial * initial, axis=0, keepdims=True))
        current = jnp.sqrt(jnp.sum(updated * updated, axis=0, keepdims=True) + 1e-06)
        out_ref[...] = (updated * (target / current)).astype(bf16)

    @pl.when(active_ref[0] == 0)
    def _():
        out_ref[...] = jnp.zeros_like(out_ref)


def renew(gradient, initial, active):
    rows, columns = gradient.shape
    vmem = pl.BlockSpec(memory_space=pltpu.VMEM)
    return pl.pallas_call(
        settle_kernel,
        out_shape=jax.ShapeDtypeStruct((rows, columns), bf16),
        in_specs=[pl.BlockSpec(memory_space=pltpu.SMEM), vmem, vmem],
        out_specs=vmem,
        scratch_shapes=[pltpu.VMEM((rows, columns), bf16)],
        compiler_params=pltpu.CompilerParams(vmem_limit_bytes=VMEM_BYTES),
        cost_estimate=pl.CostEstimate(
            flops=6 * NS_ITERS * rows * rows * columns,
            bytes_accessed=8 * rows * columns,
            transcendentals=0,
        ),
    )(jnp.reshape(active, (1,)).astype(jnp.int32), gradient, initial)


def apply_kernel(which_ref, q_ref, gate_ref, lift_ref, down_ref, att_ref, gain_ref, out_ref):
    q = q_ref[...]
    gate = mm(q, gate_ref[...])
    lift = mm(q, lift_ref[...])
    hidden = (gate / (1.0 + jnp.exp(-gate)) * lift).astype(bf16)
    result = mm(hidden, down_ref[...])
    scale = lax.rsqrt(jnp.mean(result * result, axis=1, keepdims=True) + 1e-06)
    out_ref[...] = (att_ref[...] + result * scale * gain_ref[...]).astype(bf16)


def apply_fast(q, gate, lift, down, attended, gain, which):
    tokens, width = q.shape
    rows = min(256, tokens)
    blocks = tokens // rows
    whole = pl.BlockSpec((width, width), lambda i, s: (0, 0))
    return pl.pallas_call(
        apply_kernel,
        out_shape=jax.ShapeDtypeStruct((tokens, width), bf16),
        grid_spec=pltpu.PrefetchScalarGridSpec(
            num_scalar_prefetch=1,
            grid=(blocks,),
            in_specs=[
                pl.BlockSpec((rows, width), lambda i, s: (i, 0)),
                whole,
                whole,
                whole,
                pl.BlockSpec((rows, width), lambda i, s: (s[0] * blocks + i, 0)),
                pl.BlockSpec((1, width), lambda i, s: (0, 0)),
            ],
            out_specs=pl.BlockSpec((rows, width), lambda i, s: (i, 0)),
        ),
        compiler_params=pltpu.CompilerParams(vmem_limit_bytes=VMEM_BYTES),
        cost_estimate=pl.CostEstimate(
            flops=6 * tokens * width * width,
            bytes_accessed=10 * tokens * width + 6 * width * width,
            transcendentals=tokens * width,
        ),
    )(jnp.reshape(which, (1,)).astype(jnp.int32), q, gate, lift, down, attended, gain)


def project_kernel(origins, group, has_total, spot_ref, w_ref, *refs):
    count = len(origins)
    chunk_refs = refs[:count]
    total_ref = refs[count] if has_total else None
    out_ref, sum_ref, w_rows, arrived = refs[-4:]
    depth = w_rows.shape[1]
    copies = []
    for number, (offset, head) in enumerate(origins):
        start = ((spot_ref[0] ^ offset) * group + spot_ref[1 + head]) * depth
        copy = pltpu.make_async_copy(
            w_ref.at[pl.ds(pl.multiple_of(start, depth), depth)], w_rows.at[number], arrived.at[number]
        )
        copy.start()
        copies.append(copy)
    for number in range(count):
        copies[number].wait()
        part = mm(chunk_refs[number][...], w_rows[number])
        if number > 0:
            part += sum_ref[...]
        elif has_total:
            part += total_ref[...]
        if number == count - 1:
            out_ref[...] = part.astype(out_ref.dtype)
        else:
            sum_ref[...] = part


def project(parts, group, spot, weight, total, is_last):
    chunks, origins = [part[0] for part in parts], [part[1:] for part in parts]
    count = len(chunks)
    rows, depth = chunks[0].shape
    columns = weight.shape[1]
    vmem = pl.BlockSpec(memory_space=pltpu.VMEM)
    operands = [spot, weight] + list(chunks) + ([] if total is None else [total])
    return pl.pallas_call(
        functools.partial(project_kernel, origins, group, total is not None),
        out_shape=jax.ShapeDtypeStruct((rows, columns), bf16 if is_last else f32),
        in_specs=[pl.BlockSpec(memory_space=pltpu.SMEM), pl.BlockSpec(memory_space=pltpu.HBM)]
        + [vmem] * (len(operands) - 2),
        out_specs=vmem,
        scratch_shapes=[
            pltpu.VMEM((rows, columns), f32),
            pltpu.VMEM((count, depth, columns), bf16),
            pltpu.SemaphoreType.DMA((count,)),
        ],
        compiler_params=pltpu.CompilerParams(vmem_limit_bytes=PROJECT_BYTES),
        cost_estimate=pl.CostEstimate(
            flops=16 * count * rows * depth * columns,
            bytes_accessed=2 * count * (rows + columns) * depth + 8 * rows * columns,
            transcendentals=0,
        ),
    )(*operands)


OVER_TOKENS = ((0,), (0,))


def forward(keys, gate, lift):
    gate_pre = mm(keys, gate)
    lift_pre = mm(keys, lift)
    logistic = jax.nn.sigmoid(gate_pre)
    silu = gate_pre * logistic
    hidden = (silu * lift_pre).astype(bf16)
    return hidden, lift_pre * (logistic * (1.0 + gate_pre * (1.0 - logistic))), silu


def on_device(
    queries,
    key_rows,
    value_rows,
    learning_rates,
    fast_gate,
    fast_lift,
    fast_down,
    output_gain,
    output_weight,
):
    tokens = queries.shape[0]
    group, width = fast_gate.shape[0], fast_gate.shape[1]
    context = lax.axis_size("ctx")
    columns_of = lax.axis_size("head")
    planes = context // group
    place = lax.axis_index("ctx")
    member, plane = place % group, place // group
    head_place = lax.axis_index("head")

    def to_member(array, by):
        pairs = [(i, i // group * group + (i + by) % group) for i in range(context)]
        return lax.ppermute(array, "ctx", pairs)

    def between_planes(array, pairs):
        return lax.ppermute(
            array,
            "ctx",
            [(a * group + m, b * group + m) for a, b in pairs for m in range(group)],
        )

    def by_side(array, pairs):
        moves = []
        for h in range(columns_of):
            for a, b in pairs:
                a, b = (a, b) if h % 2 == 0 else (planes - 1 - a, planes - 1 - b)
                moves += [
                    ((a * group + m) * columns_of + h, (b * group + m) * columns_of + h) for m in range(group)
                ]
        return lax.ppermute(array, ("ctx", "head"), moves)

    def head_columns(array, by):
        return lax.dynamic_slice_in_dim(array, (member + by) % group * width, width, 1)

    gate, lift, down = (
        lax.dynamic_index_in_dim(w, member, 0, keepdims=False)
        for w in (fast_gate, fast_lift, fast_down)
    )
    gain = lax.dynamic_slice_in_dim(output_gain, member * width, width, 0)[None]

    onward = [(i, i + 1) for i in range(planes - 1)]

    def in_order(blocks):
        return [pick(blocks, (member - j) % group) for j in range(group)]

    keys = [head_columns(key_rows, by) for by in range(group)]
    values = [head_columns(value_rows, by) for by in range(group)]
    asked = [head_columns(queries, by) for by in range(group)]
    rates = [
        lax.dynamic_index_in_dim(learning_rates, (member + by) % group, 0, keepdims=False)
        for by in range(group)
    ]
    sent_keys = keys[-1]
    keys = keys[:1] + [to_member(keys[by], by) for by in range(1, group)]
    rates = rates[:1] + [to_member(after(rates[by], sent_keys), by) for by in range(1, group)]
    values = values[:1] + [to_member(values[by], by) for by in range(1, group)]
    ordered_keys = in_order(keys)
    earlier_keys = between_planes(ordered_keys[-1][-WINDOW:], onward)
    forwards = [forward(block, gate, lift) for block in keys]
    hidden = forwards[-1][0]
    values = values[:1] + [after(block, hidden) for block in values[1:]]

    hiddens, slopes, silus, scaleds = [], [], [], []
    total_down = 0.0
    for by in range(group):
        hidden, slope, silu = forwards[by]
        scaled = (rates[by][:, None] * values[by].astype(f32)).astype(bf16)
        total_down = total_down + mm(hidden, scaled, OVER_TOKENS)
        slopes.append(slope)
        silus.append(silu)
        scaleds.append(scaled)
    total_gate, total_lift = 0.0, 0.0
    for by in range(group):
        scaled = scaleds[by] if by < group - 1 else after(scaleds[by], total_down, earlier_keys)
        backward = mm(scaled, down, ((1,), (1,)))
        total_gate = total_gate + mm(keys[by], (backward * slopes[by]).astype(bf16), OVER_TOKENS)
        total_lift = total_lift + mm(keys[by], (backward * silus[by]).astype(bf16), OVER_TOKENS)

    ordered_values = in_order([after(block, total_down) for block in values])
    window_values = ordered_values[-1][-WINDOW:]
    values_early = between_planes(window_values, onward[1:])

    rows = width // PIECES

    def cut(matrix):
        return [matrix[piece * rows : (piece + 1) * rows] for piece in range(PIECES)]

    def add_from(own, pairs):
        return own + between_planes(own.astype(bf16), pairs).astype(f32)

    down_levels = tree_mid(planes)
    side_plane = jnp.where(head_place % 2 == 0, plane, planes - 1 - plane)

    def add_side(own, pairs):
        return own + by_side(own.astype(bf16), pairs).astype(f32)

    sum_down = add_side(total_down, down_levels[0])
    asked = asked[:1] + [to_member(after(asked[by], sum_down), by) for by in range(1, group)]
    odd = plane % 2 == 1
    kept = cut(jnp.where(odd, total_lift, total_gate))
    given = cut(jnp.where(odd, total_gate, total_lift).astype(bf16))
    neighbours = [(i, i ^ 1) for i in range(planes)]
    given = [between_planes(after(other, sum_down, values_early), neighbours) for other in given]
    first_sum = sum_down
    for level in down_levels[1:]:
        sum_down = add_side(sum_down, level)
    kept = [own + got.astype(f32) for own, got in zip(kept, given)]
    met = list(kept)
    values_first = between_planes(after(window_values, first_sum), onward[:1])
    earlier_values = jnp.where(plane == 1, values_first, values_early)
    middle_plane = side_plane == planes // 2 - 1
    new_down = renew(after(sum_down, values_first, *met), down, middle_plane)
    for level in tree_ends(planes):
        kept = [
            after(own, new_down) + between_planes(own.astype(bf16), level).astype(f32) for own in kept
        ]

    def spread(own, pairs):
        got = between_planes(own, pairs)
        here = functools.reduce(jnp.logical_or, [plane == b for _, b in pairs])
        return jnp.where(here, got, own)

    low_plane, high_plane = plane == 0, plane == planes - 1
    new_sums = jnp.concatenate(kept)
    new_outer = renew(after(new_sums, new_down), jnp.where(low_plane, gate, lift), low_plane | high_plane)
    owned_down, owner = after(new_down, new_sums), planes // 2 - 1
    passed_on = []
    for level in reversed(down_levels):
        from_owner = [(b, a) for a, b in level if b == owner]
        got = by_side(owned_down, from_owner)
        here = functools.reduce(jnp.logical_or, [side_plane == b for _, b in from_owner])
        new_down = jnp.where(here, got, new_down)
        passed_on.append([(b, a) for a, b in level if b != owner])
    far_levels = spread_ends(planes)
    from_ends = [(i, i ^ 1) for i in (0, planes - 1)]
    from_others = [(i, i ^ 1) for i in range(1, planes - 1)]
    near, passed_by = [], []
    for own in cut(new_outer):
        passed = own
        for level in far_levels:
            got = between_planes(own, level)
            here = functools.reduce(jnp.logical_or, [plane == b for _, b in level])
            own = jnp.where(here, got, own)
            passed = got
        near.append(own)
        passed_by.append(passed if len(far_levels) == 1 else own)
    other_ends = between_planes(after(new_outer, passed_by[0]), from_ends)
    others = jnp.concatenate([between_planes(passed, from_others) for passed in passed_by])
    beside_end = (plane == 1) | (plane == planes - 2)
    for pairs in passed_on:
        if pairs:
            got = by_side(after(new_down, near[0]), pairs)
            here = functools.reduce(jnp.logical_or, [side_plane == b for _, b in pairs])
            new_down = jnp.where(here, got, new_down)

    attended = attention(
        after(jnp.concatenate(in_order(asked)), *near),
        earlier_keys,
        jnp.concatenate(ordered_keys),
        earlier_values,
        jnp.concatenate(ordered_values),
        plane,
    )
    other = jnp.where(beside_end, after(other_ends, attended), after(others, attended))
    mine, even = jnp.concatenate(near), plane % 2 == 0
    new_gate, new_lift = jnp.where(even, mine, other), jnp.where(even, other, mine)

    bits = [1 << k for k in reversed(range(columns_of.bit_length() - 1))]

    def swapped(part, bit):
        return lax.ppermute(part, "head", [(i, i ^ bit) for i in range(columns_of)])

    arrived, combined = [], None
    for by in list(range(1, group)) + [0]:
        wanted = asked[by] if combined is None else after(asked[by], combined)
        combined = apply_fast(wanted, new_gate, new_lift, new_down, attended, gain, (member - by) % group)
        if by > 0:
            arrived.append((to_member(combined, group - by), (member + by) % group))
    arrived = [(combined, member)] + arrived

    spot = jnp.stack([head_place] + [head for _, head in arrived]).astype(jnp.int32)

    def widened(parts, bits):
        for bit in bits:
            parts = [p for part, o, n in parts for p in ((part, o, n), (swapped(part, bit), o ^ bit, n))]
        return parts

    total, waiting = None, []
    for number, (chunk, _) in enumerate(arrived):
        waiting += widened([(chunk, 0, number)], bits[1:])
        far = [(swapped(chunk, bits[0]), bits[0], number)]
        if number == len(arrived) - 1:
            total = project(waiting, group, spot, output_weight, total, False)
            far = [(after(part, total), o, n) for part, o, n in far]
            waiting = []
        waiting += widened(far, bits[1:])
    return project(waiting, group, spot, output_weight, total, True)


def solution(mesh):
    return jax.shard_map(
        on_device,
        mesh=mesh,
        in_specs=(
            P("ctx", "head"),
            P("ctx", "head"),
            P("ctx", "head"),
            P("head", "ctx"),
            P("head", None, None),
            P("head", None, None),
            P("head", None, None),
            P("head"),
            P(None, "head"),
        ),
        out_specs=P("ctx", "head"),
        check_vma=False,
    )
```

```python
import functools
import math

import jax
import jax.numpy as jnp
from jax import lax
from jax.experimental import pallas as pl
from jax.experimental.pallas import tpu as pltpu
from jax.sharding import PartitionSpec as P

ATT_HD = 128
WINDOW = 512
NS_ITERS = 3
PIECES = 2
VMEM_BYTES = 20 * 1024 * 1024
PROJECT_BYTES = 28 * 1024 * 1024

quintic_first = 3.4445
quintic_second = -4.775
quintic_third = 2.0315

f32 = jnp.float32
bf16 = jnp.bfloat16


def mm(a, b, dims=((1,), (0,))):
    return lax.dot_general(a, b, (dims, ((), ())), preferred_element_type=f32)


def after(value, *earlier):
    return lax.optimization_barrier((value, *earlier))[0]


def pick(blocks, which):
    out = blocks[0]
    for number in range(1, len(blocks)):
        out = jnp.where(which == number, blocks[number], out)
    return out


def tree_low(low, high):
    levels, step = [], 1
    while step < high - low:
        levels.append(
            [(i + step, i) for i in range(low, high, 2 * step) if i + step < high]
        )
        step *= 2
    return levels


def tree_high(low, high):
    return [
        [(low + high - 1 - a, low + high - 1 - b) for a, b in level]
        for level in tree_low(low, high)
    ]


def tree_ends(count):
    low = tree_low(0, count // 2)
    return [
        [(2 * a, 2 * b) for a, b in level]
        + [(count - 1 - 2 * a, count - 1 - 2 * b) for a, b in level]
        for level in low
    ]


def tree_mid(count):
    middle = count // 2
    left, right = tree_high(0, middle), tree_low(middle, count)
    levels = []
    for k in range(max(len(left), len(right))):
        levels.append((left[k] if k < len(left) else []) + (right[k] if k < len(right) else []))
    return levels + [[(middle, middle - 1)]]


def spread_ends(count):
    levels, step = [], count // 2
    while step > 1:
        low = [(i, i + step) for i in range(0, count, 2 * step)]
        levels.append(low + [(count - 1 - a, count - 1 - b) for a, b in low])
        step //= 2
    return levels


def attention_kernel(first_ref, q_ref, kp_ref, k_ref, vp_ref, v_ref, out_ref, k_all, v_turned):
    tokens = q_ref.shape[0]
    tile = ATT_HD
    span = WINDOW + tile
    k_all[:WINDOW] = kp_ref[...]
    k_all[WINDOW:] = k_ref[...]
    v_turned[:, :WINDOW] = vp_ref[...].T
    v_turned[:, WINDOW:] = v_ref[...].T
    is_first = first_ref[0] == 0
    key = lax.broadcasted_iota(jnp.int32, (tile, tile), 0)
    query = lax.broadcasted_iota(jnp.int32, (tile, tile), 1)
    scale = ATT_HD**-0.5 * math.log2(math.e)
    for number in range(tokens // tile):
        start = number * tile
        s = mm(k_all[start : start + span], q_ref[start : start + tile], ((1,), (1,)))
        inner = s[tile:WINDOW]
        head_rows = key > query
        if start < WINDOW:
            head_rows = head_rows & jnp.logical_not(is_first)
            place = start + tile + lax.broadcasted_iota(jnp.int32, inner.shape, 0)
            inner = jnp.where((place >= WINDOW) | jnp.logical_not(is_first), inner, -1e30)
        s = jnp.concatenate(
            [
                jnp.where(head_rows, s[:tile], -1e30),
                inner,
                jnp.where(key <= query, s[WINDOW:], -1e30),
            ]
        )
        peak = jnp.max(s, axis=0, keepdims=True)
        w = jnp.exp2((s - peak) * scale)
        total = jnp.sum(w, axis=0, keepdims=True)
        o = mm(v_turned[:, start : start + span], w.astype(bf16))
        out_ref[start : start + tile] = (o / total).T


def attention(q, kp, k, vp, v, plane):
    tokens, width = q.shape
    wide = pl.BlockSpec((tokens, ATT_HD), lambda a, s: (0, a))
    before = pl.BlockSpec((WINDOW, ATT_HD), lambda a, s: (0, a))
    return pl.pallas_call(
        attention_kernel,
        out_shape=jax.ShapeDtypeStruct((tokens, width), f32),
        grid_spec=pltpu.PrefetchScalarGridSpec(
            num_scalar_prefetch=1,
            grid=(width // ATT_HD,),
            in_specs=[wide, before, wide, before, wide],
            out_specs=wide,
            scratch_shapes=[
                pltpu.VMEM((WINDOW + tokens, ATT_HD), bf16),
                pltpu.VMEM((ATT_HD, WINDOW + tokens), bf16),
            ],
        ),
        compiler_params=pltpu.CompilerParams(vmem_limit_bytes=VMEM_BYTES),
        cost_estimate=pl.CostEstimate(
            flops=4 * tokens * (WINDOW + ATT_HD) * width,
            bytes_accessed=12 * tokens * width,
            transcendentals=tokens * (WINDOW + ATT_HD) * (width // ATT_HD),
        ),
    )(jnp.reshape(plane, (1,)).astype(jnp.int32), q, kp, k, vp, v)


def settle_kernel(active_ref, grad_ref, init_ref, out_ref, x_ref):
    @pl.when(active_ref[0] == 1)
    def _():
        g = grad_ref[...]
        square = jnp.sum(jnp.sum(g * g, axis=0, keepdims=True), axis=1, keepdims=True)
        x_ref[...] = (g / (jnp.sqrt(square) + 1e-06)).astype(bf16)

        for _ in range(NS_ITERS):
            x = x_ref[...]
            gram = mm(x, x, ((1,), (1,))).astype(bf16)
            product = mm(gram, x).astype(bf16)
            second = mm(gram, product)
            x_ref[...] = (
                quintic_first * x.astype(f32)
                + quintic_second * product.astype(f32)
                + quintic_third * second
            ).astype(bf16)

        initial = init_ref[...].astype(f32)
        updated = initial + x_ref[...].astype(f32)
        target = jnp.sqrt(jnp.sum(initial * initial, axis=0, keepdims=True))
        current = jnp.sqrt(jnp.sum(updated * updated, axis=0, keepdims=True) + 1e-06)
        out_ref[...] = (updated * (target / current)).astype(bf16)

    @pl.when(active_ref[0] == 0)
    def _():
        out_ref[...] = jnp.zeros_like(out_ref)


def renew(gradient, initial, active):
    rows, columns = gradient.shape
    vmem = pl.BlockSpec(memory_space=pltpu.VMEM)
    return pl.pallas_call(
        settle_kernel,
        out_shape=jax.ShapeDtypeStruct((rows, columns), bf16),
        in_specs=[pl.BlockSpec(memory_space=pltpu.SMEM), vmem, vmem],
        out_specs=vmem,
        scratch_shapes=[pltpu.VMEM((rows, columns), bf16)],
        compiler_params=pltpu.CompilerParams(vmem_limit_bytes=VMEM_BYTES),
        cost_estimate=pl.CostEstimate(
            flops=6 * NS_ITERS * rows * rows * columns,
            bytes_accessed=8 * rows * columns,
            transcendentals=0,
        ),
    )(jnp.reshape(active, (1,)).astype(jnp.int32), gradient, initial)


def apply_kernel(which_ref, q_ref, gate_ref, lift_ref, down_ref, att_ref, gain_ref, *out_refs):
    q = q_ref[...]
    gate = mm(q, gate_ref[...])
    lift = mm(q, lift_ref[...])
    hidden = (gate / (1.0 + jnp.exp(-gate)) * lift).astype(bf16)
    result = mm(hidden, down_ref[...])
    scale = lax.rsqrt(jnp.mean(result * result, axis=1, keepdims=True) + 1e-06)
    combined = (att_ref[...] + result * scale * gain_ref[...]).astype(bf16)
    for number, out_ref in enumerate(out_refs):

        @pl.when(pl.program_id(0) == number)
        def _(out_ref=out_ref):
            out_ref[...] = combined


def apply_fast(q, gate, lift, down, attended, gain, order):
    rows, width = q.shape
    count = len(order)
    tokens = rows // count
    whole = pl.BlockSpec((width, width), lambda i, s: (0, 0))
    picked = pl.BlockSpec((tokens, width), lambda i, s: (s[i], 0))
    return pl.pallas_call(
        apply_kernel,
        out_shape=[jax.ShapeDtypeStruct((tokens, width), bf16)] * count,
        grid_spec=pltpu.PrefetchScalarGridSpec(
            num_scalar_prefetch=1,
            grid=(count,),
            in_specs=[picked, whole, whole, whole, picked, pl.BlockSpec((1, width), lambda i, s: (0, 0))],
            out_specs=[pl.BlockSpec((tokens, width), lambda i, s: (0, 0))] * count,
        ),
        compiler_params=pltpu.CompilerParams(vmem_limit_bytes=VMEM_BYTES),
        cost_estimate=pl.CostEstimate(
            flops=6 * rows * width * width,
            bytes_accessed=10 * rows * width + 6 * width * width,
            transcendentals=rows * width,
        ),
    )(jnp.stack(order).astype(jnp.int32), q, gate, lift, down, attended, gain)


def project_kernel(origins, group, has_total, spot_ref, w_ref, *refs):
    count = len(origins)
    chunk_refs = refs[:count]
    total_ref = refs[count] if has_total else None
    out_ref, joined, w_rows, arrived = refs[-4:]
    depth = chunk_refs[0].shape[1]
    copies = []
    for number, (offset, head) in enumerate(origins):
        start = ((spot_ref[0] ^ offset) * group + spot_ref[1 + head]) * depth
        copy = pltpu.make_async_copy(
            w_ref.at[pl.ds(pl.multiple_of(start, depth), depth)],
            w_rows.at[pl.ds(number * depth, depth)],
            arrived.at[number],
        )
        copy.start()
        copies.append(copy)
    for number in range(count):
        joined[:, number * depth : (number + 1) * depth] = chunk_refs[number][...]
    for copy in copies:
        copy.wait()
    result = mm(joined[...], w_rows[...])
    if has_total:
        result += total_ref[...]
    out_ref[...] = result.astype(out_ref.dtype)


def project(parts, group, spot, weight, total, is_last):
    chunks, origins = [part[0] for part in parts], [part[1:] for part in parts]
    count = len(chunks)
    rows, depth = chunks[0].shape
    columns = weight.shape[1]
    vmem = pl.BlockSpec(memory_space=pltpu.VMEM)
    operands = [spot, weight] + list(chunks) + ([] if total is None else [total])
    return pl.pallas_call(
        functools.partial(project_kernel, origins, group, total is not None),
        out_shape=jax.ShapeDtypeStruct((rows, columns), bf16 if is_last else f32),
        in_specs=[pl.BlockSpec(memory_space=pltpu.SMEM), pl.BlockSpec(memory_space=pltpu.HBM)]
        + [vmem] * (len(operands) - 2),
        out_specs=vmem,
        scratch_shapes=[
            pltpu.VMEM((rows, count * depth), bf16),
            pltpu.VMEM((count * depth, columns), bf16),
            pltpu.SemaphoreType.DMA((count,)),
        ],
        compiler_params=pltpu.CompilerParams(vmem_limit_bytes=PROJECT_BYTES),
        cost_estimate=pl.CostEstimate(
            flops=16 * count * rows * depth * columns,
            bytes_accessed=2 * count * (rows + columns) * depth + 8 * rows * columns,
            transcendentals=0,
        ),
    )(*operands)


OVER_TOKENS = ((0,), (0,))


def forward(keys, gate, lift):
    gate_pre = mm(keys, gate)
    lift_pre = mm(keys, lift)
    logistic = jax.nn.sigmoid(gate_pre)
    silu = gate_pre * logistic
    hidden = (silu * lift_pre).astype(bf16)
    return hidden, lift_pre * (logistic * (1.0 + gate_pre * (1.0 - logistic))), silu


def on_device(
    queries,
    key_rows,
    value_rows,
    learning_rates,
    fast_gate,
    fast_lift,
    fast_down,
    output_gain,
    output_weight,
):
    tokens = queries.shape[0]
    group, width = fast_gate.shape[0], fast_gate.shape[1]
    context = lax.axis_size("ctx")
    columns_of = lax.axis_size("head")
    planes = context // group
    place = lax.axis_index("ctx")
    member, plane = place % group, place // group
    head_place = lax.axis_index("head")

    def to_member(array, by):
        pairs = [(i, i // group * group + (i + by) % group) for i in range(context)]
        return lax.ppermute(array, "ctx", pairs)

    def between_planes(array, pairs):
        return lax.ppermute(
            array,
            "ctx",
            [(a * group + m, b * group + m) for a, b in pairs for m in range(group)],
        )

    def by_side(array, pairs):
        moves = []
        for h in range(columns_of):
            for a, b in pairs:
                a, b = (a, b) if h % 2 == 0 else (planes - 1 - a, planes - 1 - b)
                moves += [
                    ((a * group + m) * columns_of + h, (b * group + m) * columns_of + h) for m in range(group)
                ]
        return lax.ppermute(array, ("ctx", "head"), moves)

    def head_columns(array, by):
        return lax.dynamic_slice_in_dim(array, (member + by) % group * width, width, 1)

    gate, lift, down = (
        lax.dynamic_index_in_dim(w, member, 0, keepdims=False)
        for w in (fast_gate, fast_lift, fast_down)
    )
    gain = lax.dynamic_slice_in_dim(output_gain, member * width, width, 0)[None]

    onward = [(i, i + 1) for i in range(planes - 1)]

    def in_order(blocks):
        return [pick(blocks, (member - j) % group) for j in range(group)]

    keys = [head_columns(key_rows, by) for by in range(group)]
    values = [head_columns(value_rows, by) for by in range(group)]
    asked = [head_columns(queries, by) for by in range(group)]
    rates = [
        lax.dynamic_index_in_dim(learning_rates, (member + by) % group, 0, keepdims=False)
        for by in range(group)
    ]
    sent_keys = keys[-1]
    keys = keys[:1] + [to_member(keys[by], by) for by in range(1, group)]
    rates = rates[:1] + [to_member(after(rates[by], sent_keys), by) for by in range(1, group)]
    values = values[:1] + [to_member(values[by], by) for by in range(1, group)]
    ordered_keys = in_order(keys)
    earlier_keys = between_planes(ordered_keys[-1][-WINDOW:], onward)
    forwards = [forward(block, gate, lift) for block in keys]
    hidden = forwards[-1][0]
    values = values[:1] + [after(block, hidden) for block in values[1:]]

    hiddens, slopes, silus, scaleds = [], [], [], []
    total_down = 0.0
    for by in range(group):
        hidden, slope, silu = forwards[by]
        scaled = (rates[by][:, None] * values[by].astype(f32)).astype(bf16)
        total_down = total_down + mm(hidden, scaled, OVER_TOKENS)
        slopes.append(slope)
        silus.append(silu)
        scaleds.append(scaled)
    total_gate, total_lift = 0.0, 0.0
    for by in range(group):
        scaled = scaleds[by] if by < group - 1 else after(scaleds[by], total_down, earlier_keys)
        backward = mm(scaled, down, ((1,), (1,)))
        total_gate = total_gate + mm(keys[by], (backward * slopes[by]).astype(bf16), OVER_TOKENS)
        total_lift = total_lift + mm(keys[by], (backward * silus[by]).astype(bf16), OVER_TOKENS)

    ordered_values = in_order([after(block, backward) for block in values])
    window_values = ordered_values[-1][-WINDOW:]
    values_early = between_planes(window_values, onward[1:])

    rows = width // PIECES

    def cut(matrix):
        return [matrix[piece * rows : (piece + 1) * rows] for piece in range(PIECES)]

    def add_from(own, pairs):
        return own + between_planes(own.astype(bf16), pairs).astype(f32)

    down_levels = tree_mid(planes)
    side_plane = jnp.where(head_place % 2 == 0, plane, planes - 1 - plane)

    def add_side(own, pairs):
        return own + by_side(own.astype(bf16), pairs).astype(f32)

    sum_down = add_side(total_down, down_levels[0])
    asked = asked[:1] + [to_member(after(asked[by], sum_down), by) for by in range(1, group)]
    odd = plane % 2 == 1
    kept = jnp.where(odd, total_lift, total_gate)
    given = jnp.where(odd, total_gate, total_lift).astype(bf16)
    neighbours = [(i, i ^ 1) for i in range(planes)]
    given = between_planes(after(given, sum_down, values_early), neighbours)
    first_sum = sum_down
    for level in down_levels[1:]:
        sum_down = add_side(sum_down, level)
    kept = kept + given.astype(f32)
    met = [kept]
    values_first = between_planes(after(window_values, first_sum), onward[:1])
    earlier_values = jnp.where(plane == 1, values_first, values_early)
    middle_plane = side_plane == planes // 2 - 1
    new_down = renew(after(sum_down, values_first, *met), down, middle_plane)
    for level in tree_ends(planes):
        kept = after(kept, new_down) + between_planes(kept.astype(bf16), level).astype(f32)

    def spread(own, pairs):
        got = between_planes(own, pairs)
        here = functools.reduce(jnp.logical_or, [plane == b for _, b in pairs])
        return jnp.where(here, got, own)

    low_plane, high_plane = plane == 0, plane == planes - 1
    new_sums = kept
    new_outer = renew(after(new_sums, new_down), jnp.where(low_plane, gate, lift), low_plane | high_plane)
    owned_down, owner = after(new_down, new_sums), planes // 2 - 1
    passed_on = []
    for level in reversed(down_levels):
        from_owner = [(b, a) for a, b in level if b == owner]
        got = by_side(owned_down, from_owner)
        here = functools.reduce(jnp.logical_or, [side_plane == b for _, b in from_owner])
        new_down = jnp.where(here, got, new_down)
        passed_on.append([(b, a) for a, b in level if b != owner])
    far_levels = spread_ends(planes)
    from_ends = [(i, i ^ 1) for i in (0, planes - 1)]
    from_others = [(i, i ^ 1) for i in range(1, planes - 1)]
    near, passed_by = [], []
    for own in cut(new_outer):
        passed = own
        for level in far_levels:
            got = between_planes(own, level)
            here = functools.reduce(jnp.logical_or, [plane == b for _, b in level])
            own = jnp.where(here, got, own)
            passed = got
        near.append(own)
        passed_by.append(passed if len(far_levels) == 1 else own)
    other_ends = between_planes(after(new_outer, passed_by[0]), from_ends)
    others = jnp.concatenate([between_planes(passed, from_others) for passed in passed_by])
    beside_end = (plane == 1) | (plane == planes - 2)
    for pairs in passed_on:
        if pairs:
            got = by_side(after(new_down, near[0]), pairs)
            here = functools.reduce(jnp.logical_or, [side_plane == b for _, b in pairs])
            new_down = jnp.where(here, got, new_down)

    all_asked = jnp.concatenate(in_order(asked))
    attended = attention(
        after(all_asked, *near),
        earlier_keys,
        jnp.concatenate(ordered_keys),
        earlier_values,
        jnp.concatenate(ordered_values),
        plane,
    )
    other = jnp.where(beside_end, after(other_ends, attended), after(others, attended))
    mine, even = jnp.concatenate(near), plane % 2 == 0
    new_gate, new_lift = jnp.where(even, mine, other), jnp.where(even, other, mine)

    bits = [1 << k for k in reversed(range(columns_of.bit_length() - 1))]

    def swapped(part, bit):
        return lax.ppermute(part, "head", [(i, i ^ bit) for i in range(columns_of)])

    turns = list(range(1, group)) + [0]
    combined = apply_fast(
        all_asked, new_gate, new_lift, new_down, attended, gain, [(member - by) % group for by in turns]
    )
    arrived = [
        (to_member(rows_of, group - by), (member + by) % group) for by, rows_of in zip(turns[:-1], combined)
    ]
    combined = combined[-1]
    arrived = [(combined, member)] + arrived

    spot = jnp.stack([head_place] + [head for _, head in arrived]).astype(jnp.int32)
    parts = [(chunk, 0, number) for number, (chunk, _) in enumerate(arrived)]
    parts += [(swapped(chunk, bits[0]), bits[0], number) for number, (chunk, _) in enumerate(arrived)]
    total = project(parts[:-1], group, spot, output_weight, None, False)
    last, offset, number = parts[-1]
    parts[-1] = (after(last, total), offset, number)
    copies = [(after(part, parts[-1][0]), o, n) for part, o, n in parts]
    for bit in bits[1:]:
        copies += [(swapped(part, bit), o ^ bit, n) for part, o, n in copies]
    total = project(parts[-1:], group, spot, output_weight, total, False)
    return project(copies[len(parts) :], group, spot, output_weight, total, True)


def solution(mesh):
    return jax.shard_map(
        on_device,
        mesh=mesh,
        in_specs=(
            P("ctx", "head"),
            P("ctx", "head"),
            P("ctx", "head"),
            P("head", "ctx"),
            P("head", None, None),
            P("head", None, None),
            P("head", None, None),
            P("head"),
            P(None, "head"),
        ),
        out_specs=P("ctx", "head"),
        check_vma=False,
    )
```

```python
import functools
import math

import jax
import jax.numpy as jnp
from jax import lax
from jax.experimental import pallas as pl
from jax.experimental.pallas import tpu as pltpu
from jax.sharding import PartitionSpec as P

ATT_HD = 128
WINDOW = 512
NS_ITERS = 3
PIECES = 2
VMEM_BYTES = 20 * 1024 * 1024
PROJECT_BYTES = 28 * 1024 * 1024

quintic_first = 3.4445
quintic_second = -4.775
quintic_third = 2.0315

f32 = jnp.float32
bf16 = jnp.bfloat16


def mm(a, b, dims=((1,), (0,))):
    return lax.dot_general(a, b, (dims, ((), ())), preferred_element_type=f32)


def after(value, *earlier):
    return lax.optimization_barrier((value, *earlier))[0]


def pick(blocks, which):
    out = blocks[0]
    for number in range(1, len(blocks)):
        out = jnp.where(which == number, blocks[number], out)
    return out


def tree_low(low, high):
    levels, step = [], 1
    while step < high - low:
        levels.append(
            [(i + step, i) for i in range(low, high, 2 * step) if i + step < high]
        )
        step *= 2
    return levels


def tree_high(low, high):
    return [
        [(low + high - 1 - a, low + high - 1 - b) for a, b in level]
        for level in tree_low(low, high)
    ]


def tree_ends(count):
    low = tree_low(0, count // 2)
    return [
        [(2 * a, 2 * b) for a, b in level]
        + [(count - 1 - 2 * a, count - 1 - 2 * b) for a, b in level]
        for level in low
    ]


def tree_mid(count):
    middle = count // 2
    left, right = tree_high(0, middle), tree_low(middle, count)
    levels = []
    for k in range(max(len(left), len(right))):
        levels.append((left[k] if k < len(left) else []) + (right[k] if k < len(right) else []))
    return levels + [[(middle, middle - 1)]]


def spread_ends(count):
    levels, step = [], count // 2
    while step > 1:
        low = [(i, i + step) for i in range(0, count, 2 * step)]
        levels.append(low + [(count - 1 - a, count - 1 - b) for a, b in low])
        step //= 2
    return levels


def attention_kernel(first_ref, q_ref, kp_ref, k_ref, vp_ref, v_ref, out_ref, k_all, v_turned):
    tokens = q_ref.shape[0]
    tile = ATT_HD
    span = WINDOW + tile
    k_all[:WINDOW] = kp_ref[...]
    k_all[WINDOW:] = k_ref[...]
    v_turned[:, :WINDOW] = vp_ref[...].T
    v_turned[:, WINDOW:] = v_ref[...].T
    is_first = first_ref[0] == 0
    key = lax.broadcasted_iota(jnp.int32, (tile, tile), 0)
    query = lax.broadcasted_iota(jnp.int32, (tile, tile), 1)
    scale = ATT_HD**-0.5 * math.log2(math.e)
    for number in range(tokens // tile):
        start = number * tile
        s = mm(k_all[start : start + span], q_ref[start : start + tile], ((1,), (1,)))
        inner = s[tile:WINDOW]
        head_rows = key > query
        if start < WINDOW:
            head_rows = head_rows & jnp.logical_not(is_first)
            place = start + tile + lax.broadcasted_iota(jnp.int32, inner.shape, 0)
            inner = jnp.where((place >= WINDOW) | jnp.logical_not(is_first), inner, -1e30)
        s = jnp.concatenate(
            [
                jnp.where(head_rows, s[:tile], -1e30),
                inner,
                jnp.where(key <= query, s[WINDOW:], -1e30),
            ]
        )
        peak = jnp.max(s, axis=0, keepdims=True)
        w = jnp.exp2((s - peak) * scale)
        total = jnp.sum(w, axis=0, keepdims=True)
        o = mm(v_turned[:, start : start + span], w.astype(bf16))
        out_ref[start : start + tile] = (o / total).T


def attention(q, kp, k, vp, v, plane):
    tokens, width = q.shape
    wide = pl.BlockSpec((tokens, ATT_HD), lambda a, s: (0, a))
    before = pl.BlockSpec((WINDOW, ATT_HD), lambda a, s: (0, a))
    return pl.pallas_call(
        attention_kernel,
        out_shape=jax.ShapeDtypeStruct((tokens, width), f32),
        grid_spec=pltpu.PrefetchScalarGridSpec(
            num_scalar_prefetch=1,
            grid=(width // ATT_HD,),
            in_specs=[wide, before, wide, before, wide],
            out_specs=wide,
            scratch_shapes=[
                pltpu.VMEM((WINDOW + tokens, ATT_HD), bf16),
                pltpu.VMEM((ATT_HD, WINDOW + tokens), bf16),
            ],
        ),
        compiler_params=pltpu.CompilerParams(vmem_limit_bytes=VMEM_BYTES),
        cost_estimate=pl.CostEstimate(
            flops=4 * tokens * (WINDOW + ATT_HD) * width,
            bytes_accessed=12 * tokens * width,
            transcendentals=tokens * (WINDOW + ATT_HD) * (width // ATT_HD),
        ),
    )(jnp.reshape(plane, (1,)).astype(jnp.int32), q, kp, k, vp, v)


def settle_kernel(active_ref, grad_ref, init_ref, out_ref, x_ref):
    @pl.when(active_ref[0] == 1)
    def _():
        g = grad_ref[...]
        square = jnp.sum(jnp.sum(g * g, axis=0, keepdims=True), axis=1, keepdims=True)
        x_ref[...] = (g / (jnp.sqrt(square) + 1e-06)).astype(bf16)

        for _ in range(NS_ITERS):
            x = x_ref[...]
            gram = mm(x, x, ((1,), (1,))).astype(bf16)
            product = mm(gram, x).astype(bf16)
            second = mm(gram, product)
            x_ref[...] = (
                quintic_first * x.astype(f32)
                + quintic_second * product.astype(f32)
                + quintic_third * second
            ).astype(bf16)

        initial = init_ref[...].astype(f32)
        updated = initial + x_ref[...].astype(f32)
        target = jnp.sqrt(jnp.sum(initial * initial, axis=0, keepdims=True))
        current = jnp.sqrt(jnp.sum(updated * updated, axis=0, keepdims=True) + 1e-06)
        out_ref[...] = (updated * (target / current)).astype(bf16)

    @pl.when(active_ref[0] == 0)
    def _():
        out_ref[...] = jnp.zeros_like(out_ref)


def renew(gradient, initial, active):
    rows, columns = gradient.shape
    vmem = pl.BlockSpec(memory_space=pltpu.VMEM)
    return pl.pallas_call(
        settle_kernel,
        out_shape=jax.ShapeDtypeStruct((rows, columns), bf16),
        in_specs=[pl.BlockSpec(memory_space=pltpu.SMEM), vmem, vmem],
        out_specs=vmem,
        scratch_shapes=[pltpu.VMEM((rows, columns), bf16)],
        compiler_params=pltpu.CompilerParams(vmem_limit_bytes=VMEM_BYTES),
        cost_estimate=pl.CostEstimate(
            flops=6 * NS_ITERS * rows * rows * columns,
            bytes_accessed=8 * rows * columns,
            transcendentals=0,
        ),
    )(jnp.reshape(active, (1,)).astype(jnp.int32), gradient, initial)


def apply_kernel(which_ref, q_ref, gate_ref, lift_ref, down_ref, att_ref, gain_ref, *out_refs):
    q = q_ref[...]
    gate = mm(q, gate_ref[...])
    lift = mm(q, lift_ref[...])
    hidden = (gate / (1.0 + jnp.exp(-gate)) * lift).astype(bf16)
    result = mm(hidden, down_ref[...])
    scale = lax.rsqrt(jnp.mean(result * result, axis=1, keepdims=True) + 1e-06)
    combined = (att_ref[...] + result * scale * gain_ref[...]).astype(bf16)
    for number, out_ref in enumerate(out_refs):

        @pl.when(pl.program_id(0) == number)
        def _(out_ref=out_ref):
            out_ref[...] = combined


def apply_fast(q, gate, lift, down, attended, gain, order):
    rows, width = q.shape
    count = len(order)
    tokens = rows // count
    whole = pl.BlockSpec((width, width), lambda i, s: (0, 0))
    picked = pl.BlockSpec((tokens, width), lambda i, s: (s[i], 0))
    return pl.pallas_call(
        apply_kernel,
        out_shape=[jax.ShapeDtypeStruct((tokens, width), bf16)] * count,
        grid_spec=pltpu.PrefetchScalarGridSpec(
            num_scalar_prefetch=1,
            grid=(count,),
            in_specs=[picked, whole, whole, whole, picked, pl.BlockSpec((1, width), lambda i, s: (0, 0))],
            out_specs=[pl.BlockSpec((tokens, width), lambda i, s: (0, 0))] * count,
        ),
        compiler_params=pltpu.CompilerParams(vmem_limit_bytes=VMEM_BYTES),
        cost_estimate=pl.CostEstimate(
            flops=6 * rows * width * width,
            bytes_accessed=10 * rows * width + 6 * width * width,
            transcendentals=rows * width,
        ),
    )(jnp.stack(order).astype(jnp.int32), q, gate, lift, down, attended, gain)


def project_kernel(origins, group, has_total, spot_ref, w_ref, *refs):
    count = len(origins)
    chunk_refs = refs[:count]
    total_ref = refs[count] if has_total else None
    out_ref, joined, w_rows, arrived = refs[-4:]
    depth = chunk_refs[0].shape[1]
    copies = []
    for number, (offset, head) in enumerate(origins):
        start = ((spot_ref[0] ^ offset) * group + spot_ref[1 + head]) * depth
        copy = pltpu.make_async_copy(
            w_ref.at[pl.ds(pl.multiple_of(start, depth), depth)],
            w_rows.at[pl.ds(number * depth, depth)],
            arrived.at[number],
        )
        copy.start()
        copies.append(copy)
    for number in range(count):
        joined[:, number * depth : (number + 1) * depth] = chunk_refs[number][...]
    for copy in copies:
        copy.wait()
    tile = math.gcd(out_ref.shape[1], 256)

    @pl.loop(0, out_ref.shape[1] // tile)
    def _(number):
        at = pl.ds(pl.multiple_of(number * tile, tile), tile)
        result = mm(joined[...], w_rows[:, at])
        if has_total:
            result += total_ref[:, at]
        out_ref[:, at] = result.astype(out_ref.dtype)


def project(parts, group, spot, weight, total, is_last):
    chunks, origins = [part[0] for part in parts], [part[1:] for part in parts]
    count = len(chunks)
    rows, depth = chunks[0].shape
    columns = weight.shape[1]
    vmem = pl.BlockSpec(memory_space=pltpu.VMEM)
    operands = [spot, weight] + list(chunks) + ([] if total is None else [total])
    return pl.pallas_call(
        functools.partial(project_kernel, origins, group, total is not None),
        out_shape=jax.ShapeDtypeStruct((rows, columns), bf16 if is_last else f32),
        in_specs=[pl.BlockSpec(memory_space=pltpu.SMEM), pl.BlockSpec(memory_space=pltpu.HBM)]
        + [vmem] * (len(operands) - 2),
        out_specs=vmem,
        scratch_shapes=[
            pltpu.VMEM((rows, count * depth), bf16),
            pltpu.VMEM((count * depth, columns), bf16),
            pltpu.SemaphoreType.DMA((count,)),
        ],
        compiler_params=pltpu.CompilerParams(vmem_limit_bytes=PROJECT_BYTES),
        cost_estimate=pl.CostEstimate(
            flops=16 * count * rows * depth * columns,
            bytes_accessed=2 * count * (rows + columns) * depth + 8 * rows * columns,
            transcendentals=0,
        ),
    )(*operands)


OVER_TOKENS = ((0,), (0,))


def forward(keys, gate, lift):
    gate_pre = mm(keys, gate)
    lift_pre = mm(keys, lift)
    logistic = jax.nn.sigmoid(gate_pre)
    silu = gate_pre * logistic
    hidden = (silu * lift_pre).astype(bf16)
    return hidden, lift_pre * (logistic * (1.0 + gate_pre * (1.0 - logistic))), silu


def on_device(
    queries,
    key_rows,
    value_rows,
    learning_rates,
    fast_gate,
    fast_lift,
    fast_down,
    output_gain,
    output_weight,
):
    tokens = queries.shape[0]
    group, width = fast_gate.shape[0], fast_gate.shape[1]
    context = lax.axis_size("ctx")
    columns_of = lax.axis_size("head")
    planes = context // group
    place = lax.axis_index("ctx")
    member, plane = place % group, place // group
    head_place = lax.axis_index("head")

    def to_member(array, by):
        pairs = [(i, i // group * group + (i + by) % group) for i in range(context)]
        return lax.ppermute(array, "ctx", pairs)

    def between_planes(array, pairs):
        return lax.ppermute(
            array,
            "ctx",
            [(a * group + m, b * group + m) for a, b in pairs for m in range(group)],
        )

    def by_side(array, pairs):
        moves = []
        for h in range(columns_of):
            for a, b in pairs:
                a, b = (a, b) if h % 2 == 0 else (planes - 1 - a, planes - 1 - b)
                moves += [
                    ((a * group + m) * columns_of + h, (b * group + m) * columns_of + h) for m in range(group)
                ]
        return lax.ppermute(array, ("ctx", "head"), moves)

    def head_columns(array, by):
        return lax.dynamic_slice_in_dim(array, (member + by) % group * width, width, 1)

    gate, lift, down = (
        lax.dynamic_index_in_dim(w, member, 0, keepdims=False)
        for w in (fast_gate, fast_lift, fast_down)
    )
    gain = lax.dynamic_slice_in_dim(output_gain, member * width, width, 0)[None]

    onward = [(i, i + 1) for i in range(planes - 1)]

    def in_order(blocks):
        return [pick(blocks, (member - j) % group) for j in range(group)]

    keys = [head_columns(key_rows, by) for by in range(group)]
    values = [head_columns(value_rows, by) for by in range(group)]
    asked = [head_columns(queries, by) for by in range(group)]
    rates = [
        lax.dynamic_index_in_dim(learning_rates, (member + by) % group, 0, keepdims=False)
        for by in range(group)
    ]
    sent_keys = keys[-1]
    keys = keys[:1] + [to_member(keys[by], by) for by in range(1, group)]
    rates = rates[:1] + [to_member(after(rates[by], sent_keys), by) for by in range(1, group)]
    values = values[:1] + [to_member(values[by], by) for by in range(1, group)]
    ordered_keys = in_order(keys)
    earlier_keys = between_planes(ordered_keys[-1][-WINDOW:], onward)
    forwards = [forward(block, gate, lift) for block in keys]
    hidden = forwards[-1][0]
    values = values[:1] + [after(block, hidden) for block in values[1:]]

    hiddens, slopes, silus, scaleds = [], [], [], []
    total_down = 0.0
    for by in range(group):
        hidden, slope, silu = forwards[by]
        scaled = (rates[by][:, None] * values[by].astype(f32)).astype(bf16)
        total_down = total_down + mm(hidden, scaled, OVER_TOKENS)
        slopes.append(slope)
        silus.append(silu)
        scaleds.append(scaled)
    total_gate, total_lift = 0.0, 0.0
    for by in range(group):
        scaled = scaleds[by] if by < group - 1 else after(scaleds[by], total_down, earlier_keys)
        backward = mm(scaled, down, ((1,), (1,)))
        total_gate = total_gate + mm(keys[by], (backward * slopes[by]).astype(bf16), OVER_TOKENS)
        total_lift = total_lift + mm(keys[by], (backward * silus[by]).astype(bf16), OVER_TOKENS)

    ordered_values = in_order([after(block, backward) for block in values])
    window_values = ordered_values[-1][-WINDOW:]
    values_early = between_planes(window_values, onward[1:])

    rows = width // PIECES

    def cut(matrix):
        return [matrix[piece * rows : (piece + 1) * rows] for piece in range(PIECES)]

    def add_from(own, pairs):
        return own + between_planes(own.astype(bf16), pairs).astype(f32)

    down_levels = tree_mid(planes)
    side_plane = jnp.where(head_place % 2 == 0, plane, planes - 1 - plane)

    def add_side(own, pairs):
        return own + by_side(own.astype(bf16), pairs).astype(f32)

    sum_down = add_side(total_down, down_levels[0])
    asked = asked[:1] + [to_member(after(asked[by], sum_down), by) for by in range(1, group)]
    odd = plane % 2 == 1
    kept = jnp.where(odd, total_lift, total_gate)
    given = jnp.where(odd, total_gate, total_lift).astype(bf16)
    neighbours = [(i, i ^ 1) for i in range(planes)]
    given = between_planes(after(given, sum_down, values_early), neighbours)
    first_sum = sum_down
    for level in down_levels[1:]:
        sum_down = add_side(sum_down, level)
    kept = kept + given.astype(f32)
    met = [kept]
    values_first = between_planes(after(window_values, first_sum), onward[:1])
    earlier_values = jnp.where(plane == 1, values_first, values_early)
    middle_plane = side_plane == planes // 2 - 1
    new_down = renew(after(sum_down, values_first, *met), down, middle_plane)
    for level in tree_ends(planes):
        kept = after(kept, new_down) + between_planes(kept.astype(bf16), level).astype(f32)

    def spread(own, pairs):
        got = between_planes(own, pairs)
        here = functools.reduce(jnp.logical_or, [plane == b for _, b in pairs])
        return jnp.where(here, got, own)

    low_plane, high_plane = plane == 0, plane == planes - 1
    new_sums = kept
    new_outer = renew(after(new_sums, new_down), jnp.where(low_plane, gate, lift), low_plane | high_plane)
    owned_down, owner = after(new_down, new_sums), planes // 2 - 1
    passed_on = []
    for level in reversed(down_levels):
        from_owner = [(b, a) for a, b in level if b == owner]
        got = by_side(owned_down, from_owner)
        here = functools.reduce(jnp.logical_or, [side_plane == b for _, b in from_owner])
        new_down = jnp.where(here, got, new_down)
        passed_on.append([(b, a) for a, b in level if b != owner])
    far_levels = spread_ends(planes)
    from_ends = [(i, i ^ 1) for i in (0, planes - 1)]
    from_others = [(i, i ^ 1) for i in range(1, planes - 1)]
    near, passed_by = [], []
    for own in cut(new_outer):
        passed = own
        for level in far_levels:
            got = between_planes(own, level)
            here = functools.reduce(jnp.logical_or, [plane == b for _, b in level])
            own = jnp.where(here, got, own)
            passed = got
        near.append(own)
        passed_by.append(passed if len(far_levels) == 1 else own)
    other_ends = between_planes(after(new_outer, passed_by[0]), from_ends)
    others = jnp.concatenate([between_planes(passed, from_others) for passed in passed_by])
    beside_end = (plane == 1) | (plane == planes - 2)
    for pairs in passed_on:
        if pairs:
            got = by_side(after(new_down, near[0]), pairs)
            here = functools.reduce(jnp.logical_or, [side_plane == b for _, b in pairs])
            new_down = jnp.where(here, got, new_down)

    all_asked = jnp.concatenate(in_order(asked))
    attended = attention(
        after(all_asked, *near),
        earlier_keys,
        jnp.concatenate(ordered_keys),
        earlier_values,
        jnp.concatenate(ordered_values),
        plane,
    )
    other = jnp.where(beside_end, after(other_ends, attended), after(others, attended))
    mine, even = jnp.concatenate(near), plane % 2 == 0
    new_gate, new_lift = jnp.where(even, mine, other), jnp.where(even, other, mine)

    bits = [1 << k for k in reversed(range(columns_of.bit_length() - 1))]

    def swapped(part, bit):
        return lax.ppermute(part, "head", [(i, i ^ bit) for i in range(columns_of)])

    turns = list(range(1, group)) + [0]
    combined = apply_fast(
        all_asked, new_gate, new_lift, new_down, attended, gain, [(member - by) % group for by in turns]
    )
    arrived = [
        (to_member(rows_of, group - by), (member + by) % group) for by, rows_of in zip(turns[:-1], combined)
    ]
    combined = combined[-1]
    arrived = [(combined, member)] + arrived

    spot = jnp.stack([head_place] + [head for _, head in arrived]).astype(jnp.int32)
    parts = [(chunk, 0, number) for number, (chunk, _) in enumerate(arrived)]
    parts += [(swapped(chunk, bits[0]), bits[0], number) for number, (chunk, _) in enumerate(arrived)]
    total = project(parts[:-1], group, spot, output_weight, None, False)
    last, offset, number = parts[-1]
    parts[-1] = (after(last, total), offset, number)
    copies = [(after(part, parts[-1][0]), o, n) for part, o, n in parts]
    for bit in bits[1:]:
        copies += [(swapped(part, bit), o ^ bit, n) for part, o, n in copies]
    total = project(parts[-1:], group, spot, output_weight, total, False)
    return project(copies[len(parts) :], group, spot, output_weight, total, True)


def solution(mesh):
    return jax.shard_map(
        on_device,
        mesh=mesh,
        in_specs=(
            P("ctx", "head"),
            P("ctx", "head"),
            P("ctx", "head"),
            P("head", "ctx"),
            P("head", None, None),
            P("head", None, None),
            P("head", None, None),
            P("head"),
            P(None, "head"),
        ),
        out_specs=P("ctx", "head"),
        check_vma=False,
    )
```

```python
import functools
import math

import jax
import jax.numpy as jnp
from jax import lax
from jax.experimental import pallas as pl
from jax.experimental.pallas import tpu as pltpu
from jax.sharding import PartitionSpec as P

ATT_HD = 128
WINDOW = 512
NS_ITERS = 3
PIECES = 2
VMEM_BYTES = 20 * 1024 * 1024

quintic_first = 3.4445
quintic_second = -4.775
quintic_third = 2.0315

f32 = jnp.float32
bf16 = jnp.bfloat16


def mm(a, b, dims=((1,), (0,))):
    return lax.dot_general(a, b, (dims, ((), ())), preferred_element_type=f32)


def after(value, *earlier):
    return lax.optimization_barrier((value, *earlier))[0]


def pick(blocks, which):
    out = blocks[0]
    for number in range(1, len(blocks)):
        out = jnp.where(which == number, blocks[number], out)
    return out


def tree_low(low, high):
    levels, step = [], 1
    while step < high - low:
        levels.append(
            [(i + step, i) for i in range(low, high, 2 * step) if i + step < high]
        )
        step *= 2
    return levels


def tree_high(low, high):
    return [
        [(low + high - 1 - a, low + high - 1 - b) for a, b in level]
        for level in tree_low(low, high)
    ]


def tree_ends(count):
    low = tree_low(0, count // 2)
    return [
        [(2 * a, 2 * b) for a, b in level]
        + [(count - 1 - 2 * a, count - 1 - 2 * b) for a, b in level]
        for level in low
    ]


def tree_mid(count):
    middle = count // 2
    left, right = tree_high(0, middle), tree_low(middle, count)
    levels = []
    for k in range(max(len(left), len(right))):
        levels.append((left[k] if k < len(left) else []) + (right[k] if k < len(right) else []))
    return levels + [[(middle, middle - 1)]]


def spread_ends(count):
    levels, step = [], count // 2
    while step > 1:
        low = [(i, i + step) for i in range(0, count, 2 * step)]
        levels.append(low + [(count - 1 - a, count - 1 - b) for a, b in low])
        step //= 2
    return levels


def attention_kernel(first_ref, q_ref, kp_ref, k_ref, vp_ref, v_ref, out_ref, k_all, v_turned):
    tokens = q_ref.shape[0]
    tile = ATT_HD
    span = WINDOW + tile
    k_all[:WINDOW] = kp_ref[...]
    k_all[WINDOW:] = k_ref[...]
    v_turned[:, :WINDOW] = vp_ref[...].T
    v_turned[:, WINDOW:] = v_ref[...].T
    is_first = first_ref[0] == 0
    key = lax.broadcasted_iota(jnp.int32, (tile, tile), 0)
    query = lax.broadcasted_iota(jnp.int32, (tile, tile), 1)
    scale = ATT_HD**-0.5 * math.log2(math.e)
    for number in range(tokens // tile):
        start = number * tile
        s = mm(k_all[start : start + span], q_ref[start : start + tile], ((1,), (1,)))
        inner = s[tile:WINDOW]
        head_rows = key > query
        if start < WINDOW:
            head_rows = head_rows & jnp.logical_not(is_first)
            place = start + tile + lax.broadcasted_iota(jnp.int32, inner.shape, 0)
            inner = jnp.where((place >= WINDOW) | jnp.logical_not(is_first), inner, -1e30)
        s = jnp.concatenate(
            [
                jnp.where(head_rows, s[:tile], -1e30),
                inner,
                jnp.where(key <= query, s[WINDOW:], -1e30),
            ]
        )
        peak = jnp.max(s, axis=0, keepdims=True)
        w = jnp.exp2((s - peak) * scale)
        total = jnp.sum(w, axis=0, keepdims=True)
        o = mm(v_turned[:, start : start + span], w.astype(bf16))
        out_ref[start : start + tile] = (o / total).T


def attention(q, kp, k, vp, v, plane):
    tokens, width = q.shape
    wide = pl.BlockSpec((tokens, ATT_HD), lambda a, s: (0, a))
    before = pl.BlockSpec((WINDOW, ATT_HD), lambda a, s: (0, a))
    return pl.pallas_call(
        attention_kernel,
        out_shape=jax.ShapeDtypeStruct((tokens, width), f32),
        grid_spec=pltpu.PrefetchScalarGridSpec(
            num_scalar_prefetch=1,
            grid=(width // ATT_HD,),
            in_specs=[wide, before, wide, before, wide],
            out_specs=wide,
            scratch_shapes=[
                pltpu.VMEM((WINDOW + tokens, ATT_HD), bf16),
                pltpu.VMEM((ATT_HD, WINDOW + tokens), bf16),
            ],
        ),
        compiler_params=pltpu.CompilerParams(vmem_limit_bytes=VMEM_BYTES),
        cost_estimate=pl.CostEstimate(
            flops=4 * tokens * (WINDOW + ATT_HD) * width,
            bytes_accessed=12 * tokens * width,
            transcendentals=tokens * (WINDOW + ATT_HD) * (width // ATT_HD),
        ),
    )(jnp.reshape(plane, (1,)).astype(jnp.int32), q, kp, k, vp, v)


def settle_kernel(active_ref, grad_ref, init_ref, out_ref, x_ref):
    @pl.when(active_ref[0] == 1)
    def _():
        g = grad_ref[...]
        square = jnp.sum(jnp.sum(g * g, axis=0, keepdims=True), axis=1, keepdims=True)
        x_ref[...] = (g / (jnp.sqrt(square) + 1e-06)).astype(bf16)

        for _ in range(NS_ITERS):
            x = x_ref[...]
            gram = mm(x, x, ((1,), (1,))).astype(bf16)
            product = mm(gram, x).astype(bf16)
            second = mm(gram, product)
            x_ref[...] = (
                quintic_first * x.astype(f32)
                + quintic_second * product.astype(f32)
                + quintic_third * second
            ).astype(bf16)

        initial = init_ref[...].astype(f32)
        updated = initial + x_ref[...].astype(f32)
        target = jnp.sqrt(jnp.sum(initial * initial, axis=0, keepdims=True))
        current = jnp.sqrt(jnp.sum(updated * updated, axis=0, keepdims=True) + 1e-06)
        out_ref[...] = (updated * (target / current)).astype(bf16)

    @pl.when(active_ref[0] == 0)
    def _():
        out_ref[...] = jnp.zeros_like(out_ref)


def renew(gradient, initial, active):
    rows, columns = gradient.shape
    vmem = pl.BlockSpec(memory_space=pltpu.VMEM)
    return pl.pallas_call(
        settle_kernel,
        out_shape=jax.ShapeDtypeStruct((rows, columns), bf16),
        in_specs=[pl.BlockSpec(memory_space=pltpu.SMEM), vmem, vmem],
        out_specs=vmem,
        scratch_shapes=[pltpu.VMEM((rows, columns), bf16)],
        compiler_params=pltpu.CompilerParams(vmem_limit_bytes=VMEM_BYTES),
        cost_estimate=pl.CostEstimate(
            flops=6 * NS_ITERS * rows * rows * columns,
            bytes_accessed=8 * rows * columns,
            transcendentals=0,
        ),
    )(jnp.reshape(active, (1,)).astype(jnp.int32), gradient, initial)


def apply_kernel(which_ref, q_ref, gate_ref, lift_ref, down_ref, att_ref, gain_ref, *out_refs):
    q = q_ref[...]
    gate = mm(q, gate_ref[...])
    lift = mm(q, lift_ref[...])
    hidden = (gate / (1.0 + jnp.exp(-gate)) * lift).astype(bf16)
    result = mm(hidden, down_ref[...])
    scale = lax.rsqrt(jnp.mean(result * result, axis=1, keepdims=True) + 1e-06)
    combined = (att_ref[...] + result * scale * gain_ref[...]).astype(bf16)
    for number, out_ref in enumerate(out_refs):

        @pl.when(pl.program_id(0) == number)
        def _(out_ref=out_ref):
            out_ref[...] = combined


def apply_fast(q, gate, lift, down, attended, gain, order):
    rows, width = q.shape
    count = len(order)
    tokens = rows // count
    whole = pl.BlockSpec((width, width), lambda i, s: (0, 0))
    picked = pl.BlockSpec((tokens, width), lambda i, s: (s[i], 0))
    return pl.pallas_call(
        apply_kernel,
        out_shape=[jax.ShapeDtypeStruct((tokens, width), bf16)] * count,
        grid_spec=pltpu.PrefetchScalarGridSpec(
            num_scalar_prefetch=1,
            grid=(count,),
            in_specs=[picked, whole, whole, whole, picked, pl.BlockSpec((1, width), lambda i, s: (0, 0))],
            out_specs=[pl.BlockSpec((tokens, width), lambda i, s: (0, 0))] * count,
        ),
        compiler_params=pltpu.CompilerParams(vmem_limit_bytes=VMEM_BYTES),
        cost_estimate=pl.CostEstimate(
            flops=6 * rows * width * width,
            bytes_accessed=10 * rows * width + 6 * width * width,
            transcendentals=rows * width,
        ),
    )(jnp.stack(order).astype(jnp.int32), q, gate, lift, down, attended, gain)


def fetch_kernel(groups, group, depth, spot_ref, w_ref, after_ref, *refs):
    arrived = refs[-1]
    copies = []
    for origins, out_ref in zip(groups, refs[:-1]):
        for number, (offset, head) in enumerate(origins):
            start = ((spot_ref[0] ^ offset) * group + spot_ref[1 + head]) * depth
            copy = pltpu.make_async_copy(
                w_ref.at[pl.ds(pl.multiple_of(start, depth), depth)],
                out_ref.at[pl.ds(number * depth, depth)],
                arrived.at[len(copies)],
            )
            copy.start()
            copies.append(copy)
    for copy in copies:
        copy.wait()


def fetched(groups, group, depth, spot, weight, after_this):
    columns, count = weight.shape[1], sum(map(len, groups))
    hbm = pl.BlockSpec(memory_space=pltpu.HBM)
    return pl.pallas_call(
        functools.partial(fetch_kernel, groups, group, depth),
        out_shape=[jax.ShapeDtypeStruct((len(g) * depth, columns), bf16) for g in groups],
        in_specs=[pl.BlockSpec(memory_space=pltpu.SMEM), hbm, hbm],
        out_specs=[pl.BlockSpec(memory_space=pltpu.VMEM)] * len(groups),
        scratch_shapes=[pltpu.SemaphoreType.DMA((count,))],
        compiler_params=pltpu.CompilerParams(vmem_limit_bytes=VMEM_BYTES),
        cost_estimate=pl.CostEstimate(
            flops=10**10, bytes_accessed=4 * count * depth * columns, transcendentals=0
        ),
    )(spot, weight, after_this)


def project_kernel(count, rows_ref, *refs):
    chunk_refs = refs[:count]
    total_ref = refs[count] if len(refs) == count + 3 else None
    out_ref, joined = refs[-2:]
    depth = chunk_refs[0].shape[1]
    for number in range(count):
        joined[:, number * depth : (number + 1) * depth] = chunk_refs[number][...]
    tile = math.gcd(out_ref.shape[1], 256)

    @pl.loop(0, out_ref.shape[1] // tile)
    def _(number):
        at = pl.ds(pl.multiple_of(number * tile, tile), tile)
        result = mm(joined[...], rows_ref[:, at])
        if total_ref is not None:
            result += total_ref[:, at]
        out_ref[:, at] = result.astype(out_ref.dtype)


def project(chunks, rows, total, is_last):
    count = len(chunks)
    tokens, depth = chunks[0].shape
    columns = rows.shape[1]
    vmem = pl.BlockSpec(memory_space=pltpu.VMEM)
    operands = [rows] + list(chunks) + ([] if total is None else [total])
    return pl.pallas_call(
        functools.partial(project_kernel, count),
        out_shape=jax.ShapeDtypeStruct((tokens, columns), bf16 if is_last else f32),
        in_specs=[vmem] * len(operands),
        out_specs=vmem,
        scratch_shapes=[pltpu.VMEM((tokens, count * depth), bf16)],
        compiler_params=pltpu.CompilerParams(vmem_limit_bytes=VMEM_BYTES),
        cost_estimate=pl.CostEstimate(
            flops=16 * count * tokens * depth * columns,
            bytes_accessed=2 * count * depth * (tokens + columns),
            transcendentals=0,
        ),
    )(*operands)


OVER_TOKENS = ((0,), (0,))


def forward(keys, gate, lift):
    gate_pre = mm(keys, gate)
    lift_pre = mm(keys, lift)
    logistic = jax.nn.sigmoid(gate_pre)
    silu = gate_pre * logistic
    hidden = (silu * lift_pre).astype(bf16)
    return hidden, lift_pre * (logistic * (1.0 + gate_pre * (1.0 - logistic))), silu


def on_device(
    queries,
    key_rows,
    value_rows,
    learning_rates,
    fast_gate,
    fast_lift,
    fast_down,
    output_gain,
    output_weight,
):
    tokens = queries.shape[0]
    group, width = fast_gate.shape[0], fast_gate.shape[1]
    context = lax.axis_size("ctx")
    columns_of = lax.axis_size("head")
    planes = context // group
    place = lax.axis_index("ctx")
    member, plane = place % group, place // group
    head_place = lax.axis_index("head")

    def to_member(array, by):
        pairs = [(i, i // group * group + (i + by) % group) for i in range(context)]
        return lax.ppermute(array, "ctx", pairs)

    def between_planes(array, pairs):
        return lax.ppermute(
            array,
            "ctx",
            [(a * group + m, b * group + m) for a, b in pairs for m in range(group)],
        )

    def by_side(array, pairs):
        moves = []
        for h in range(columns_of):
            for a, b in pairs:
                a, b = (a, b) if h % 2 == 0 else (planes - 1 - a, planes - 1 - b)
                moves += [
                    ((a * group + m) * columns_of + h, (b * group + m) * columns_of + h) for m in range(group)
                ]
        return lax.ppermute(array, ("ctx", "head"), moves)

    def head_columns(array, by):
        return lax.dynamic_slice_in_dim(array, (member + by) % group * width, width, 1)

    gate, lift, down = (
        lax.dynamic_index_in_dim(w, member, 0, keepdims=False)
        for w in (fast_gate, fast_lift, fast_down)
    )
    gain = lax.dynamic_slice_in_dim(output_gain, member * width, width, 0)[None]

    onward = [(i, i + 1) for i in range(planes - 1)]

    def in_order(blocks):
        return [pick(blocks, (member - j) % group) for j in range(group)]

    keys = [head_columns(key_rows, by) for by in range(group)]
    values = [head_columns(value_rows, by) for by in range(group)]
    asked = [head_columns(queries, by) for by in range(group)]
    rates = [
        lax.dynamic_index_in_dim(learning_rates, (member + by) % group, 0, keepdims=False)
        for by in range(group)
    ]
    sent_keys = keys[-1]
    keys = keys[:1] + [to_member(keys[by], by) for by in range(1, group)]
    rates = rates[:1] + [to_member(after(rates[by], sent_keys), by) for by in range(1, group)]
    values = values[:1] + [to_member(values[by], by) for by in range(1, group)]
    ordered_keys = in_order(keys)
    earlier_keys = between_planes(ordered_keys[-1][-WINDOW:], onward)
    forwards = [forward(block, gate, lift) for block in keys]
    hidden = forwards[-1][0]
    values = values[:1] + [after(block, hidden) for block in values[1:]]

    hiddens, slopes, silus, scaleds = [], [], [], []
    total_down = 0.0
    for by in range(group):
        hidden, slope, silu = forwards[by]
        scaled = (rates[by][:, None] * values[by].astype(f32)).astype(bf16)
        total_down = total_down + mm(hidden, scaled, OVER_TOKENS)
        slopes.append(slope)
        silus.append(silu)
        scaleds.append(scaled)
    total_gate, total_lift = 0.0, 0.0
    for by in range(group):
        scaled = scaleds[by] if by < group - 1 else after(scaleds[by], total_down, earlier_keys)
        backward = mm(scaled, down, ((1,), (1,)))
        total_gate = total_gate + mm(keys[by], (backward * slopes[by]).astype(bf16), OVER_TOKENS)
        total_lift = total_lift + mm(keys[by], (backward * silus[by]).astype(bf16), OVER_TOKENS)

    ordered_values = in_order([after(block, backward) for block in values])
    window_values = ordered_values[-1][-WINDOW:]
    values_early = between_planes(window_values, onward[1:])

    rows = width // PIECES

    def cut(matrix):
        return [matrix[piece * rows : (piece + 1) * rows] for piece in range(PIECES)]

    def add_from(own, pairs):
        return own + between_planes(own.astype(bf16), pairs).astype(f32)

    down_levels = tree_mid(planes)
    side_plane = jnp.where(head_place % 2 == 0, plane, planes - 1 - plane)

    def add_side(own, pairs):
        return own + by_side(own.astype(bf16), pairs).astype(f32)

    sum_down = add_side(total_down, down_levels[0])
    asked = asked[:1] + [to_member(after(asked[by], sum_down), by) for by in range(1, group)]
    odd = plane % 2 == 1
    kept = jnp.where(odd, total_lift, total_gate)
    given = jnp.where(odd, total_gate, total_lift).astype(bf16)
    neighbours = [(i, i ^ 1) for i in range(planes)]
    given = between_planes(after(given, sum_down, values_early), neighbours)
    first_sum = sum_down
    for level in down_levels[1:]:
        sum_down = add_side(sum_down, level)
    kept = kept + given.astype(f32)
    met = [kept]
    values_first = between_planes(after(window_values, first_sum), onward[:1])
    earlier_values = jnp.where(plane == 1, values_first, values_early)
    middle_plane = side_plane == planes // 2 - 1
    new_down = renew(after(sum_down, values_first, *met), down, middle_plane)
    for level in tree_ends(planes):
        kept = after(kept, new_down) + between_planes(kept.astype(bf16), level).astype(f32)

    def spread(own, pairs):
        got = between_planes(own, pairs)
        here = functools.reduce(jnp.logical_or, [plane == b for _, b in pairs])
        return jnp.where(here, got, own)

    low_plane, high_plane = plane == 0, plane == planes - 1
    new_sums = kept
    new_outer = renew(after(new_sums, new_down), jnp.where(low_plane, gate, lift), low_plane | high_plane)
    owned_down, owner = after(new_down, new_sums), planes // 2 - 1
    passed_on = []
    for level in reversed(down_levels):
        from_owner = [(b, a) for a, b in level if b == owner]
        got = by_side(owned_down, from_owner)
        here = functools.reduce(jnp.logical_or, [side_plane == b for _, b in from_owner])
        new_down = jnp.where(here, got, new_down)
        passed_on.append([(b, a) for a, b in level if b != owner])
    far_levels = spread_ends(planes)
    from_ends = [(i, i ^ 1) for i in (0, planes - 1)]
    from_others = [(i, i ^ 1) for i in range(1, planes - 1)]
    near, passed_by = [], []
    for own in cut(new_outer):
        passed = own
        for level in far_levels:
            got = between_planes(own, level)
            here = functools.reduce(jnp.logical_or, [plane == b for _, b in level])
            own = jnp.where(here, got, own)
            passed = got
        near.append(own)
        passed_by.append(passed if len(far_levels) == 1 else own)
    other_ends = between_planes(after(new_outer, passed_by[0]), from_ends)
    others = jnp.concatenate([between_planes(passed, from_others) for passed in passed_by])
    beside_end = (plane == 1) | (plane == planes - 2)
    for pairs in passed_on:
        if pairs:
            got = by_side(after(new_down, near[0]), pairs)
            here = functools.reduce(jnp.logical_or, [side_plane == b for _, b in pairs])
            new_down = jnp.where(here, got, new_down)

    all_asked = jnp.concatenate(in_order(asked))
    attended = attention(
        after(all_asked, *near),
        earlier_keys,
        jnp.concatenate(ordered_keys),
        earlier_values,
        jnp.concatenate(ordered_values),
        plane,
    )
    other = jnp.where(beside_end, after(other_ends, attended), after(others, attended))
    mine, even = jnp.concatenate(near), plane % 2 == 0
    new_gate, new_lift = jnp.where(even, mine, other), jnp.where(even, other, mine)

    bits = [1 << k for k in reversed(range(columns_of.bit_length() - 1))]

    def swapped(part, bit):
        return lax.ppermute(part, "head", [(i, i ^ bit) for i in range(columns_of)])

    turns = list(range(1, group)) + [0]
    combined = apply_fast(
        all_asked, new_gate, new_lift, new_down, attended, gain, [(member - by) % group for by in turns]
    )
    arrived = [
        (to_member(rows_of, group - by), (member + by) % group) for by, rows_of in zip(turns[:-1], combined)
    ]
    combined = combined[-1]
    arrived = [(combined, member)] + arrived

    spot = jnp.stack([head_place] + [head for _, head in arrived]).astype(jnp.int32)
    parts = [(chunk, 0, number) for number, (chunk, _) in enumerate(arrived)]
    parts += [(swapped(chunk, bits[0]), bits[0], number) for number, (chunk, _) in enumerate(arrived)]
    places = [part[1:] for part in parts]
    found = list(places)
    for bit in bits[1:]:
        found += [(o ^ bit, n) for o, n in found]
    groups = [places[:-1], places[-1:], found[len(places) :]]
    rows = fetched(groups, group, width, spot, output_weight, combined)
    chunks = [part[0] for part in parts]
    total = project(chunks[:-1], rows[0], None, False)
    chunks[-1] = after(chunks[-1], total)
    copies = [after(chunk, total) for chunk in chunks]
    for bit in bits[1:]:
        copies += [swapped(chunk, bit) for chunk in copies]
    total = project(chunks[-1:], rows[1], total, False)
    return project(copies[len(chunks) :], rows[2], total, True)


def solution(mesh):
    return jax.shard_map(
        on_device,
        mesh=mesh,
        in_specs=(
            P("ctx", "head"),
            P("ctx", "head"),
            P("ctx", "head"),
            P("head", "ctx"),
            P("head", None, None),
            P("head", None, None),
            P("head", None, None),
            P("head"),
            P(None, "head"),
        ),
        out_specs=P("ctx", "head"),
        check_vma=False,
    )
```

```python
import functools
import math

import jax
import jax.numpy as jnp
from jax import lax
from jax.experimental import pallas as pl
from jax.experimental.pallas import tpu as pltpu
from jax.sharding import PartitionSpec as P

ATT_HD = 128
WINDOW = 512
NS_ITERS = 3
PIECES = 2
VMEM_BYTES = 20 * 1024 * 1024

quintic_first = 3.4445
quintic_second = -4.775
quintic_third = 2.0315

f32 = jnp.float32
bf16 = jnp.bfloat16


def mm(a, b, dims=((1,), (0,))):
    return lax.dot_general(a, b, (dims, ((), ())), preferred_element_type=f32)


def after(value, *earlier):
    return lax.optimization_barrier((value, *earlier))[0]


def pick(blocks, which):
    out = blocks[0]
    for number in range(1, len(blocks)):
        out = jnp.where(which == number, blocks[number], out)
    return out


def tree_low(low, high):
    levels, step = [], 1
    while step < high - low:
        levels.append(
            [(i + step, i) for i in range(low, high, 2 * step) if i + step < high]
        )
        step *= 2
    return levels


def tree_high(low, high):
    return [
        [(low + high - 1 - a, low + high - 1 - b) for a, b in level]
        for level in tree_low(low, high)
    ]


def tree_ends(count):
    low = tree_low(0, count // 2)
    return [
        [(2 * a, 2 * b) for a, b in level]
        + [(count - 1 - 2 * a, count - 1 - 2 * b) for a, b in level]
        for level in low
    ]


def tree_mid(count):
    middle = count // 2
    left, right = tree_high(0, middle), tree_low(middle, count)
    levels = []
    for k in range(max(len(left), len(right))):
        levels.append((left[k] if k < len(left) else []) + (right[k] if k < len(right) else []))
    return levels + [[(middle, middle - 1)]]


def spread_ends(count):
    levels, step = [], count // 2
    while step > 1:
        low = [(i, i + step) for i in range(0, count, 2 * step)]
        levels.append(low + [(count - 1 - a, count - 1 - b) for a, b in low])
        step //= 2
    return levels


def attention_kernel(first_ref, q_ref, kp_ref, k_ref, vp_ref, v_ref, out_ref, k_all, v_turned):
    tokens = q_ref.shape[0]
    tile = ATT_HD
    span = WINDOW + tile
    k_all[:WINDOW] = kp_ref[...]
    k_all[WINDOW:] = k_ref[...]
    v_turned[:, :WINDOW] = vp_ref[...].T
    v_turned[:, WINDOW:] = v_ref[...].T
    is_first = first_ref[0] == 0
    key = lax.broadcasted_iota(jnp.int32, (tile, tile), 0)
    query = lax.broadcasted_iota(jnp.int32, (tile, tile), 1)
    scale = ATT_HD**-0.5 * math.log2(math.e)
    for number in range(tokens // tile):
        start = number * tile
        s = mm(k_all[start : start + span], q_ref[start : start + tile], ((1,), (1,)))
        inner = s[tile:WINDOW]
        head_rows = key > query
        if start < WINDOW:
            head_rows = head_rows & jnp.logical_not(is_first)
            place = start + tile + lax.broadcasted_iota(jnp.int32, inner.shape, 0)
            inner = jnp.where((place >= WINDOW) | jnp.logical_not(is_first), inner, -1e30)
        s = jnp.concatenate(
            [
                jnp.where(head_rows, s[:tile], -1e30),
                inner,
                jnp.where(key <= query, s[WINDOW:], -1e30),
            ]
        )
        peak = jnp.max(s, axis=0, keepdims=True)
        w = jnp.exp2((s - peak) * scale)
        total = jnp.sum(w, axis=0, keepdims=True)
        o = mm(v_turned[:, start : start + span], w.astype(bf16))
        out_ref[start : start + tile] = (o / total).T


def attention(q, kp, k, vp, v, plane):
    tokens, width = q.shape
    wide = pl.BlockSpec((tokens, ATT_HD), lambda a, s: (0, a))
    before = pl.BlockSpec((WINDOW, ATT_HD), lambda a, s: (0, a))
    return pl.pallas_call(
        attention_kernel,
        out_shape=jax.ShapeDtypeStruct((tokens, width), f32),
        grid_spec=pltpu.PrefetchScalarGridSpec(
            num_scalar_prefetch=1,
            grid=(width // ATT_HD,),
            in_specs=[wide, before, wide, before, wide],
            out_specs=wide,
            scratch_shapes=[
                pltpu.VMEM((WINDOW + tokens, ATT_HD), bf16),
                pltpu.VMEM((ATT_HD, WINDOW + tokens), bf16),
            ],
        ),
        compiler_params=pltpu.CompilerParams(vmem_limit_bytes=VMEM_BYTES),
        cost_estimate=pl.CostEstimate(
            flops=4 * tokens * (WINDOW + ATT_HD) * width,
            bytes_accessed=12 * tokens * width,
            transcendentals=tokens * (WINDOW + ATT_HD) * (width // ATT_HD),
        ),
    )(jnp.reshape(plane, (1,)).astype(jnp.int32), q, kp, k, vp, v)


def settle_kernel(active_ref, grad_ref, init_ref, out_ref, x_ref):
    @pl.when(active_ref[0] == 1)
    def _():
        g = grad_ref[...]
        square = jnp.sum(jnp.sum(g * g, axis=0, keepdims=True), axis=1, keepdims=True)
        x_ref[...] = (g / (jnp.sqrt(square) + 1e-06)).astype(bf16)

        for _ in range(NS_ITERS):
            x = x_ref[...]
            gram = mm(x, x, ((1,), (1,))).astype(bf16)
            product = mm(gram, x).astype(bf16)
            second = mm(gram, product)
            x_ref[...] = (
                quintic_first * x.astype(f32)
                + quintic_second * product.astype(f32)
                + quintic_third * second
            ).astype(bf16)

        initial = init_ref[...].astype(f32)
        updated = initial + x_ref[...].astype(f32)
        target = jnp.sqrt(jnp.sum(initial * initial, axis=0, keepdims=True))
        current = jnp.sqrt(jnp.sum(updated * updated, axis=0, keepdims=True) + 1e-06)
        out_ref[...] = (updated * (target / current)).astype(bf16)

    @pl.when(active_ref[0] == 0)
    def _():
        out_ref[...] = jnp.zeros_like(out_ref)


def renew(gradient, initial, active):
    rows, columns = gradient.shape
    vmem = pl.BlockSpec(memory_space=pltpu.VMEM)
    return pl.pallas_call(
        settle_kernel,
        out_shape=jax.ShapeDtypeStruct((rows, columns), bf16),
        in_specs=[pl.BlockSpec(memory_space=pltpu.SMEM), vmem, vmem],
        out_specs=vmem,
        scratch_shapes=[pltpu.VMEM((rows, columns), bf16)],
        compiler_params=pltpu.CompilerParams(vmem_limit_bytes=VMEM_BYTES),
        cost_estimate=pl.CostEstimate(
            flops=6 * NS_ITERS * rows * rows * columns,
            bytes_accessed=8 * rows * columns,
            transcendentals=0,
        ),
    )(jnp.reshape(active, (1,)).astype(jnp.int32), gradient, initial)


def apply_kernel(which_ref, q_ref, gate_ref, lift_ref, down_ref, att_ref, gain_ref, *out_refs):
    q = q_ref[...]
    gate = mm(q, gate_ref[...])
    lift = mm(q, lift_ref[...])
    hidden = (gate / (1.0 + jnp.exp(-gate)) * lift).astype(bf16)
    result = mm(hidden, down_ref[...])
    scale = lax.rsqrt(jnp.mean(result * result, axis=1, keepdims=True) + 1e-06)
    combined = (att_ref[...] + result * scale * gain_ref[...]).astype(bf16)
    for number, out_ref in enumerate(out_refs):

        @pl.when(pl.program_id(0) == number)
        def _(out_ref=out_ref):
            out_ref[...] = combined


def apply_fast(q, gate, lift, down, attended, gain, order):
    rows, width = q.shape
    count = len(order)
    tokens = rows // count
    whole = pl.BlockSpec((width, width), lambda i, s: (0, 0))
    picked = pl.BlockSpec((tokens, width), lambda i, s: (s[i], 0))
    return pl.pallas_call(
        apply_kernel,
        out_shape=[jax.ShapeDtypeStruct((tokens, width), bf16)] * count,
        grid_spec=pltpu.PrefetchScalarGridSpec(
            num_scalar_prefetch=1,
            grid=(count,),
            in_specs=[picked, whole, whole, whole, picked, pl.BlockSpec((1, width), lambda i, s: (0, 0))],
            out_specs=[pl.BlockSpec((tokens, width), lambda i, s: (0, 0))] * count,
        ),
        compiler_params=pltpu.CompilerParams(vmem_limit_bytes=VMEM_BYTES),
        cost_estimate=pl.CostEstimate(
            flops=6 * rows * width * width,
            bytes_accessed=10 * rows * width + 6 * width * width,
            transcendentals=rows * width,
        ),
    )(jnp.stack(order).astype(jnp.int32), q, gate, lift, down, attended, gain)


def fetch_kernel(groups, group, depth, spot_ref, w_ref, after_ref, *refs):
    arrived = refs[-1]
    copies = []
    for origins, out_ref in zip(groups, refs[:-1]):
        for number, (offset, head) in enumerate(origins):
            start = ((spot_ref[0] ^ offset) * group + spot_ref[1 + head]) * depth
            copy = pltpu.make_async_copy(
                w_ref.at[pl.ds(pl.multiple_of(start, depth), depth)],
                out_ref.at[pl.ds(number * depth, depth)],
                arrived.at[len(copies)],
            )
            copy.start()
            copies.append(copy)
    for copy in copies:
        copy.wait()


def fetched(groups, group, depth, spot, weight, after_this):
    columns, count = weight.shape[1], sum(map(len, groups))
    hbm = pl.BlockSpec(memory_space=pltpu.HBM)
    return pl.pallas_call(
        functools.partial(fetch_kernel, groups, group, depth),
        out_shape=[jax.ShapeDtypeStruct((len(g) * depth, columns), bf16) for g in groups],
        in_specs=[pl.BlockSpec(memory_space=pltpu.SMEM), hbm, hbm],
        out_specs=[pl.BlockSpec(memory_space=pltpu.VMEM)] * len(groups),
        scratch_shapes=[pltpu.SemaphoreType.DMA((count,))],
        compiler_params=pltpu.CompilerParams(vmem_limit_bytes=VMEM_BYTES),
        cost_estimate=pl.CostEstimate(
            flops=10**10, bytes_accessed=4 * count * depth * columns, transcendentals=0
        ),
    )(spot, weight, after_this)


def project_kernel(count, rows_ref, *refs):
    chunk_refs = refs[:count]
    total_ref = refs[count] if len(refs) == count + 3 else None
    out_ref, joined = refs[-2:]
    depth = chunk_refs[0].shape[1]
    for number in range(count):
        joined[:, number * depth : (number + 1) * depth] = chunk_refs[number][...]
    tile = math.gcd(out_ref.shape[1], 256)

    @pl.loop(0, out_ref.shape[1] // tile)
    def _(number):
        at = pl.ds(pl.multiple_of(number * tile, tile), tile)
        result = mm(joined[...], rows_ref[:, at])
        if total_ref is not None:
            result += total_ref[:, at]
        out_ref[:, at] = result.astype(out_ref.dtype)


def project(chunks, rows, total, is_last):
    count = len(chunks)
    tokens, depth = chunks[0].shape
    columns = rows.shape[1]
    vmem = pl.BlockSpec(memory_space=pltpu.VMEM)
    operands = [rows] + list(chunks) + ([] if total is None else [total])
    return pl.pallas_call(
        functools.partial(project_kernel, count),
        out_shape=jax.ShapeDtypeStruct((tokens, columns), bf16 if is_last else f32),
        in_specs=[vmem] * len(operands),
        out_specs=vmem,
        scratch_shapes=[pltpu.VMEM((tokens, count * depth), bf16)],
        compiler_params=pltpu.CompilerParams(vmem_limit_bytes=VMEM_BYTES),
        cost_estimate=pl.CostEstimate(
            flops=16 * count * tokens * depth * columns,
            bytes_accessed=2 * count * depth * (tokens + columns),
            transcendentals=0,
        ),
    )(*operands)


OVER_TOKENS = ((0,), (0,))


def forward(keys, gate, lift):
    gate_pre = mm(keys, gate)
    lift_pre = mm(keys, lift)
    logistic = jax.nn.sigmoid(gate_pre)
    silu = gate_pre * logistic
    hidden = (silu * lift_pre).astype(bf16)
    return hidden, lift_pre * (logistic * (1.0 + gate_pre * (1.0 - logistic))), silu


def on_device(
    queries,
    key_rows,
    value_rows,
    learning_rates,
    fast_gate,
    fast_lift,
    fast_down,
    output_gain,
    output_weight,
):
    tokens = queries.shape[0]
    group, width = fast_gate.shape[0], fast_gate.shape[1]
    context = lax.axis_size("ctx")
    columns_of = lax.axis_size("head")
    planes = context // group
    place = lax.axis_index("ctx")
    member, plane = place % group, place // group
    head_place = lax.axis_index("head")

    def to_member(array, by):
        pairs = [(i, i // group * group + (i + by) % group) for i in range(context)]
        return lax.ppermute(array, "ctx", pairs)

    def between_planes(array, pairs):
        return lax.ppermute(
            array,
            "ctx",
            [(a * group + m, b * group + m) for a, b in pairs for m in range(group)],
        )

    def by_side(array, pairs):
        moves = []
        for h in range(columns_of):
            for a, b in pairs:
                a, b = (a, b) if h % 2 == 0 else (planes - 1 - a, planes - 1 - b)
                moves += [
                    ((a * group + m) * columns_of + h, (b * group + m) * columns_of + h) for m in range(group)
                ]
        return lax.ppermute(array, ("ctx", "head"), moves)

    def head_columns(array, by):
        return lax.dynamic_slice_in_dim(array, (member + by) % group * width, width, 1)

    gate, lift, down = (
        lax.dynamic_index_in_dim(w, member, 0, keepdims=False)
        for w in (fast_gate, fast_lift, fast_down)
    )
    gain = lax.dynamic_slice_in_dim(output_gain, member * width, width, 0)[None]

    onward = [(i, i + 1) for i in range(planes - 1)]

    def in_order(blocks):
        return [pick(blocks, (member - j) % group) for j in range(group)]

    keys = [head_columns(key_rows, by) for by in range(group)]
    values = [head_columns(value_rows, by) for by in range(group)]
    asked = [head_columns(queries, by) for by in range(group)]
    rates = [
        lax.dynamic_index_in_dim(learning_rates, (member + by) % group, 0, keepdims=False)
        for by in range(group)
    ]
    sent_keys = keys[-1]
    keys = keys[:1] + [to_member(keys[by], by) for by in range(1, group)]
    rates = rates[:1] + [to_member(after(rates[by], sent_keys), by) for by in range(1, group)]
    values = values[:1] + [to_member(values[by], by) for by in range(1, group)]
    ordered_keys = in_order(keys)
    earlier_keys = between_planes(ordered_keys[-1][-WINDOW:], onward)
    forwards = [forward(block, gate, lift) for block in keys]
    hidden = forwards[-1][0]
    values = values[:1] + [after(block, hidden) for block in values[1:]]

    hiddens, slopes, silus, scaleds = [], [], [], []
    total_down = 0.0
    for by in range(group):
        hidden, slope, silu = forwards[by]
        scaled = (rates[by][:, None] * values[by].astype(f32)).astype(bf16)
        total_down = total_down + mm(hidden, scaled, OVER_TOKENS)
        slopes.append(slope)
        silus.append(silu)
        scaleds.append(scaled)
    total_gate, total_lift = 0.0, 0.0
    for by in range(group):
        scaled = scaleds[by] if by < group - 1 else after(scaleds[by], total_down, earlier_keys)
        backward = mm(scaled, down, ((1,), (1,)))
        total_gate = total_gate + mm(keys[by], (backward * slopes[by]).astype(bf16), OVER_TOKENS)
        total_lift = total_lift + mm(keys[by], (backward * silus[by]).astype(bf16), OVER_TOKENS)

    ordered_values = in_order([after(block, backward) for block in values])
    window_values = ordered_values[-1][-WINDOW:]
    values_early = between_planes(window_values, onward[1:])

    rows = width // PIECES

    def cut(matrix):
        return [matrix[piece * rows : (piece + 1) * rows] for piece in range(PIECES)]

    def add_from(own, pairs):
        return own + between_planes(own.astype(bf16), pairs).astype(f32)

    down_levels = tree_mid(planes)
    side_plane = jnp.where(head_place % 2 == 0, plane, planes - 1 - plane)

    def add_side(own, pairs):
        return own + by_side(own.astype(bf16), pairs).astype(f32)

    sum_down = add_side(total_down, down_levels[0])
    asked = asked[:1] + [to_member(after(asked[by], sum_down), by) for by in range(1, group)]
    odd = plane % 2 == 1
    kept = jnp.where(odd, total_lift, total_gate)
    given = jnp.where(odd, total_gate, total_lift).astype(bf16)
    neighbours = [(i, i ^ 1) for i in range(planes)]
    given = between_planes(after(given, sum_down, values_early), neighbours)
    first_sum = sum_down
    for level in down_levels[1:]:
        sum_down = add_side(sum_down, level)
    kept = kept + given.astype(f32)
    met = [kept]
    values_first = between_planes(after(window_values, first_sum), onward[:1])
    earlier_values = jnp.where(plane == 1, values_first, values_early)
    middle_plane = side_plane == planes // 2 - 1
    new_down = renew(after(sum_down, values_first, *met), down, middle_plane)
    for level in tree_ends(planes):
        kept = after(kept, new_down) + between_planes(kept.astype(bf16), level).astype(f32)

    def spread(own, pairs):
        got = between_planes(own, pairs)
        here = functools.reduce(jnp.logical_or, [plane == b for _, b in pairs])
        return jnp.where(here, got, own)

    low_plane, high_plane = plane == 0, plane == planes - 1
    new_sums = kept
    new_outer = renew(after(new_sums, new_down), jnp.where(low_plane, gate, lift), low_plane | high_plane)
    owned_down, owner = after(new_down, new_sums), planes // 2 - 1
    passed_on = []
    for level in reversed(down_levels):
        from_owner = [(b, a) for a, b in level if b == owner]
        got = by_side(owned_down, from_owner)
        here = functools.reduce(jnp.logical_or, [side_plane == b for _, b in from_owner])
        new_down = jnp.where(here, got, new_down)
        passed_on.append([(b, a) for a, b in level if b != owner])
    far_levels = spread_ends(planes)
    from_ends = [(i, i ^ 1) for i in (0, planes - 1)]
    from_others = [(i, i ^ 1) for i in range(1, planes - 1)]
    near, passed_by = [], []
    for own in cut(new_outer):
        passed = own
        for level in far_levels:
            got = between_planes(own, level)
            here = functools.reduce(jnp.logical_or, [plane == b for _, b in level])
            own = jnp.where(here, got, own)
            passed = got
        near.append(own)
        passed_by.append(passed if len(far_levels) == 1 else own)
    other_ends = between_planes(after(new_outer, passed_by[0]), from_ends)
    others = jnp.concatenate([between_planes(passed, from_others) for passed in passed_by])
    beside_end = (plane == 1) | (plane == planes - 2)
    for pairs in passed_on:
        if pairs:
            got = by_side(after(new_down, near[0]), pairs)
            here = functools.reduce(jnp.logical_or, [side_plane == b for _, b in pairs])
            new_down = jnp.where(here, got, new_down)

    all_asked = jnp.concatenate(in_order(asked))
    attended = attention(
        after(all_asked, *near),
        earlier_keys,
        jnp.concatenate(ordered_keys),
        earlier_values,
        jnp.concatenate(ordered_values),
        plane,
    )
    other = jnp.where(beside_end, after(other_ends, attended), after(others, attended))
    mine, even = jnp.concatenate(near), plane % 2 == 0
    new_gate, new_lift = jnp.where(even, mine, other), jnp.where(even, other, mine)

    bits = [1 << k for k in reversed(range(columns_of.bit_length() - 1))]

    def swapped(part, bit):
        return lax.ppermute(part, "head", [(i, i ^ bit) for i in range(columns_of)])

    turns = list(range(group))
    combined = apply_fast(
        all_asked, new_gate, new_lift, new_down, attended, gain, [(member - by) % group for by in turns]
    )
    arrived = [
        (to_member(rows_of, group - by), (member + by) % group) for by, rows_of in zip(turns[1:], combined[1:])
    ]
    combined = combined[0]
    arrived = [(combined, member)] + arrived

    spot = jnp.stack([head_place] + [head for _, head in arrived]).astype(jnp.int32)
    parts = [(chunk, 0, number) for number, (chunk, _) in enumerate(arrived)]
    parts += [(swapped(chunk, bits[0]), bits[0], number) for number, (chunk, _) in enumerate(arrived)]
    places = [part[1:] for part in parts]
    found = list(places)
    for bit in bits[1:]:
        found += [(o ^ bit, n) for o, n in found]
    groups = [places[:-1], places[-1:], found[len(places) :]]
    rows = fetched(groups, group, width, spot, output_weight, combined)
    chunks = [part[0] for part in parts]
    total = project(chunks[:-1], rows[0], None, False)
    chunks[-1] = after(chunks[-1], total)
    copies = [after(chunk, total) for chunk in chunks]
    for bit in bits[1:]:
        copies += [swapped(chunk, bit) for chunk in copies]
    total = project(chunks[-1:], rows[1], total, False)
    return project(copies[len(chunks) :], rows[2], total, True)


def solution(mesh):
    return jax.shard_map(
        on_device,
        mesh=mesh,
        in_specs=(
            P("ctx", "head"),
            P("ctx", "head"),
            P("ctx", "head"),
            P("head", "ctx"),
            P("head", None, None),
            P("head", None, None),
            P("head", None, None),
            P("head"),
            P(None, "head"),
        ),
        out_specs=P("ctx", "head"),
        check_vma=False,
    )
```
